128 devices in a mesh: section: 2 (over x_hi), seq: 4 (over z), fsdp: 16 (over y, x_lo, core).
Axes of the slice: x: 4 (x_hi: 2, x_lo: 2; x = x_hi * 2 + x_lo), y: 4, z: 4, core: 2. Of those that a mesh axis runs over, the one named last changes fastest.
Arguments:
- images_in: bfloat16 [2, 16, 640, 768], P(None, 'fsdp', 'seq'), may hold values from -6 to 6
- counts: int32 [2, 16, 4], P(None, 'fsdp'), may hold values from 1 to 160, 577 in all within a row
- cotangent: bfloat16 [2, 16, 640, 768], P(None, 'fsdp', 'seq'), may hold values from -6 to 6
- gain_one: bfloat16 [2, 768], P('section', 'fsdp'), may hold values from 0.5 to 1.5
- shift_one: bfloat16 [2, 768], P('section', 'fsdp'), may hold values from -3 to 3
- w_qkv: bfloat16 [2, 768, 2304], P('section', 'fsdp'), may hold values from -0.21875 to 0.21875
- bias_query: bfloat16 [2, 768], P('section', 'fsdp'), may hold values from -3 to 3
- bias_value: bfloat16 [2, 768], P('section', 'fsdp'), may hold values from -3 to 3
- w_out: bfloat16 [2, 768, 768], P('section', 'fsdp'), may hold values from -3 to 3
- bias_out: bfloat16 [2, 768], P('section', 'fsdp'), may hold values from -3 to 3
- gain_two: bfloat16 [2, 768], P('section', 'fsdp'), may hold values from 0.5 to 1.5
- shift_two: bfloat16 [2, 768], P('section', 'fsdp'), may hold values from -3 to 3
- w_up: bfloat16 [2, 768, 3072], P('section', 'fsdp'), may hold values from -0.21875 to 0.21875
- bias_up: bfloat16 [2, 3072], P('section', 'fsdp'), may hold values from -3 to 3
- w_down: bfloat16 [2, 3072, 768], P('section', 'fsdp'), may hold values from -0.109375 to 0.109375
- bias_down: bfloat16 [2, 768], P('section', 'fsdp'), may hold values from -3 to 3
Outputs:
- layer_out: bfloat16 [2, 2, 16, 640, 768], P('section', None, 'fsdp', 'seq')
- input_grad: bfloat16 [2, 2, 16, 640, 768], P('section', None, 'fsdp', 'seq')
- grad_gain_one: float32 [2, 768], P('section', 'fsdp')
- grad_shift_one: float32 [2, 768], P('section', 'fsdp')
- grad_w_qkv: float32 [2, 768, 2304], P('section', 'fsdp')
- grad_bias_query: float32 [2, 768], P('section', 'fsdp')
- grad_bias_value: float32 [2, 768], P('section', 'fsdp')
- grad_w_out: float32 [2, 768, 768], P('section', 'fsdp')
- grad_bias_out: float32 [2, 768], P('section', 'fsdp')
- grad_gain_two: float32 [2, 768], P('section', 'fsdp')
- grad_shift_two: float32 [2, 768], P('section', 'fsdp')
- grad_w_up: float32 [2, 768, 3072], P('section', 'fsdp')
- grad_bias_up: float32 [2, 3072], P('section', 'fsdp')
- grad_w_down: float32 [2, 3072, 768], P('section', 'fsdp')
- grad_bias_down: float32 [2, 768], P('section', 'fsdp')
The draws below stay inside these ranges and needn't reach their ends.
Inputs may be any that keep to these rules, and one draw needn't show every extreme that they name: For each image the 4 counts sum to 577 and at least one of them is 160; slots j < count of an index of seq hold live tokens, the others are padding.
All inputs are finite; a program needn't handle non-finite values.
Results may differ from the reference program's by a relative error of at most 0.019.
Values may be sent and summed in bfloat16 or wider, within the bound.
A program may use at most 256 MiB of HBM per device.

```python
import math
import jax
import jax.numpy as jnp
import numpy as np
from jax import lax

D = 768
HEADS = 12
HD = 64
FF = 3072
SEQ = 577
CAP = 160
MB = 2
IMAGES_MB = 16
SLOTS = 640
N_SECTION = 2
N_SEQ = 4


def block_scale(stream_key, extent, split, smallest, high):
    loudness, own = 1.0, jax.random.fold_in(stream_key, 6)
    for dim, parts in split:
        steps = jnp.exp(jax.random.uniform(jax.random.fold_in(own, dim), (parts,), jnp.float32, smallest / len(split), high / len(split)))
        loudness = loudness * jnp.repeat(steps, extent[dim] // parts).reshape([-1 if axis == dim else 1 for axis in range(len(extent))])
    return loudness


def split_up(number_of, total, most, slope):
    weights = [(1 << 20) // math.isqrt(standing ** slope) + 1 for standing in range(2, number_of + 1)]
    spare, given = total - most - (number_of - 1), [1] * (number_of - 1)
    while spare > 0:
        movable = [i for i in range(number_of - 1) if given[i] < most]
        pool, remaining = sum([weights[i] for i in movable]), spare
        for i in movable:
            extra = min(most - given[i], max(1, remaining * weights[i] // pool), spare)
            given[i] = given[i] + extra
            spare = spare - extra
    return np.array([most] + given)


def uneven(key, count, total, limit, skew):
    if count == 2:
        one = jax.random.randint(key, (), max(1, total - limit), min(limit, total - 1) + 1)
        return jnp.stack([one, total - one])
    lengths = jnp.asarray(split_up(count, total, limit, skew), jnp.int32)
    twos = (count - 1) // 2
    source_of, sink = lengths[1:1 + 2 * twos:2], lengths[2:2 + 2 * twos:2]
    room = jnp.minimum(source_of - 1, limit - sink)
    moved = jax.random.randint(jax.random.fold_in(key, 1), (twos,), 0, 1 << 20) % (room + 1)
    lengths = lengths.at[1:1 + 2 * twos:2].set(source_of - moved).at[2:2 + 2 * twos:2].set(sink + moved)
    return lengths[jax.random.permutation(jax.random.fold_in(key, 2), count)]


def scatter_about(key, extent, width, limit, split=(), held_as=jnp.bfloat16):
    gain = block_scale(key, extent, split, -0.22, 0.18) if split else 1.0
    array = jax.random.normal(key, extent, jnp.float32) * width * gain
    return jnp.minimum(jnp.maximum(array, -limit), limit).astype(held_as)


def setup_inputs(seed: int = 0) -> dict:
    arg_keys = jax.random.split(jax.random.key(seed), 17)
    return {
        "images_in": scatter_about(arg_keys[0], (MB, IMAGES_MB, SLOTS, D), 1.0, 6.0, ((1, 16), (2, 4))),
        "counts": jax.vmap(lambda own: uneven(own, N_SEQ, SEQ, CAP, 2))(jax.random.split(arg_keys[1], MB * IMAGES_MB)).reshape((MB, IMAGES_MB, N_SEQ)).astype(jnp.int32),
        "cotangent": scatter_about(arg_keys[2], (MB, IMAGES_MB, SLOTS, D), 1.0, 6.0, ((1, 16), (2, 4))),
        "gain_one": jnp.clip(0.5 + 1.0 * jax.random.uniform(arg_keys[3], (N_SECTION, D), jnp.float32) ** block_scale(arg_keys[3], (N_SECTION, D), ((0, 2), (1, 16)), -0.2, 0.2), 0.5, 1.5).astype(jnp.bfloat16),
        "shift_one": scatter_about(arg_keys[4], (N_SECTION, D), 0.3, 3.0, ((0, 2), (1, 16))),
        "w_qkv": scatter_about(arg_keys[5], (N_SECTION, D, 3 * D), D ** -0.5, 0.21875, ((0, 2), (1, 16))),
        "bias_query": scatter_about(arg_keys[6], (N_SECTION, D), 0.5, 3.0, ((0, 2), (1, 16))),
        "bias_value": scatter_about(arg_keys[7], (N_SECTION, D), 0.5, 3.0, ((0, 2), (1, 16))),
        "w_out": scatter_about(arg_keys[8], (N_SECTION, D, D), 4 ** -0.5, 3.0, ((0, 2), (1, 16))),
        "bias_out": scatter_about(arg_keys[9], (N_SECTION, D), 0.3, 3.0, ((0, 2), (1, 16))),
        "gain_two": jnp.clip(0.5 + 1.0 * jax.random.uniform(arg_keys[10], (N_SECTION, D), jnp.float32) ** block_scale(arg_keys[10], (N_SECTION, D), ((0, 2), (1, 16)), -0.2, 0.2), 0.5, 1.5).astype(jnp.bfloat16),
        "shift_two": scatter_about(arg_keys[11], (N_SECTION, D), 0.3, 3.0, ((0, 2), (1, 16))),
        "w_up": scatter_about(arg_keys[12], (N_SECTION, D, FF), D ** -0.5, 0.21875, ((0, 2), (1, 16))),
        "bias_up": scatter_about(arg_keys[13], (N_SECTION, FF), 0.5, 3.0, ((0, 2), (1, 16))),
        "w_down": scatter_about(arg_keys[14], (N_SECTION, FF, D), FF ** -0.5, 0.109375, ((0, 2), (1, 16))),
        "bias_down": scatter_about(arg_keys[15], (N_SECTION, D), 0.3, 3.0, ((0, 2), (1, 16))),
    }


@jax.custom_vjp
def low(v):
    return lax.optimization_barrier(v.astype(jnp.bfloat16)).astype(jnp.float32)

@jax.custom_vjp
def low_back(v):
    return v

def low_keep(v):
    return (low(v), None)

def low_pass(kept, grad):
    return (grad,)

def back_keep(v):
    return (v, None)

def back_low(kept, grad):
    return (low(grad),)
low.defvjp(low_keep, low_pass)
low_back.defvjp(back_keep, back_low)
epsilon = 1e-06
masked_score = -1000000000.0

def layer_norm(values, gain_vector, offset):
    average = lax.optimization_barrier(jnp.mean(values, axis=-1, keepdims=True))
    centered = values - average
    spread = lax.optimization_barrier(jnp.mean(centered * centered, axis=-1, keepdims=True))
    return centered * lax.rsqrt(spread + epsilon) * gain_vector + offset

def gelu_tanh(values):
    return jax.nn.gelu(values, approximate=True)

def attend_image(packed):
    triples, key_valid = packed
    query_side = triples[:, 0]
    key_side = triples[:, 1]
    value_side = triples[:, 2]
    scores = jnp.einsum('qhd,khd->hqk', query_side, key_side, precision=lax.Precision.HIGHEST) * HD ** (-0.5)
    scores = low_back(scores)
    scores = jnp.where(key_valid[None, None, :] > 0, scores, masked_score)
    weights_soft = jax.nn.softmax(scores, axis=-1)
    return jnp.einsum('hqk,khd->qhd', low(weights_soft), value_side, precision=lax.Precision.HIGHEST)

def layer(inputs, valid_rows, key_valid, params):
    gain_one, shift_one, w_qkv, bias_query, bias_value, w_out, bias_out, gain_two, shift_two, w_up, bias_up, w_down, bias_down = params
    highest = lax.Precision.HIGHEST
    images = key_valid.shape[0]
    normed = low(layer_norm(inputs, gain_one, shift_one))
    bias_all = jnp.concatenate([bias_query, jnp.zeros_like(bias_query), bias_value])
    triples = low(low_back(jnp.dot(normed, w_qkv, precision=highest, preferred_element_type=jnp.float32) + bias_all))
    triples = triples.reshape(images, SLOTS, 3, HEADS, HD)
    mixture = lax.map(jax.checkpoint(attend_image), (triples, key_valid))
    mixture = low(low_back(mixture.reshape(images * SLOTS, D)))
    middle = inputs + low_back(jnp.dot(mixture, w_out, precision=highest, preferred_element_type=jnp.float32) + bias_out)
    normed_two = low(layer_norm(middle, gain_two, shift_two))
    hidden = low_back(jnp.dot(normed_two, w_up, precision=highest, preferred_element_type=jnp.float32) + bias_up)
    activated = low(gelu_tanh(hidden))
    branch_two = low_back(jnp.dot(activated, w_down, precision=highest, preferred_element_type=jnp.float32) + bias_down)
    return (middle + branch_two) * valid_rows[:, None]

def reference(images_in, counts, cotangent, gain_one, shift_one, w_qkv, bias_query, bias_value, w_out, bias_out, gain_two, shift_two, w_up, bias_up, w_down, bias_down):
    image_count = MB * IMAGES_MB
    flat_input = images_in.astype(jnp.float32).reshape(image_count * SLOTS, D)
    count_table = counts.reshape(image_count, N_SEQ).astype(jnp.int32)
    positions = jnp.arange(CAP, dtype=jnp.int32)
    key_valid = (positions[None, None, :] < count_table[:, :, None]).astype(jnp.float32).reshape(image_count, SLOTS)
    valid_rows = key_valid.reshape(image_count * SLOTS)
    params = tuple((member.astype(jnp.float32) for member in (gain_one, shift_one, w_qkv, bias_query, bias_value, w_out, bias_out, gain_two, shift_two, w_up, bias_up, w_down, bias_down)))
    link_zero = jnp.zeros_like(flat_input)

    def forward(flat_values, param_values, link_values):
        first_out = layer(flat_values, valid_rows, key_valid, tuple((member[0] for member in param_values)))
        passed = low(low_back(first_out + link_values))
        second = layer(passed, valid_rows, key_valid, tuple((member[1] for member in param_values)))
        return (passed, second)
    (passed, second), pullback = jax.vjp(forward, flat_input, params, link_zero)
    cot_flat = cotangent.astype(jnp.float32).reshape(image_count * SLOTS, D)
    grad_flat, grad_params, grad_link = pullback((jnp.zeros_like(passed), cot_flat))
    shape_out = (N_SECTION, MB, IMAGES_MB, SLOTS, D)
    layer_out = jnp.stack([passed, second]).reshape(shape_out).astype(jnp.bfloat16)
    input_grad = jnp.stack([grad_flat, grad_link]).reshape(shape_out).astype(jnp.bfloat16)
    return (layer_out, input_grad, grad_params[0], grad_params[1], grad_params[2], grad_params[3], grad_params[4], grad_params[5], grad_params[6], grad_params[7], grad_params[8], grad_params[9], grad_params[10], grad_params[11], grad_params[12])
```

```python
import functools

import jax
import jax.numpy as jnp
from jax import lax
from jax.experimental import pallas as pl
from jax.experimental.pallas import tpu as pltpu
from jax.sharding import PartitionSpec as P

HD = 64
epsilon = 1e-06
masked_score = -1000000000.0
MESH = pl.DeviceIdType.MESH
bf16 = jnp.bfloat16
f32 = jnp.float32
VMEM_LIMIT = 56 * 1024 * 1024


def nn(a, b):
    return jnp.dot(a, b, preferred_element_type=f32)


def nt(a, b):
    return lax.dot_general(a, b, (((1,), (1,)), ((), ())), preferred_element_type=f32)


def tn(a, b):
    return lax.dot_general(a, b, (((0,), (0,)), ((), ())), preferred_element_type=f32)


def norm_parts(values):
    average = jnp.mean(values, axis=-1, keepdims=True)
    centered = values - average
    spread = jnp.mean(centered * centered, axis=-1, keepdims=True)
    inverse = lax.rsqrt(spread + epsilon)
    return centered * inverse, inverse


def norm_back(incoming, gain, xhat, inverse):
    e = incoming * gain
    inner = jnp.mean(e * xhat, axis=-1, keepdims=True)
    return (e - jnp.mean(e, axis=-1, keepdims=True) - xhat * inner) * inverse


def gelu_both(v):
    c = 0.7978845608028654
    square = v * v
    t = jnp.tanh(c * v * (1.0 + 0.044715 * square))
    half = 0.5 * (1.0 + t)
    slope = half + 0.5 * v * (1.0 - t * t) * (c * (1.0 + 0.134145 * square))
    return v * half, slope


def row_valid(counts, batch, cap, index):
    pos = lax.broadcasted_iota(jnp.int32, (cap, 1), 0)
    return jnp.concatenate([pos < counts[b, index] for b in range(batch)], axis=0)


def key_valid(counts, b, cap, sources):
    pos = lax.broadcasted_iota(jnp.int32, (cap, 1), 0)
    return jnp.concatenate([pos < counts[b, s] for s in sources], axis=0)


def greet(axis_ids):
    barrier = pltpu.get_barrier_semaphore()
    for ids in axis_ids:
        pl.semaphore_signal(barrier, inc=1, device_id=ids, device_id_type=MESH)
    pl.semaphore_wait(barrier, len(axis_ids))


def remote(src, dst, ssem, rsem, ids):
    return pltpu.make_async_remote_copy(
        src_ref=src, dst_ref=dst, send_sem=ssem, recv_sem=rsem, device_id=ids, device_id_type=MESH
    )


def load_weights(shards, wq_h, wo_h, wu_h, wd_h, wq, wo, wu, wd, sems, order):
    def start_q():
        rows = wq_h.shape[2]
        for f in range(shards):
            pltpu.make_async_copy(
                wq_h.at[f], wq.at[:, pl.ds(f * rows, rows), :], sems.at[0]
            ).start()

    starts = {
        "q": start_q,
        "o": lambda: pltpu.make_async_copy(wo_h, wo, sems.at[1]).start(),
        "u": lambda: pltpu.make_async_copy(wu_h, wu, sems.at[2]).start(),
        "d": lambda: pltpu.make_async_copy(wd_h, wd, sems.at[3]).start(),
    }
    for name in order:
        starts[name]()

    def wait(name):
        i, ref = {"q": (0, wq), "o": (1, wo), "u": (2, wu), "d": (3, wd)}[name]
        pltpu.make_async_copy(ref, ref, sems.at[i]).wait()

    return wait


def forward_kernel(
    shape,
    counts, own, got, gain1, shift1, bqkv, bo, gain2, shift2, bu, bd, wq_h, wo_h, wu_h, wd_h,
    y_out, next_out, qkv_out, lse_out, normed_out, mid_out, merged_out, n2_out, act_out, slope_out,
    wq, wo, wu, wd, sendq, recvq, senda, recva, land, wsem, sq, rq, sa, ra, ss, rs,
):
    batch, cap, seqs, shards, chunks = shape
    rows = batch * cap
    me = lax.axis_index("seq")
    sec = lax.axis_index("section")
    ahead = [lax.rem(me + d, seqs) for d in range(seqs)]
    behind = [lax.rem(me + seqs - d, seqs) for d in range(seqs)]
    peers = [{"seq": ahead[d]} for d in range(1, seqs)] + [{"section": 1 - sec}]
    wait_weight = load_weights(
        shards, wq_h, wo_h, wu_h, wd_h, wq, wo, wu, wd, wsem, ("q", "o", "u", "d")
    )
    x = jnp.where(sec == 0, own[...], got[...]).astype(f32)
    xhat, _ = norm_parts(x)
    normed = (xhat * gain1[...].astype(f32) + shift1[...].astype(f32)).astype(bf16)
    normed_out[...] = normed
    greet(peers)
    wait_weight("q")
    copies = []
    for d in list(range(1, seqs)) + [0]:
        t = ahead[d]
        res = (nn(normed_out[...], wq[t]) + bqkv[t].astype(f32)).astype(bf16)
        res = res.reshape(batch, cap, res.shape[-1])
        if d == 0:
            recvq[0] = res
        else:
            sendq[d - 1] = res
            copy = remote(sendq.at[d - 1], recvq.at[d], sq.at[d - 1], rq.at[d - 1], {"seq": t})
            copy.start()
            copies.append(copy)
    for copy in copies:
        copy.wait()
    keep = pltpu.make_async_copy(recvq, qkv_out, wsem.at[4])
    keep.start()
    width = recvq.shape[-1] // 3
    heads = width // HD
    lane = lax.broadcasted_iota(jnp.int32, (1, width), 1) // HD
    back = []
    for b in range(batch):
        qkv = recvq[:, b].reshape(seqs * cap, 3 * width)
        q, k, v = (qkv[:, i * width : (i + 1) * width] for i in range(3))
        q = q * jnp.asarray(HD ** (-0.5), bf16)
        vt = v.T
        live = key_valid(counts, b, cap, behind)
        outs = []
        for h in range(heads):
            qm = jnp.where(lane == h, q, jnp.zeros_like(q))
            s = jnp.where(live, nt(k, qm), masked_score)
            highest = jnp.max(s, axis=0, keepdims=True)
            raised = jnp.exp(s - highest)
            total = jnp.sum(raised, axis=0, keepdims=True)
            p = (raised * (1.0 / total)).astype(bf16)
            outs.append(nn(vt[h * HD : (h + 1) * HD], p))
            lse_out[b, h : h + 1, :] = highest + jnp.log(total)
        o = jnp.concatenate(outs, axis=0).T.astype(bf16).reshape(seqs, cap, width)
        recva[0, b] = o[0]
        for d in range(1, seqs):
            senda[d - 1, b] = o[d]
            copy = remote(
                senda.at[d - 1, b], recva.at[d, b], sa.at[d - 1, b], ra.at[d - 1, b], {"seq": behind[d]}
            )
            copy.start()
            back.append(copy)
    wait_weight("o")
    mid = jnp.where(sec == 0, own[...], got[...]).astype(f32) + bo[...].astype(f32)
    for copy in back:
        copy.wait()
    for d in range(seqs):
        part = recva[d].reshape(rows, width)
        merged_out[ahead[d]] = part
        mid = mid + nn(part, wo[ahead[d]])
    mid_out[...] = mid
    xhat2, _ = norm_parts(mid)
    n2_out[...] = (xhat2 * gain2[...].astype(f32) + shift2[...].astype(f32)).astype(bf16)
    wait_weight("u")
    wait_weight("d")
    total = None
    size = wu.shape[1] // chunks
    for c in range(chunks):
        part = slice(c * size, (c + 1) * size)
        hidden = nn(n2_out[...], wu[:, part]) + bu[:, part].astype(f32)
        activated, slope = gelu_both(hidden)
        activated = activated.astype(bf16)
        act_out[:, part] = activated
        slope_out[:, part] = slope.astype(bf16)
        term = nn(activated, wd[part])
        total = term if total is None else total + term
    live_rows = row_valid(counts, batch, cap, me)
    y = mid_out[...] + (total + bd[...].astype(f32))
    y_out[...] = jnp.where(live_rows, y, 0.0).astype(bf16)
    hop = remote(y_out, land, ss, rs, {"section": 1 - sec})
    hop.start()
    hop.wait()
    next_out[...] = land[...]
    keep.wait()


def backward_kernel(
    shape,
    counts, own, got, cot, ggot, lse, normed, mid, act, slope, gain1, gain2, qkv_h, wq_h, wo_h, wu_h, wd_h,
    dx_out, next_out, ddown_out, dhid_out, dbranch_out, dqkv_out, dgain1, dshift1, dbqkv, dbo, dgain2, dshift2, dbu, dbd,
    wq, wo, wu, wd, qkv, senda, recva, sendq, recvq, land, dmid, wsem, sa, ra, sq, rq, ss, rs,
):
    batch, cap, seqs, shards, chunks = shape
    rows = batch * cap
    me = lax.axis_index("seq")
    sec = lax.axis_index("section")
    ahead = [lax.rem(me + d, seqs) for d in range(seqs)]
    behind = [lax.rem(me + seqs - d, seqs) for d in range(seqs)]
    peers = [{"seq": ahead[d]} for d in range(1, seqs)] + [{"section": 1 - sec}]
    wait_weight = load_weights(
        shards, wq_h, wo_h, wu_h, wd_h, wq, wo, wu, wd, wsem, ("d", "u", "o", "q")
    )
    fetch = pltpu.make_async_copy(qkv_h, qkv, wsem.at[4])
    fetch.start()
    live_rows = row_valid(counts, batch, cap, me)
    g = jnp.where(sec == 0, ggot[...], cot[...])
    ddown_out[...] = jnp.where(live_rows, g.astype(f32), 0.0).astype(bf16)
    greet(peers)
    wait_weight("d")
    wait_weight("u")
    h2 = None
    size = wu.shape[1] // chunks
    for c in range(chunks):
        part = slice(c * size, (c + 1) * size)
        da = nt(ddown_out[...], wd[part])
        dh = (da * slope[:, part].astype(f32)).astype(bf16)
        dhid_out[:, part] = dh
        term = nt(dh, wu[:, part])
        h2 = term if h2 is None else h2 + term
    xhat2, inverse2 = norm_parts(mid[...])
    dmid[...] = ddown_out[...].astype(f32) + norm_back(h2, gain2[...].astype(f32), xhat2, inverse2)
    dbranch_out[...] = dmid[...].astype(bf16)
    wait_weight("o")
    copies = []
    for d in list(range(1, seqs)) + [0]:
        t = ahead[d]
        res = nt(dbranch_out[...], wo[t]).astype(bf16)
        res = res.reshape(batch, cap, res.shape[-1])
        if d == 0:
            recva[0] = res
        else:
            senda[d - 1] = res
            copy = remote(senda.at[d - 1], recva.at[d], sa.at[d - 1], ra.at[d - 1], {"seq": t})
            copy.start()
            copies.append(copy)
    dgain2[...] = jnp.sum(h2 * xhat2, axis=0, keepdims=True)
    dshift2[...] = jnp.sum(h2, axis=0, keepdims=True)
    dbd[...] = jnp.sum(ddown_out[...].astype(f32), axis=0, keepdims=True)
    dbo[...] = jnp.sum(dbranch_out[...].astype(f32), axis=0, keepdims=True)
    for c in range(chunks):
        part = slice(c * size, (c + 1) * size)
        dbu[:, part] = jnp.sum(dhid_out[:, part].astype(f32), axis=0, keepdims=True)
    fetch.wait()
    for copy in copies:
        copy.wait()
    width = qkv.shape[-1] // 3
    heads = width // HD
    lane = lax.broadcasted_iota(jnp.int32, (1, width), 1) // HD
    back = []
    for b in range(batch):
        packed = qkv[:, b].reshape(seqs * cap, 3 * width)
        q, k, v = (packed[:, i * width : (i + 1) * width] for i in range(3))
        q = q * jnp.asarray(HD ** (-0.5), bf16)
        kt = k.T
        da = recva[:, b].reshape(seqs * cap, width)
        live = key_valid(counts, b, cap, behind)
        dk = dv = None
        dqt = []
        for h in range(heads):
            qm = jnp.where(lane == h, q, jnp.zeros_like(q))
            dam = jnp.where(lane == h, da, jnp.zeros_like(da))
            s = jnp.where(live, nt(k, qm), masked_score)
            p = jnp.exp(s - lse[b, h : h + 1, :])
            dp = nt(v, dam)
            inner = jnp.sum(p * dp, axis=0, keepdims=True)
            ds = (p * (dp - inner)).astype(bf16)
            dvh = nn(p.astype(bf16), dam)
            dkh = nn(ds, qm)
            dv = dvh if dv is None else dv + dvh
            dk = dkh if dk is None else dk + dkh
            dqt.append(nn(kt[h * HD : (h + 1) * HD], ds))
        dq = jnp.concatenate(dqt, axis=0).T * HD ** (-0.5)
        grads = jnp.concatenate([dq.astype(bf16), dk.astype(bf16), dv.astype(bf16)], axis=1)
        grads = grads.reshape(seqs, cap, 3 * width)
        recvq[0, b] = grads[0]
        for d in range(1, seqs):
            sendq[d - 1, b] = grads[d]
            copy = remote(
                sendq.at[d - 1, b], recvq.at[d, b], sq.at[d - 1, b], rq.at[d - 1, b], {"seq": behind[d]}
            )
            copy.start()
            back.append(copy)
    x = jnp.where(sec == 0, own[...], got[...]).astype(f32)
    xhat1, inverse1 = norm_parts(x)
    wait_weight("q")
    for copy in back:
        copy.wait()
    h1 = None
    for d in range(seqs):
        t = ahead[d]
        part = recvq[d].reshape(rows, 3 * width)
        dqkv_out[t] = part
        dbqkv[t] = jnp.sum(part.astype(f32), axis=0, keepdims=True)
        term = nt(part, wq[t])
        h1 = term if h1 is None else h1 + term
    dx = dmid[...] + norm_back(h1, gain1[...].astype(f32), xhat1, inverse1)
    dx_out[...] = dx.astype(bf16)
    hop = remote(dx_out, land, ss, rs, {"section": 1 - sec})
    hop.start()
    dgain1[...] = jnp.sum(h1 * xhat1, axis=0, keepdims=True)
    dshift1[...] = jnp.sum(h1, axis=0, keepdims=True)
    hop.wait()
    next_out[...] = land[...]


LINKS = ("x", "yl", "zl", "yh", "zh")


def position():
    f, z = lax.axis_index("fsdp"), lax.axis_index("seq")
    y = lax.div(f, 4)
    c, x = lax.rem(f, 2), lax.rem(lax.div(f, 2), 2)
    yh, zh = lax.div(y, 2), lax.div(z, 2)
    bits = {"c": c, "x": x, "yh": yh, "zh": zh, "yl": lax.rem(y + yh, 2), "zl": lax.rem(z + zh, 2)}
    low = lax.rem(f, 4)
    partner = {
        "c": {"fsdp": f + 1 - 2 * c},
        "x": {"fsdp": f + 2 - 4 * x},
        "yl": {"fsdp": 4 * (y + 1 - 2 * lax.rem(y, 2)) + low},
        "yh": {"fsdp": 4 * (3 - y) + low},
        "zl": {"seq": z + 1 - 2 * lax.rem(z, 2)},
        "zh": {"seq": 3 - z},
    }
    return f, bits, partner


def owner_bits(f):
    y = f // 4
    return {"c": f % 2, "x": (f // 2) % 2, "yh": y // 2, "yl": (y + y // 2) % 2}


def link_of(portion, step):
    return LINKS[(portion + step) % 5]


def piece_of(portion, bits):
    return sum(bits[link_of(portion, s)] << (4 - s) for s in range(5))


def row_groups(start, count):
    row, end = start, start + count
    while row < end:
        portion = min(row // 128, 4)
        size = 32 if portion < 4 else 16
        inner = row - 128 * portion
        take = min(end - row, size - inner % size)
        yield portion, inner // size, inner % size, row - start, take
        row += take


def weight_grad_kernel(
    shape,
    act, ddown, n2, dhid, merged, dbranch, normed, dqkv, dg1, ds1, dbqkv, dbo, dg2, ds2, dbd, dbu,
    gdown, gup, gout, gqkv, og1, os1, obq, obv, obo, og2, os2, obd, obu,
    *scratch,
):
    batch, cap, seqs, shards, chunks = shape
    held, core_in, step_in, final = (scratch[5 * i : 5 * i + 5] for i in range(4))
    vec, vec_in, csem, ssem, zsem, vsem = scratch[20:]
    f, bits, partner = position()
    c = bits["c"]
    greet([partner[n] for n in ("c", "x", "yl", "yh", "zl", "zh")])
    features = ddown.shape[1]
    owned = features // shards

    width = dqkv.shape[2] // 3
    vec[0] = jnp.concatenate(
        [dg1[...], ds1[...]]
        + [jnp.concatenate([dbqkv[t][:, j * width : (j + 1) * width] for t in range(seqs)], axis=1) for j in (0, 2)]
        + [dbo[...], dg2[...], ds2[...], dbd[...]]
        + [dbu[:, j * features : (j + 1) * features] for j in range(chunks)]
        + [jnp.zeros((4, features), f32)],
        axis=0,
    )

    def vec_copy(s):
        name = ("c", "x", "yl", "yh", "zl", "zh")[s]
        return remote(vec.at[s], vec_in.at[s], vsem.at[0, s], vsem.at[1, s], partner[name])

    def vec_step(s):
        copy = vec_copy(s)
        copy.wait()
        vec[s + 1] = vec[s] + vec_in[s]
        if s < 5:
            vec_copy(s + 1).start()

    def put(owner, start, value):
        value = value.astype(bf16)
        own = owner_bits(owner)
        for portion, quarter, inner, at, take in row_groups(start, value.shape[0]):
            place = piece_of(portion, {**own, "zh": quarter // 2, "zl": quarter % 2})
            held[portion][own["c"], place, inner : inner + take] = value[at : at + take]

    def core_copy(i, half):
        b = bits[link_of(i, 0)]
        at = pl.ds(16 * (1 - b if half == 0 else b), 16)
        return remote(
            held[i].at[1 - c, at], core_in[i].at[at], csem.at[0, i, half], csem.at[1, i, half], partner["c"]
        )

    def ready(i):
        core_copy(i, 0).start()
        core_copy(i, 1).start()

    vec_copy(0).start()
    part = lambda j: slice(j * features, (j + 1) * features)
    for j in range(chunks):
        res = tn(act[:, part(j)], ddown[...])
        for k in range(4):
            put(4 * j + k, 0, res[4 * owned * k : 4 * owned * (k + 1)])
    ready(0)
    for j in range(chunks):
        res = tn(n2[...], dhid[:, part(j)])
        for k in range(shards):
            put(k, 192 + owned * j, res[owned * k : owned * (k + 1)])
        if j == 1:
            ready(1)
    ready(2)
    for t in range(seqs):
        res = tn(merged[t], dbranch[...])
        for k in range(4):
            put(4 * t + k, 384, res[owned * k : owned * (k + 1)])
    for j in range(3):
        right = jnp.concatenate([dqkv[t][:, j * width : (j + 1) * width] for t in range(seqs)], axis=1)
        res = tn(normed[...], right)
        for k in range(shards):
            put(k, 432 + owned * j, res[owned * k : owned * (k + 1)])
    ready(3)
    ready(4)

    def add_into(i, base, source, at, count):
        group = min(count, 4)

        def body(k, carry):
            here = pl.ds(base + group * k, group)
            held[i][c, here] = held[i][c, here] + source[pl.ds(at + group * k, group)]
            return carry

        lax.fori_loop(0, count // group, body, 0)

    bases = [0] * 5

    def step_copy(i, s, base):
        name = link_of(i, s)
        half = 16 >> s
        at = 32 - 2 * half
        return remote(
            held[i].at[c, pl.ds(base + (1 - bits[name]) * half, half)],
            step_in[i].at[pl.ds(at, half)],
            ssem.at[0, i, s],
            ssem.at[1, i, s],
            partner[name],
        )

    for i in range(5):
        core_copy(i, 0).wait()
        b = bits[link_of(i, 0)]
        add_into(i, 16 * (1 - b), core_in[i], 16 * (1 - b), 16)
        step_copy(i, 0, 0).start()
    vec_step(0)
    for i in range(5):
        core_copy(i, 1).wait()
        b = bits[link_of(i, 0)]
        add_into(i, 16 * b, core_in[i], 16 * b, 16)
    own_at = []
    for s in range(5):
        for i in range(5):
            half = 16 >> s
            copy = step_copy(i, s, bases[i])
            bases[i] = bases[i] + bits[link_of(i, s)] * half
            copy.wait()
            add_into(i, bases[i], step_in[i], 32 - 2 * half, half)
            if s < 4:
                step_copy(i, s + 1, bases[i]).start()
        vec_step(s + 1)

    def z_copy(i, s):
        first, second = ("zl", "zh") if i % 2 == 0 else ("zh", "zl")
        if s == 0:
            at, to = pl.ds(2 * bits[second] + bits[first], 1), partner[first]
        else:
            at, to = pl.ds(2 * bits[second], 2), partner[second]
        return remote(final[i].at[at], final[i].at[at], zsem.at[0, i, s], zsem.at[1, i, s], to)

    for i in range(5):
        first, second = ("zl", "zh") if i % 2 == 0 else ("zh", "zl")
        final[i][2 * bits[second] + bits[first]] = held[i][c, bases[i]]
        z_copy(i, 0).start()
    for i in range(5):
        z_copy(i, 0).wait()
        z_copy(i, 1).start()
    total = vec[6]
    mine = pltpu.roll(total, lax.rem(features - f * owned, features), 1)
    for r, out in enumerate((og1, os1, obq, obv, obo, og2, os2, obd)):
        out[...] = mine[r : r + 1, :owned]
    wide = 4 * owned
    quarter = pltpu.roll(total, lax.rem(features - lax.rem(f, 4) * wide, features), 1)
    chosen = lax.broadcasted_iota(jnp.int32, (16, 1), 0) == 8 + lax.div(f, 4)
    obu[...] = jnp.sum(jnp.where(chosen, quarter, 0.0), axis=0, keepdims=True)[:, :wide]
    for i in range(5):
        z_copy(i, 1).wait()

    def share(start, count):
        got = []
        for portion, quarter, inner, _, take in row_groups(start, count):
            zh, zl = quarter // 2, quarter % 2
            place = 2 * zh + zl if portion % 2 == 0 else 2 * zl + zh
            got.append(final[portion][place, inner : inner + take])
        return jnp.concatenate(got, axis=0)

    gdown[...] = share(0, 4 * owned)
    for j in range(chunks):
        gup[:, part(j)] = share(192 + owned * j, owned)
    gout[...] = share(384, owned)
    for j in range(3):
        gqkv[:, part(j)] = share(432 + owned * j, owned)


def per_device(
    images_in, counts, cotangent, gain_one, shift_one, w_qkv, bias_query, bias_value, w_out,
    bias_out, gain_two, shift_two, w_up, bias_up, w_down, bias_down,
):
    micro, images, cap, features = images_in.shape
    batch = micro * images
    seqs = lax.axis_size("seq")
    shards = lax.axis_size("fsdp")
    rows = batch * cap
    width = features // seqs
    owned = features // shards
    ff = w_up.shape[-1]
    chunks = ff // features

    def blocks_of(columns):
        return columns.reshape(-1, 3, seqs, width).transpose(2, 0, 1, 3).reshape(seqs, -1, 3 * width)

    def gathered(a):
        return lax.all_gather(a, "fsdp", axis=0, tiled=True)

    small = jnp.concatenate(
        [gain_one[0], shift_one[0], bias_query[0], bias_value[0], bias_out[0], gain_two[0],
         shift_two[0], bias_down[0], bias_up[0]]
    )
    small = lax.all_gather(small, "fsdp", axis=0, tiled=False)
    vec = [small[:, i * owned : (i + 1) * owned].reshape(1, features) for i in range(8)]
    g1, s1, bq, bv, bo, g2, s2, bd = vec
    bu = small[:, 8 * owned :].reshape(1, ff)
    bqkv = jnp.concatenate([bq, jnp.zeros_like(bq), bv], axis=1)
    bqkv = blocks_of(bqkv)
    wq_h = lax.all_gather(blocks_of(w_qkv[0]), "fsdp", axis=0, tiled=False)
    wo_h = gathered(w_out[0]).reshape(seqs, width, features)
    wu_h = gathered(w_up[0])
    wd_h = gathered(w_down[0])

    own = images_in.reshape(rows, features)
    cot = cotangent.reshape(rows, features)
    table = counts.reshape(batch, seqs)
    shape = (batch, cap, seqs, shards, chunks)
    vmem = pl.BlockSpec(memory_space=pltpu.VMEM)
    smem = pl.BlockSpec(memory_space=pltpu.SMEM)
    hbm = pl.BlockSpec(memory_space=pl.ANY)
    weight_scratch = [
        pltpu.VMEM((seqs, features, 3 * width), bf16),
        pltpu.VMEM((seqs, width, features), bf16),
        pltpu.VMEM((features, ff), bf16),
        pltpu.VMEM((ff, features), bf16),
    ]
    dma = pltpu.SemaphoreType.DMA
    sds = jax.ShapeDtypeStruct

    def forward(got):
        return pl.pallas_call(
            functools.partial(forward_kernel, shape),
            name="forward_stage",
            out_shape=(
                sds((rows, features), bf16),
                sds((rows, features), bf16),
                sds((seqs, batch, cap, 3 * width), bf16),
                sds((batch, 8, seqs * cap), f32),
                sds((rows, features), bf16),
                sds((rows, features), f32),
                sds((seqs, rows, width), bf16),
                sds((rows, features), bf16),
                sds((rows, ff), bf16),
                sds((rows, ff), bf16),
            ),
            in_specs=[smem] + [vmem] * 10 + [hbm] * 4,
            out_specs=[vmem, vmem, hbm] + [vmem] * 7,
            scratch_shapes=weight_scratch
            + [
                pltpu.VMEM((seqs - 1, batch, cap, 3 * width), bf16),
                pltpu.VMEM((seqs, batch, cap, 3 * width), bf16),
                pltpu.VMEM((seqs - 1, batch, cap, width), bf16),
                pltpu.VMEM((seqs, batch, cap, width), bf16),
                pltpu.VMEM((rows, features), bf16),
                dma((5,)),
                dma((seqs - 1,)),
                dma((seqs - 1,)),
                dma((seqs - 1, batch)),
                dma((seqs - 1, batch)),
                dma,
                dma,
            ],
            compiler_params=pltpu.CompilerParams(
                collective_id=0, has_side_effects=True, vmem_limit_bytes=VMEM_LIMIT
            ),
        )(table, own, got, g1, s1, bqkv, bo, g2, s2, bu, bd, wq_h, wo_h, wu_h, wd_h)

    def backward(got, ggot, stash):
        qkv, lse, normed, mid, act, slope = stash
        vector = sds((1, features), f32)
        return pl.pallas_call(
            functools.partial(backward_kernel, shape),
            name="backward_stage",
            out_shape=(
                sds((rows, features), bf16),
                sds((rows, features), bf16),
                sds((rows, features), bf16),
                sds((rows, ff), bf16),
                sds((rows, features), bf16),
                sds((seqs, rows, 3 * width), bf16),
                vector,
                vector,
                sds((seqs, 1, 3 * width), f32),
                vector,
                vector,
                vector,
                sds((1, ff), f32),
                vector,
            ),
            in_specs=[smem] + [vmem] * 11 + [hbm] * 5,
            out_specs=[vmem] * 14,
            scratch_shapes=weight_scratch
            + [
                pltpu.VMEM((seqs, batch, cap, 3 * width), bf16),
                pltpu.VMEM((seqs - 1, batch, cap, width), bf16),
                pltpu.VMEM((seqs, batch, cap, width), bf16),
                pltpu.VMEM((seqs - 1, batch, cap, 3 * width), bf16),
                pltpu.VMEM((seqs, batch, cap, 3 * width), bf16),
                pltpu.VMEM((rows, features), bf16),
                pltpu.VMEM((rows, features), f32),
                dma((5,)),
                dma((seqs - 1,)),
                dma((seqs - 1,)),
                dma((seqs - 1, batch)),
                dma((seqs - 1, batch)),
                dma,
                dma,
            ],
            compiler_params=pltpu.CompilerParams(
                collective_id=1, has_side_effects=True, vmem_limit_bytes=VMEM_LIMIT
            ),
        )(table, own, got, cot, ggot, lse, normed, mid, act, slope, g1, g2, qkv, wq_h, wo_h, wu_h, wd_h)

    first = forward(own)
    y, _, qkv, lse, normed, mid, merged, n2, act, slope = forward(first[1])
    stash = (qkv, lse, normed, mid, act, slope)
    early = backward(first[1], cot, stash)
    dx, _, ddown, dhid, dbranch, dqkv, dg1, ds1, dbqkv, dbo, dg2, ds2, dbu, dbd = backward(
        first[1], early[1], stash
    )

    sizes = (32, 32, 32, 32, 16)
    vector = sds((1, owned), f32)
    grads = pl.pallas_call(
        functools.partial(weight_grad_kernel, shape),
        name="weight_gradients",
        out_shape=(
            sds((4 * owned, features), bf16),
            sds((owned, ff), bf16),
            sds((owned, features), bf16),
            sds((owned, 3 * features), bf16),
            *([vector] * 8),
            sds((1, 4 * owned), f32),
        ),
        in_specs=[vmem] * 16,
        out_specs=[vmem] * 13,
        scratch_shapes=[pltpu.VMEM((2, 32, r, features), bf16) for r in sizes]
        + [pltpu.VMEM((32, r, features), bf16) for r in sizes]
        + [pltpu.VMEM((32, r, features), bf16) for r in sizes]
        + [pltpu.VMEM((4, r, features), bf16) for r in sizes]
        + [
            pltpu.VMEM((7, 16, features), f32),
            pltpu.VMEM((6, 16, features), f32),
            dma((2, 5, 2)),
            dma((2, 5, 5)),
            dma((2, 5, 2)),
            dma((2, 6)),
        ],
        compiler_params=pltpu.CompilerParams(
            collective_id=2, has_side_effects=True, vmem_limit_bytes=VMEM_LIMIT
        ),
    )(act, ddown, n2, dhid, merged, dbranch, normed, dqkv, dg1, ds1, dbqkv, dbo, dg2, ds2, dbd, dbu)
    gw_down, gw_up, gw_out, gw_qkv = (g.astype(f32)[None] for g in grads[:4])
    gg1, gs1, gbq, gbv, gbo, gg2, gs2, gbd, gbu = grads[4:]
    out_shape = (1, micro, images, cap, features)
    return (
        y.reshape(out_shape), dx.reshape(out_shape), gg1, gs1, gw_qkv, gbq, gbv, gw_out, gbo, gg2, gs2,
        gw_up, gbu, gw_down, gbd,
    )


def solution(mesh):
    token = P(None, "fsdp", "seq", None)
    vector = P("section", "fsdp")
    matrix = P("section", "fsdp", None)
    result = P("section", None, "fsdp", "seq", None)
    return jax.shard_map(
        per_device,
        mesh=mesh,
        in_specs=(
            token, P(None, "fsdp", None), token, vector, vector, matrix, vector, vector, matrix, vector,
            vector, vector, matrix, vector, matrix, vector,
        ),
        out_specs=(
            result, result, vector, vector, matrix, vector, vector, matrix, vector, vector, vector,
            matrix, vector, matrix, vector,
        ),
        check_vma=False,
    )
```

```python
import functools

import jax
import jax.numpy as jnp
from jax import lax
from jax.experimental import pallas as pl
from jax.experimental.pallas import tpu as pltpu
from jax.sharding import PartitionSpec as P

HD = 64
epsilon = 1e-06
masked_score = -1000000000.0
MESH = pl.DeviceIdType.MESH
bf16 = jnp.bfloat16
f32 = jnp.float32
VMEM_LIMIT = 56 * 1024 * 1024


def nn(a, b):
    return jnp.dot(a, b, preferred_element_type=f32)


def nt(a, b):
    return lax.dot_general(a, b, (((1,), (1,)), ((), ())), preferred_element_type=f32)


def tn(a, b):
    return lax.dot_general(a, b, (((0,), (0,)), ((), ())), preferred_element_type=f32)


def norm_parts(values):
    average = jnp.mean(values, axis=-1, keepdims=True)
    centered = values - average
    spread = jnp.mean(centered * centered, axis=-1, keepdims=True)
    inverse = lax.rsqrt(spread + epsilon)
    return centered * inverse, inverse


def norm_back(incoming, gain, xhat, inverse):
    e = incoming * gain
    inner = jnp.mean(e * xhat, axis=-1, keepdims=True)
    return (e - jnp.mean(e, axis=-1, keepdims=True) - xhat * inner) * inverse


def gelu_both(v):
    c = 0.7978845608028654
    square = v * v
    t = jnp.tanh(c * v * (1.0 + 0.044715 * square))
    half = 0.5 * (1.0 + t)
    slope = half + 0.5 * v * (1.0 - t * t) * (c * (1.0 + 0.134145 * square))
    return v * half, slope


def live_slots(counts, cap, cores):
    pos = lax.broadcasted_iota(jnp.int32, (cap, 1), 0)
    return jnp.concatenate([pos < counts[0, 2 * r + 1 - c] for c in cores for r in (0, 1)], axis=0)


def stacked_heads(pair):
    low = lax.broadcasted_iota(jnp.int32, (1, 2 * HD), 1) < HD
    zero = jnp.zeros_like(pair)
    return jnp.concatenate([jnp.where(low, pair, zero), jnp.where(low, zero, pair)], axis=0)


def joined_heads(stacked):
    low = lax.broadcasted_iota(jnp.int32, (1, 2 * HD), 1) < HD
    rows = stacked.shape[0] // 2
    return jnp.where(low, stacked[:rows], stacked[rows:])


def greet(axis_ids):
    barrier = pltpu.get_barrier_semaphore()
    for ids in axis_ids:
        pl.semaphore_signal(barrier, inc=1, device_id=ids, device_id_type=MESH)
    pl.semaphore_wait(barrier, len(axis_ids))


def remote(src, dst, ssem, rsem, ids):
    return pltpu.make_async_remote_copy(
        src_ref=src, dst_ref=dst, send_sem=ssem, recv_sem=rsem, device_id=ids, device_id_type=MESH
    )


def load_weights(refs, sems, order):
    for name in order:
        i, source, ref = refs[name]
        pltpu.make_async_copy(source, ref, sems.at[i]).start()

    def wait(name):
        i, source, ref = refs[name]
        pltpu.make_async_copy(source, ref, sems.at[i]).wait()

    return wait


def weight_refs(wq_h, wo_h, wu_h, wd_h, wq, wo, wu, wd):
    half = wq_h.shape[2]
    return {
        "k": (0, wq_h.at[1], wq.at[:, pl.ds(half, half)]),
        "q": (1, wq_h.at[0], wq.at[:, pl.ds(0, half)]),
        "o": (2, wo_h, wo),
        "u": (3, wu_h, wu),
        "d": (4, wd_h, wd),
    }


def forward_kernel(first, counts, *refs):
    if first:
        (own, vec, wq_h, wo_h, wu_h, wd_h, next_out,
         wq, wo, wu, wd, kv, att, y_out, wsem, ksem, hsem) = refs
    else:
        (own, got, vec, wq_h, wo_h, wu_h, wd_h,
         y_out, x_out, q_out, kv, lse_out, normed_out, mid_out, att, n2_out, act_out, slope_out,
         wq, wo, wu, wd, wsem, ksem) = refs
    rows, features = own.shape
    cap = rows // 2
    sec = lax.axis_index("section")
    _, bits, partner = position()
    c = bits["c"]
    wait_weight = load_weights(
        weight_refs(wq_h, wo_h, wu_h, wd_h, wq, wo, wu, wd), wsem, ("k", "q", "o", "u", "d")
    )
    gain1, shift1, bq, bv, bo, gain2, shift2, bd = (vec[i : i + 1] for i in range(8))
    x_low = own[...] if first else jnp.where(sec == 0, own[...], got[...])
    x = x_low.astype(f32)
    normed = (norm_parts(x)[0] * gain1 + shift1).astype(bf16)
    greet([partner["c"]] + ([{"section": 1 - sec}] if first else []))
    wait_weight("k")
    wait_weight("q")
    kv[0, :, :features] = nn(normed, wq[:, features : 2 * features]).astype(bf16)
    kv[0, :, features:] = (nn(normed, wq[:, 2 * features :]) + bv).astype(bf16)
    swap = remote(kv.at[0], kv.at[1], ksem.at[0], ksem.at[1], partner["c"])
    swap.start()
    q = (nn(normed, wq[:, :features]) + bq).astype(bf16)
    if not first:
        x_out[...] = x_low
        normed_out[...] = normed
        q_out[...] = q
    live = live_slots(counts, cap, (c, 1 - c))
    swap.wait()
    for pair in range(features // (2 * HD)):
        cols = slice(2 * HD * pair, 2 * HD * (pair + 1))
        k = kv[:, :, cols].reshape(2 * rows, 2 * HD)
        v = kv[:, :, features + cols.start : features + cols.stop].reshape(2 * rows, 2 * HD)
        qs = stacked_heads(q[:, cols] * jnp.asarray(HD ** (-0.5), bf16))
        s = jnp.where(live, nt(k, qs), masked_score)
        highest = jnp.max(s, axis=0, keepdims=True)
        raised = jnp.exp(s - highest)
        total = jnp.sum(raised, axis=0, keepdims=True)
        p = (raised * (1.0 / total)).astype(bf16)
        att[:, cols] = joined_heads(nn(v.T, p).T).astype(bf16)
        if not first:
            lse_out[pair : pair + 1, :] = highest + jnp.log(total)
    wait_weight("o")
    wait_weight("u")
    wait_weight("d")
    mid = x + (nn(att[...], wo[...]) + bo)
    n2 = (norm_parts(mid)[0] * gain2 + shift2).astype(bf16)
    if not first:
        mid_out[...] = mid
        n2_out[...] = n2
    size = wu.shape[2]
    mine = live_slots(counts, cap, (c,))
    hops = []
    pieces = 2 if first else 1
    for b in range(pieces):
        at = slice(b * rows // pieces, (b + 1) * rows // pieces)
        total = None
        for j in range(wu.shape[0]):
            part = slice(j * size, (j + 1) * size)
            hidden = nn(n2[at], wu[j]) + vec[8 + j : 9 + j]
            activated, slope = gelu_both(hidden)
            activated = activated.astype(bf16)
            if not first:
                act_out[at, part] = activated
                slope_out[at, part] = slope.astype(bf16)
            term = nn(activated, wd[part])
            total = term if total is None else total + term
        y = mid[at] + (total + bd)
        y_out[at] = jnp.where(mine[at], y, 0.0).astype(bf16)
        if first:
            here = pl.ds(at.start, at.stop - at.start)
            hop = remote(
                y_out.at[here], next_out.at[here], hsem.at[0, b], hsem.at[1, b], {"section": 1 - sec}
            )
            hop.start()
            hops.append(hop)
    for hop in hops:
        hop.wait()


def backward_kernel(first, counts, *refs):
    cot, *refs = refs
    ggot = None
    if not first:
        ggot, *refs = refs
    (x, q, kv, lse, mid, act_slope, vec, wq_h, wo_h, wu_h, wd_h), refs = refs[:11], refs[11:]
    if first:
        y, next_out, home_out, dx_out, ddown_out, dhid, dqkv = *refs[:3], *refs[7:11]
        wq, wo, wu, wd = refs[3:7]
        own_dkv, send, land, wsem, ksem, hsem, tsem = refs[11:]
        refs = None
        y_in = y
    else:
        (dx_out, ddown_out, dhid, dbranch_out, dqkv, sums,
         wq, wo, wu, wd, own_dkv, send, land, wsem, ksem) = refs
    rows, features = cot.shape
    cap = rows // 2
    sec = lax.axis_index("section")
    _, bits, partner = position()
    c = bits["c"]
    wait_weight = load_weights(
        weight_refs(wq_h, wo_h, wu_h, wd_h, wq, wo, wu, wd), wsem, ("d", "u", "o", "q", "k")
    )
    gain1, gain2 = vec[0:1], vec[5:6]
    mine = live_slots(counts, cap, (c,))
    g = cot[...] if first else jnp.where(sec == 0, ggot[...], cot[...])
    ddown = jnp.where(mine, g.astype(f32), 0.0).astype(bf16)
    ddown_out[...] = ddown
    holders, homes = token_peers()
    if first:
        greet([partner["c"], {"section": 1 - sec}] + holders + homes)
        token_copies(y_in, home_out, tsem, homes, start=True)
    else:
        greet([partner["c"]])

    def column_sum(values):
        return jnp.sum(values.astype(f32), axis=0, keepdims=True)

    wait_weight("d")
    wait_weight("u")
    size = wu.shape[2]
    h2 = None
    for j in range(wu.shape[0]):
        part = slice(j * size, (j + 1) * size)
        dh = (nt(ddown, wd[part]) * act_slope[:, part].astype(f32)).astype(bf16)
        dhid[:, part] = dh
        term = nt(dh, wu[j])
        h2 = term if h2 is None else h2 + term
    xhat2, inverse2 = norm_parts(mid[...])
    dmid = ddown.astype(f32) + norm_back(h2, gain2, xhat2, inverse2)
    dbranch = dmid.astype(bf16)
    wait_weight("o")
    datt = nt(dbranch, wo[...]).astype(bf16)
    live = live_slots(counts, cap, (c, 1 - c))
    swaps = []
    for pair in range(features // (2 * HD)):
        cols = slice(2 * HD * pair, 2 * HD * (pair + 1))
        k = kv[:, :, cols].reshape(2 * rows, 2 * HD)
        v = kv[:, :, features + cols.start : features + cols.stop].reshape(2 * rows, 2 * HD)
        qs = stacked_heads(q[:, cols] * jnp.asarray(HD ** (-0.5), bf16))
        das = stacked_heads(datt[:, cols])
        s = jnp.where(live, nt(k, qs), masked_score)
        p = jnp.exp(s - lse[pair : pair + 1, :])
        dp = nt(v, das)
        inner = jnp.sum(p * dp, axis=0, keepdims=True)
        ds = (p * (dp - inner)).astype(bf16)
        dv = nn(p.astype(bf16), das)
        dk = nn(ds, qs)
        dqkv[:, cols] = (joined_heads(nn(k.T, ds).T) * HD ** (-0.5)).astype(bf16)
        send[pair, 0] = dk[rows:].astype(bf16)
        send[pair, 1] = dv[rows:].astype(bf16)
        swap = remote(send.at[pair], land.at[pair], ksem.at[0, pair], ksem.at[1, pair], partner["c"])
        swap.start()
        swaps.append(swap)
        own_dkv[pair, 0] = dk[:rows]
        own_dkv[pair, 1] = dv[:rows]
    xhat1, inverse1 = norm_parts(x[...].astype(f32))
    if not first:
        dbranch_out[...] = dbranch
        sums[5:6] = column_sum(h2 * xhat2)
        sums[6:7] = column_sum(h2)
        sums[7:8] = column_sum(ddown)
        sums[4:5] = column_sum(dbranch)
        for j in range(wu.shape[0]):
            sums[8 + j : 9 + j] = column_sum(dhid[:, j * size : (j + 1) * size])
        sums[12:16] = jnp.zeros((4, features), f32)
    wait_weight("q")
    wait_weight("k")
    for pair, swap in enumerate(swaps):
        cols = slice(features + 2 * HD * pair, features + 2 * HD * (pair + 1))
        swap.wait()
        dqkv[:, cols] = (own_dkv[pair, 0] + land[pair, 0].astype(f32)).astype(bf16)
        dqkv[:, features + cols.start : features + cols.stop] = (
            own_dkv[pair, 1] + land[pair, 1].astype(f32)
        ).astype(bf16)
    hops = []
    pieces = 2 if first else 1
    for b in range(pieces):
        at = slice(b * rows // pieces, (b + 1) * rows // pieces)
        h1 = nt(dqkv[at], wq[...])
        dx = dmid[at] + norm_back(h1, gain1, xhat1[at], inverse1[at])
        dx_out[at] = dx.astype(bf16)
        if first:
            here = pl.ds(at.start, at.stop - at.start)
            hop = remote(
                dx_out.at[here], next_out.at[here], hsem.at[0, b], hsem.at[1, b], {"section": 1 - sec}
            )
            hop.start()
            hops.append(hop)
    if first:
        token_copies(y_in, home_out, tsem, homes, start=False)
    else:
        sums[0:1] = column_sum(h1 * xhat1)
        sums[1:2] = column_sum(h1)
        sums[2:3] = column_sum(dqkv[:, :features])
        sums[3:4] = column_sum(dqkv[:, 2 * features :])
    for hop in hops:
        hop.wait()


LINKS = ("x", "yl", "zl", "yh", "zh")


def position():
    f, z = lax.axis_index("fsdp"), lax.axis_index("seq")
    y = lax.div(f, 4)
    c, x = lax.rem(f, 2), lax.rem(lax.div(f, 2), 2)
    yh, zh = lax.div(y, 2), lax.div(z, 2)
    bits = {"c": c, "x": x, "yh": yh, "zh": zh, "yl": lax.rem(y + yh, 2), "zl": lax.rem(z + zh, 2)}
    low = lax.rem(f, 4)
    partner = {
        "c": {"fsdp": f + 1 - 2 * c},
        "x": {"fsdp": f + 2 - 4 * x},
        "yl": {"fsdp": 4 * (y + 1 - 2 * lax.rem(y, 2)) + low},
        "yh": {"fsdp": 4 * (3 - y) + low},
        "zl": {"seq": z + 1 - 2 * lax.rem(z, 2)},
        "zh": {"seq": 3 - z},
    }
    return f, bits, partner


def token_peers():
    f, z = lax.axis_index("fsdp"), lax.axis_index("seq")
    c = lax.rem(f, 2)
    base = f - c
    holders = [{"seq": 2 * m + c, "fsdp": base + lax.rem(z + 1, 2)} for m in (0, 1)]
    homes = [{"seq": 2 * r + 1 - c, "fsdp": base + lax.rem(z, 2)} for r in (0, 1)]
    return holders, homes


def token_copies(source, target, sems, peers, start):
    z = lax.axis_index("seq")
    place = lax.div(z, 2)
    cap = source.shape[0] // 2
    rows = lambda b: pl.ds(b * cap if isinstance(b, int) else pl.multiple_of(b * cap, 16), cap)
    for b in (0, 1):
        out = remote(
            source.at[rows(b)], target.at[rows(place)], sems.at[0, b], sems.at[1, place], peers[b]
        )
        if start:
            out.start()
        else:
            out.wait_send()
    if not start:
        for b in (0, 1):
            remote(
                source.at[rows(b)], target.at[rows(b)], sems.at[0, b], sems.at[1, b], peers[b]
            ).wait_recv()


def owner_bits(f):
    y = f // 4
    return {"c": f % 2, "x": (f // 2) % 2, "yh": y // 2, "yl": (y + y // 2) % 2}


def link_of(portion, step):
    return LINKS[(portion + step) % 5]


def piece_of(portion, bits):
    return sum(bits[link_of(portion, s)] << (4 - s) for s in range(5))


def row_groups(start, count):
    row, end = start, start + count
    while row < end:
        portion = min(row // 128, 4)
        size = 32 if portion < 4 else 16
        inner = row - 128 * portion
        take = min(end - row, size - inner % size)
        yield portion, inner // size, inner % size, row - start, take
        row += take


def weight_grad_kernel(
    shape,
    act, ddown, n2, dhid, merged, dbranch, normed, dqkv, sums, dx,
    gdown, gup, gout, gqkv, home_out, og1, os1, obq, obv, obo, og2, os2, obd, obu,
    *scratch,
):
    shards, chunks = shape
    held, core_in, step_in, final = (scratch[5 * i : 5 * i + 5] for i in range(4))
    vec, vec_in, csem, ssem, zsem, vsem, tsem = scratch[20:]
    f, bits, partner = position()
    c = bits["c"]
    holders, homes = token_peers()
    greet([partner[n] for n in ("c", "x", "yl", "yh", "zl", "zh")] + holders + homes)
    token_copies(dx, home_out, tsem, homes, start=True)
    features = ddown.shape[1]
    owned = features // shards

    vec[0] = sums[...]

    def vec_copy(s):
        name = ("c", "x", "yl", "yh", "zl", "zh")[s]
        return remote(vec.at[s], vec_in.at[s], vsem.at[0, s], vsem.at[1, s], partner[name])

    def vec_step(s):
        copy = vec_copy(s)
        copy.wait()
        vec[s + 1] = vec[s] + vec_in[s]
        if s < 5:
            vec_copy(s + 1).start()

    def put(owner, start, value):
        value = value.astype(bf16)
        own = owner_bits(owner)
        for portion, quarter, inner, at, take in row_groups(start, value.shape[0]):
            place = piece_of(portion, {**own, "zh": quarter // 2, "zl": quarter % 2})
            held[portion][own["c"], place, inner : inner + take] = value[at : at + take]

    def core_copy(i, half):
        b = bits[link_of(i, 0)]
        at = pl.ds(16 * (1 - b if half == 0 else b), 16)
        return remote(
            held[i].at[1 - c, at], core_in[i].at[at], csem.at[0, i, half], csem.at[1, i, half], partner["c"]
        )

    def ready(i):
        core_copy(i, 0).start()
        core_copy(i, 1).start()

    vec_copy(0).start()
    part = lambda j: slice(j * features, (j + 1) * features)
    for j in range(chunks):
        res = tn(act[:, part(j)], ddown[...])
        for k in range(4):
            put(4 * j + k, 0, res[4 * owned * k : 4 * owned * (k + 1)])
    ready(0)
    for j in range(chunks):
        res = tn(n2[...], dhid[:, part(j)])
        for k in range(shards):
            put(k, 192 + owned * j, res[owned * k : owned * (k + 1)])
        if j == 1:
            ready(1)
    ready(2)
    res = tn(merged[...], dbranch[...])
    for k in range(shards):
        put(k, 384, res[owned * k : owned * (k + 1)])
    for j in range(3):
        res = tn(normed[...], dqkv[:, part(j)])
        for k in range(shards):
            put(k, 432 + owned * j, res[owned * k : owned * (k + 1)])
    ready(3)
    ready(4)

    def add_into(i, base, source, at, count):
        group = min(count, 4)

        def body(k, carry):
            here = pl.ds(base + group * k, group)
            held[i][c, here] = held[i][c, here] + source[pl.ds(at + group * k, group)]
            return carry

        lax.fori_loop(0, count // group, body, 0)

    bases = [0] * 5

    def step_copy(i, s, base):
        name = link_of(i, s)
        half = 16 >> s
        at = 32 - 2 * half
        return remote(
            held[i].at[c, pl.ds(base + (1 - bits[name]) * half, half)],
            step_in[i].at[pl.ds(at, half)],
            ssem.at[0, i, s],
            ssem.at[1, i, s],
            partner[name],
        )

    for i in range(5):
        core_copy(i, 0).wait()
        b = bits[link_of(i, 0)]
        add_into(i, 16 * (1 - b), core_in[i], 16 * (1 - b), 16)
        step_copy(i, 0, 0).start()
    vec_step(0)
    for i in range(5):
        core_copy(i, 1).wait()
        b = bits[link_of(i, 0)]
        add_into(i, 16 * b, core_in[i], 16 * b, 16)
    own_at = []
    for s in range(5):
        for i in range(5):
            half = 16 >> s
            copy = step_copy(i, s, bases[i])
            bases[i] = bases[i] + bits[link_of(i, s)] * half
            copy.wait()
            add_into(i, bases[i], step_in[i], 32 - 2 * half, half)
            if s < 4:
                step_copy(i, s + 1, bases[i]).start()
        vec_step(s + 1)

    def z_copy(i, s):
        first, second = ("zl", "zh") if i % 2 == 0 else ("zh", "zl")
        if s == 0:
            at, to = pl.ds(2 * bits[second] + bits[first], 1), partner[first]
        else:
            at, to = pl.ds(2 * bits[second], 2), partner[second]
        return remote(final[i].at[at], final[i].at[at], zsem.at[0, i, s], zsem.at[1, i, s], to)

    for i in range(5):
        first, second = ("zl", "zh") if i % 2 == 0 else ("zh", "zl")
        final[i][2 * bits[second] + bits[first]] = held[i][c, bases[i]]
        z_copy(i, 0).start()
    for i in range(5):
        z_copy(i, 0).wait()
        z_copy(i, 1).start()
    total = vec[6]
    mine = pltpu.roll(total, lax.rem(features - f * owned, features), 1)
    for r, out in enumerate((og1, os1, obq, obv, obo, og2, os2, obd)):
        out[...] = mine[r : r + 1, :owned]
    wide = 4 * owned
    quarter = pltpu.roll(total, lax.rem(features - lax.rem(f, 4) * wide, features), 1)
    chosen = lax.broadcasted_iota(jnp.int32, (16, 1), 0) == 8 + lax.div(f, 4)
    obu[...] = jnp.sum(jnp.where(chosen, quarter, 0.0), axis=0, keepdims=True)[:, :wide]
    for i in range(5):
        z_copy(i, 1).wait()

    def share(start, count):
        got = []
        for portion, quarter, inner, _, take in row_groups(start, count):
            zh, zl = quarter // 2, quarter % 2
            place = 2 * zh + zl if portion % 2 == 0 else 2 * zl + zh
            got.append(final[portion][place, inner : inner + take])
        return jnp.concatenate(got, axis=0)

    gdown[...] = share(0, 4 * owned)
    for j in range(chunks):
        gup[:, part(j)] = share(192 + owned * j, owned)
    gout[...] = share(384, owned)
    for j in range(3):
        gqkv[:, part(j)] = share(432 + owned * j, owned)
    token_copies(dx, home_out, tsem, homes, start=False)


def gather_kernel(
    wq_in, wo_in, wu_in, wd_in, small_in, x_in, cot_in, count_in,
    wq_out, wo_out, wu_out, wd_out, x_out, cot_out, vec_out, count_out,
    small, count_land, lsem, sems, tsem, nsem,
):
    _, bits, partner = position()
    f, z = lax.axis_index("fsdp"), lax.axis_index("seq")
    y = lax.div(f, 4)
    g = 2 * bits["zh"] + bits["zl"]
    rows, features = wo_in.shape
    half = features // 2
    quarter = lambda: pl.ds(pl.multiple_of(g * features, 128), features)
    fifth = lambda i: [link_of(i, s) for s in range(5)]
    everything, left, right = slice(None), pl.ds(0, half), pl.ds(half, half)
    owners_last = ("zh", "zl", "y", "x", "c")
    items = [
        (wq_out, ("zh", "y", "x", "c"), ["x", "yl", "yh", "zh"], everything),
        (wu_out, owners_last, fifth(1), left),
        (wu_out, owners_last, fifth(2), right),
        (wd_out, ("y", "x", "c", "zh", "zl"), fifth(3), left),
        (wd_out, ("y", "x", "c", "zh", "zl"), fifth(4), right),
        (wo_out, ("y", "x", "c"), ["x", "yl", "yh"], everything),
        (small, ("y", "x", "c"), ["x", "yl", "yh"], everything),
    ]

    def places(item, free, fixed):
        ref, dims, _, columns = items[item]
        at = {n: slice(None) if n in free else fixed[n] for n in ("x", "c", "zh", "zl")}
        if "yl" in free and "yh" in free:
            ys = [slice(None)]
        elif "yl" in free:
            ys = [pl.ds(2 * fixed["yh"], 2)]
        else:
            here = 2 * fixed["yh"] + lax.rem(fixed["yh"] + fixed["yl"], 2)
            ys = [here, 3 - here] if "yh" in free else [here]
        return [
            ref.at[tuple(yy if n == "y" else at[n] for n in dims) + (slice(None), columns)] for yy in ys
        ]

    def copies(item, step, free, fixed, name):
        return [
            remote(p, p, sems.at[0, item, step, k], sems.at[1, item, step, k], partner[name])
            for k, p in enumerate(places(item, free, fixed))
        ]

    def link_copies(item, s):
        order = items[item][2]
        return copies(item, s, order[:s], bits, order[s])

    def core_copies(item, late):
        order = items[item][2]
        fixed = dict(bits)
        if late:
            fixed[order[-1]] = 1 - bits[order[-1]]
        return copies(item, 5 + late, order[:-1], fixed, "c")

    own = [
        (
            wq_in.at[:, pl.ds(pl.multiple_of(bits["zh"] * 3 * half, 128), 3 * half)],
            places(0, (), bits)[0],
        ),
        (wu_in.at[:, quarter()], wu_out.at[bits["zh"], bits["zl"], y, bits["x"], bits["c"]]),
        (wd_in.at[pl.ds(g * rows, rows)], wd_out.at[y, bits["x"], bits["c"], bits["zh"], bits["zl"]]),
        (wo_in, places(5, (), bits)[0]),
        (small_in, places(6, (), bits)[0]),
    ]
    local = [pltpu.make_async_copy(a, b, lsem.at[k]) for k, (a, b) in enumerate(own)]
    for copy in local:
        copy.start()
    holders, homes = token_peers()
    greet([partner[n] for n in ("c", "x", "yl", "yh", "zl", "zh")] + holders + homes)
    counted = remote(count_in, count_land, nsem.at[0], nsem.at[1], partner["c"])
    counted.start()
    for copy in local:
        copy.wait()
    for item in range(len(items)):
        for copy in link_copies(item, 0):
            copy.start()
    token_copies(x_in, x_out, tsem.at[0], holders, start=True)
    token_copies(cot_in, cot_out, tsem.at[1], holders, start=True)
    for s in range(5):
        for item, (_, _, order, _) in enumerate(items):
            if s >= len(order):
                continue
            for copy in link_copies(item, s):
                copy.wait()
            if s + 1 < len(order):
                for copy in link_copies(item, s + 1):
                    copy.start()
            if s + 2 == len(order):
                for copy in core_copies(item, 0):
                    copy.start()
            if s + 1 == len(order):
                for copy in core_copies(item, 1):
                    copy.start()
    for item in range(len(items)):
        for late in (0, 1):
            for copy in core_copies(item, late):
                copy.wait()
    token_copies(x_in, x_out, tsem.at[0], holders, start=False)
    token_copies(cot_in, cot_out, tsem.at[1], holders, start=False)
    counted.wait()
    chosen = jnp.where(lax.rem(z, 2) == bits["c"], count_in[...], count_land[...])
    chosen = jnp.where(lax.div(z, 2) == 0, chosen[0:1], chosen[1:2])
    count_out[...] = jnp.broadcast_to(chosen, count_out.shape)
    table = jnp.concatenate(
        [small[k // 4, (k // 2) % 2, k % 2][0:1].astype(f32) for k in range(16)], axis=0
    )
    lines = [
        jnp.concatenate([table[k : k + 1, j * rows : (j + 1) * rows] for k in range(16)], axis=1)
        for j in range(8)
    ]
    for r in range(4):
        lines.append(
            jnp.concatenate([table[k : k + 1, 8 * rows : 12 * rows] for k in range(4 * r, 4 * r + 4)], axis=1)
        )
    vec_out[...] = jnp.concatenate(lines + [jnp.zeros((4, features), f32)], axis=0)


def per_device(
    images_in, counts, cotangent, gain_one, shift_one, w_qkv, bias_query, bias_value, w_out,
    bias_out, gain_two, shift_two, w_up, bias_up, w_down, bias_down,
):
    micro, images, cap, features = images_in.shape
    shards = lax.axis_size("fsdp")
    rows = micro * images * cap
    owned = features // shards
    ff = w_up.shape[-1]
    chunks = ff // features
    vmem = pl.BlockSpec(memory_space=pltpu.VMEM)
    smem = pl.BlockSpec(memory_space=pltpu.SMEM)
    hbm = pl.BlockSpec(memory_space=pl.ANY)
    dma = pltpu.SemaphoreType.DMA
    sds = jax.ShapeDtypeStruct

    def params(collective_id):
        return pltpu.CompilerParams(
            collective_id=collective_id, has_side_effects=True, vmem_limit_bytes=VMEM_LIMIT
        )

    small = jnp.concatenate(
        [gain_one[0], shift_one[0], bias_query[0], bias_value[0], bias_out[0], gain_two[0],
         shift_two[0], bias_down[0], bias_up[0]]
    )
    small = jnp.broadcast_to(jnp.pad(small, (0, 640 - small.shape[0]))[None], (16, 640))
    table = counts.reshape(micro * images, -1)
    table = jnp.pad(table, ((0, 8 - table.shape[0]), (0, 128 - table.shape[1])))
    tokens = sds((rows, features), bf16)
    wq_h, wo_h, wu_h, wd_h, own, cot, vec, table = pl.pallas_call(
        gather_kernel,
        name="gather_weights",
        out_shape=(
            sds((2, 4, 2, 2, owned, 3 * features // 2), bf16),
            sds((4, 2, 2, owned, features), bf16),
            sds((2, 2, 4, 2, 2, owned, features), bf16),
            sds((4, 2, 2, 2, 2, owned, features), bf16),
            tokens,
            tokens,
            sds((16, features), f32),
            sds((8, 128), jnp.int32),
        ),
        in_specs=[hbm] * 7 + [vmem],
        out_specs=[hbm] * 6 + [vmem] * 2,
        scratch_shapes=[
            pltpu.VMEM((4, 2, 2, 16, 640), bf16),
            pltpu.VMEM((8, 128), jnp.int32),
            dma((5,)),
            dma((2, 7, 7, 2)),
            dma((2, 2, 2)),
            dma((2,)),
        ],
        compiler_params=params(0),
    )(
        w_qkv[0], w_out[0], w_up[0], w_down[0], small, images_in.reshape(rows, features),
        cotangent.reshape(rows, features), table,
    )
    weights = (
        vec,
        wq_h.reshape(2, features, 3 * features // 2),
        wo_h.reshape(features, features),
        wu_h.reshape(chunks, features, features),
        wd_h.reshape(ff, features),
    )
    weight_scratch = [
        pltpu.VMEM((features, 3 * features), bf16),
        pltpu.VMEM((features, features), bf16),
        pltpu.VMEM((chunks, features, features), bf16),
        pltpu.VMEM((ff, features), bf16),
    ]
    pairs = features // (2 * HD)
    kv_shape = (2, rows, 2 * features)
    got = pl.pallas_call(
        functools.partial(forward_kernel, True),
        name="forward_first",
        out_shape=tokens,
        in_specs=[smem] + [vmem] * 2 + [hbm] * 4,
        out_specs=vmem,
        scratch_shapes=weight_scratch
        + [
            pltpu.VMEM(kv_shape, bf16),
            pltpu.VMEM((rows, features), bf16),
            pltpu.VMEM((rows, features), bf16),
            dma((5,)),
            dma((2,)),
            dma((2, 2)),
        ],
        compiler_params=params(1),
    )(table, own, *weights)
    y, x, q, kv, lse, normed, mid, att, n2, act, slope = pl.pallas_call(
        functools.partial(forward_kernel, False),
        name="forward_second",
        out_shape=(
            tokens,
            tokens,
            tokens,
            sds(kv_shape, bf16),
            sds((8, 2 * rows), f32),
            tokens,
            sds((rows, features), f32),
            tokens,
            tokens,
            sds((rows, ff), bf16),
            sds((rows, ff), bf16),
        ),
        in_specs=[smem] + [vmem] * 3 + [hbm] * 4,
        out_specs=[vmem] * 11,
        scratch_shapes=weight_scratch + [dma((5,)), dma((2,))],
        compiler_params=params(2),
    )(table, own, got, *weights)
    exchange = [
        pltpu.VMEM((pairs, 2, rows, 2 * HD), f32),
        pltpu.VMEM((pairs, 2, rows, 2 * HD), bf16),
        pltpu.VMEM((pairs, 2, rows, 2 * HD), bf16),
        dma((5,)),
        dma((2, pairs)),
    ]
    ggot, layer_out = pl.pallas_call(
        functools.partial(backward_kernel, True),
        name="backward_first",
        out_shape=(tokens, tokens),
        in_specs=[smem] + [vmem] * 8 + [hbm] * 4 + [vmem],
        out_specs=[vmem] * 2,
        scratch_shapes=weight_scratch
        + [
            pltpu.VMEM((rows, features), bf16),
            pltpu.VMEM((rows, features), bf16),
            pltpu.VMEM((rows, ff), bf16),
            pltpu.VMEM((rows, 3 * features), bf16),
        ]
        + exchange
        + [dma((2, 2)), dma((2, 2))],
        compiler_params=params(3),
    )(table, cot, x, q, kv, lse, mid, slope, *weights, y)
    dx, ddown, dhid, dbranch, dqkv, sums = pl.pallas_call(
        functools.partial(backward_kernel, False),
        name="backward_second",
        out_shape=(
            tokens,
            tokens,
            sds((rows, ff), bf16),
            tokens,
            sds((rows, 3 * features), bf16),
            sds((16, features), f32),
        ),
        in_specs=[smem] + [vmem] * 9 + [hbm] * 4,
        out_specs=[vmem] * 6,
        scratch_shapes=weight_scratch + exchange,
        compiler_params=params(4),
    )(table, cot, ggot, x, q, kv, lse, mid, slope, *weights)

    sizes = (32, 32, 32, 32, 16)
    vector = sds((1, owned), f32)
    grads = pl.pallas_call(
        functools.partial(weight_grad_kernel, (shards, chunks)),
        name="weight_gradients",
        out_shape=(
            sds((4 * owned, features), bf16),
            sds((owned, ff), bf16),
            sds((owned, features), bf16),
            sds((owned, 3 * features), bf16),
            tokens,
            *([vector] * 8),
            sds((1, 4 * owned), f32),
        ),
        in_specs=[vmem] * 10,
        out_specs=[vmem] * 14,
        scratch_shapes=[pltpu.VMEM((2, 32, r, features), bf16) for r in sizes]
        + [pltpu.VMEM((32, r, features), bf16) for r in sizes]
        + [pltpu.VMEM((32, r, features), bf16) for r in sizes]
        + [pltpu.VMEM((4, r, features), bf16) for r in sizes]
        + [
            pltpu.VMEM((7, 16, features), f32),
            pltpu.VMEM((6, 16, features), f32),
            dma((2, 5, 2)),
            dma((2, 5, 5)),
            dma((2, 5, 2)),
            dma((2, 6)),
            dma((2, 2)),
        ],
        compiler_params=params(5),
    )(act, ddown, n2, dhid, att, dbranch, normed, dqkv, sums, dx)
    gw_down, gw_up, gw_out, gw_qkv = (g.astype(f32)[None] for g in grads[:4])
    input_grad = grads[4]
    gg1, gs1, gbq, gbv, gbo, gg2, gs2, gbd, gbu = grads[5:]
    out_shape = (1, micro, images, cap, features)
    return (
        layer_out.reshape(out_shape), input_grad.reshape(out_shape), gg1, gs1, gw_qkv, gbq, gbv,
        gw_out, gbo, gg2, gs2, gw_up, gbu, gw_down, gbd,
    )


def solution(mesh):
    token = P(None, "fsdp", "seq", None)
    vector = P("section", "fsdp")
    matrix = P("section", "fsdp", None)
    result = P("section", None, "fsdp", "seq", None)
    return jax.shard_map(
        per_device,
        mesh=mesh,
        in_specs=(
            token, P(None, "fsdp", None), token, vector, vector, matrix, vector, vector, matrix, vector,
            vector, vector, matrix, vector, matrix, vector,
        ),
        out_specs=(
            result, result, vector, vector, matrix, vector, vector, matrix, vector, vector, vector,
            matrix, vector, matrix, vector,
        ),
        check_vma=False,
    )
```

```python
import functools

import jax
import jax.numpy as jnp
from jax import lax
from jax.experimental import pallas as pl
from jax.experimental.pallas import tpu as pltpu
from jax.sharding import PartitionSpec as P

HD = 64
epsilon = 1e-06
masked_score = -1000000000.0
MESH = pl.DeviceIdType.MESH
bf16 = jnp.bfloat16
f32 = jnp.float32
VMEM_LIMIT = 56 * 1024 * 1024


def nn(a, b):
    return jnp.dot(a, b, preferred_element_type=f32)


def nt(a, b):
    return lax.dot_general(a, b, (((1,), (1,)), ((), ())), preferred_element_type=f32)


def tn(a, b):
    return lax.dot_general(a, b, (((0,), (0,)), ((), ())), preferred_element_type=f32)


def norm_parts(values):
    average = jnp.mean(values, axis=-1, keepdims=True)
    centered = values - average
    spread = jnp.mean(centered * centered, axis=-1, keepdims=True)
    inverse = lax.rsqrt(spread + epsilon)
    return centered * inverse, inverse


def norm_back(incoming, gain, xhat, inverse):
    e = incoming * gain
    inner = jnp.mean(e * xhat, axis=-1, keepdims=True)
    return (e - jnp.mean(e, axis=-1, keepdims=True) - xhat * inner) * inverse


def gelu_both(v):
    c = 0.7978845608028654
    square = v * v
    t = jnp.tanh(c * v * (1.0 + 0.044715 * square))
    half = 0.5 * (1.0 + t)
    slope = half + 0.5 * v * (1.0 - t * t) * (c * (1.0 + 0.134145 * square))
    return v * half, slope


def live_slots(count_of, cap, cores):
    pos = lax.broadcasted_iota(jnp.int32, (cap, 1), 0).astype(f32)
    return jnp.concatenate([pos < count_of(2 * r + 1 - c) for c in cores for r in (0, 1)], axis=0)


def counts_from(table):
    return lambda i: table[0, i].astype(f32)


def stacked_heads(pair):
    low = lax.broadcasted_iota(jnp.int32, (1, 2 * HD), 1) < HD
    zero = jnp.zeros_like(pair)
    return jnp.concatenate([jnp.where(low, pair, zero), jnp.where(low, zero, pair)], axis=0)


def joined_heads(stacked):
    low = lax.broadcasted_iota(jnp.int32, (1, 2 * HD), 1) < HD
    rows = stacked.shape[0] // 2
    return jnp.where(low, stacked[:rows], stacked[rows:])


def greet(axis_ids):
    barrier = pltpu.get_barrier_semaphore()
    for ids in axis_ids:
        pl.semaphore_signal(barrier, inc=1, device_id=ids, device_id_type=MESH)
    pl.semaphore_wait(barrier, len(axis_ids))


def remote(src, dst, ssem, rsem, ids):
    return pltpu.make_async_remote_copy(
        src_ref=src, dst_ref=dst, send_sem=ssem, recv_sem=rsem, device_id=ids, device_id_type=MESH
    )


def load_weights(refs, sems, order):
    for name in order:
        i, source, ref = refs[name]
        pltpu.make_async_copy(source, ref, sems.at[i]).start()

    def wait(name):
        i, source, ref = refs[name]
        pltpu.make_async_copy(source, ref, sems.at[i]).wait()

    return wait


def weight_refs(qa_h, qb_h, wo_h, wu_h, wd_h, wq, wo, wu, wd):
    a, b, size = qa_h.shape[2], qb_h.shape[2], wo.shape[0]
    return {
        "q0": (0, qa_h.at[0], wq.at[:, pl.ds(0, a)]),
        "q1": (1, qa_h.at[1], wq.at[:, pl.ds(a, a)]),
        "q2": (2, qb_h.at[0], wq.at[:, pl.ds(2 * a, b)]),
        "q3": (3, qb_h.at[1], wq.at[:, pl.ds(2 * a + b, b)]),
        "o": (4, wo_h, wo),
        **{f"u{j}": (5 + j, wu_h.at[j], wu.at[j]) for j in range(4)},
        **{f"d{j}": (9 + j, wd_h.at[pl.ds(j * size, size)], wd.at[pl.ds(j * size, size)]) for j in range(4)},
    }


def attend(kv, q, live, att, lse_out):
    rows, features = q.shape
    for pair in range(features // (2 * HD)):
        cols = slice(2 * HD * pair, 2 * HD * (pair + 1))
        k = kv[:, :, cols].reshape(2 * rows, 2 * HD)
        v = kv[:, :, features + cols.start : features + cols.stop].reshape(2 * rows, 2 * HD)
        qs = stacked_heads(q[:, cols] * jnp.asarray(HD ** (-0.5), bf16))
        s = jnp.where(live, nt(k, qs), masked_score)
        highest = jnp.max(s, axis=0, keepdims=True)
        raised = jnp.exp(s - highest)
        total = jnp.sum(raised, axis=0, keepdims=True)
        p = (raised * (1.0 / total)).astype(bf16)
        att[:, cols] = joined_heads(nn(v.T, p).T).astype(bf16)
        if lse_out is not None:
            lse_out[pair : pair + 1, :] = highest + jnp.log(total)


def feed_forward(n2, mid, vec, up, down, bd, mine, keep=None):
    total = None
    size = n2.shape[1]
    for j in range(4):
        part = slice(j * size, (j + 1) * size)
        hidden = nn(n2, up(j)) + vec[8 + j : 9 + j]
        activated, slope = gelu_both(hidden)
        activated = activated.astype(bf16)
        if keep is not None:
            keep[0][:, part] = activated
            keep[1][:, part] = slope.astype(bf16)
        term = nn(activated, down(j))
        total = term if total is None else total + term
    return jnp.where(mine, mid + (total + bd), 0.0).astype(bf16)


def forward_kernel(
    counts, own, got, vec, qa_h, qb_h, wo_h, wu_h, wd_h,
    y_out, x_out, q_out, kv, lse_out, normed_out, mid_out, att, n2_out, act_out, slope_out,
    wq, wo, wu, wd, wsem, ksem,
):
    rows, features = own.shape
    cap = rows // 2
    sec = lax.axis_index("section")
    _, bits, partner = position()
    c = bits["c"]
    wait_weight = load_weights(
        weight_refs(qa_h, qb_h, wo_h, wu_h, wd_h, wq, wo, wu, wd),
        wsem,
        ("q0", "q1", "q2", "q3", "o", "u0", "d0", "u1", "d1", "u2", "d2", "u3", "d3"),
    )
    gain1, shift1, bq, bv, bo, gain2, shift2, bd = (vec[i : i + 1] for i in range(8))
    x_low = jnp.where(sec == 0, own[...], got[...])
    x = x_low.astype(f32)
    normed = (norm_parts(x)[0] * gain1 + shift1).astype(bf16)
    greet([partner["c"]])
    for n in ("q0", "q1", "q2", "q3"):
        wait_weight(n)
    kv[0, :, :features] = nn(normed, wq[:, features : 2 * features]).astype(bf16)
    kv[0, :, features:] = (nn(normed, wq[:, 2 * features :]) + bv).astype(bf16)
    swap = remote(kv.at[0], kv.at[1], ksem.at[0], ksem.at[1], partner["c"])
    swap.start()
    q = (nn(normed, wq[:, :features]) + bq).astype(bf16)
    x_out[...] = x_low
    normed_out[...] = normed
    q_out[...] = q
    count_of = counts_from(counts)
    live = live_slots(count_of, cap, (c, 1 - c))
    swap.wait()
    attend(kv, q, live, att, lse_out)
    wait_weight("o")
    mid = x + (nn(att[...], wo[...]) + bo)
    n2 = (norm_parts(mid)[0] * gain2 + shift2).astype(bf16)
    mid_out[...] = mid
    n2_out[...] = n2
    for j in range(4):
        wait_weight(f"u{j}")
        wait_weight(f"d{j}")
    y_out[...] = feed_forward(
        n2, mid, vec, lambda j: wu[j], lambda j: wd[j * features : (j + 1) * features], bd,
        live_slots(count_of, cap, (c,)), (act_out, slope_out),
    )


def backward_kernel(first, counts, *refs):
    cot, *refs = refs
    ggot = None
    if not first:
        ggot, *refs = refs
    (x, q, kv, lse, mid, act_slope, vec, qa_h, qb_h, wo_h, wu_h, wd_h), refs = refs[:12], refs[12:]
    if first:
        y, next_out, home_out, dx_out, ddown_out, dhid, dqkv = *refs[:3], *refs[7:11]
        wq, wo, wu, wd = refs[3:7]
        own_dkv, send, land, wsem, ksem, hsem, tsem = refs[11:]
        refs = None
        y_in = y
    else:
        (dx_out, ddown_out, dhid, dbranch_out, dqkv, sums,
         wq, wo, wu, wd, own_dkv, send, land, wsem, ksem) = refs
    rows, features = cot.shape
    cap = rows // 2
    sec = lax.axis_index("section")
    _, bits, partner = position()
    c = bits["c"]
    wait_weight = load_weights(
        weight_refs(qa_h, qb_h, wo_h, wu_h, wd_h, wq, wo, wu, wd),
        wsem,
        ("d0", "u0", "d1", "u1", "d2", "u2", "d3", "u3", "o", "q0", "q1", "q2", "q3"),
    )
    gain1, gain2 = vec[0:1], vec[5:6]
    mine = live_slots(counts_from(counts), cap, (c,))
    g = cot[...] if first else jnp.where(sec == 0, ggot[...], cot[...])
    ddown = jnp.where(mine, g.astype(f32), 0.0).astype(bf16)
    ddown_out[...] = ddown
    holders, homes = token_peers()
    if first:
        greet([partner["c"], {"section": 1 - sec}] + holders + homes)
        token_copies(y_in, home_out, tsem, homes, start=True)
    else:
        greet([partner["c"]])

    def column_sum(values):
        return jnp.sum(values.astype(f32), axis=0, keepdims=True)

    size = wu.shape[2]
    h2 = None
    for j in range(wu.shape[0]):
        wait_weight(f"d{j}")
        wait_weight(f"u{j}")
        part = slice(j * size, (j + 1) * size)
        dh = (nt(ddown, wd[part]) * act_slope[:, part].astype(f32)).astype(bf16)
        dhid[:, part] = dh
        term = nt(dh, wu[j])
        h2 = term if h2 is None else h2 + term
    xhat2, inverse2 = norm_parts(mid[...])
    dmid = ddown.astype(f32) + norm_back(h2, gain2, xhat2, inverse2)
    dbranch = dmid.astype(bf16)
    wait_weight("o")
    datt = nt(dbranch, wo[...]).astype(bf16)
    live = live_slots(counts_from(counts), cap, (c, 1 - c))
    swaps = []
    for pair in range(features // (2 * HD)):
        cols = slice(2 * HD * pair, 2 * HD * (pair + 1))
        k = kv[:, :, cols].reshape(2 * rows, 2 * HD)
        v = kv[:, :, features + cols.start : features + cols.stop].reshape(2 * rows, 2 * HD)
        qs = stacked_heads(q[:, cols] * jnp.asarray(HD ** (-0.5), bf16))
        das = stacked_heads(datt[:, cols])
        s = jnp.where(live, nt(k, qs), masked_score)
        p = jnp.exp(s - lse[pair : pair + 1, :])
        dp = nt(v, das)
        inner = jnp.sum(p * dp, axis=0, keepdims=True)
        ds = (p * (dp - inner)).astype(bf16)
        dv = nn(p.astype(bf16), das)
        dk = nn(ds, qs)
        dqkv[:, cols] = (joined_heads(nn(k.T, ds).T) * HD ** (-0.5)).astype(bf16)
        send[pair, 0] = dk[rows:].astype(bf16)
        send[pair, 1] = dv[rows:].astype(bf16)
        swap = remote(send.at[pair], land.at[pair], ksem.at[0, pair], ksem.at[1, pair], partner["c"])
        swap.start()
        swaps.append(swap)
        own_dkv[pair, 0] = dk[:rows]
        own_dkv[pair, 1] = dv[:rows]
    xhat1, inverse1 = norm_parts(x[...].astype(f32))
    if not first:
        dbranch_out[...] = dbranch
        sums[5:6] = column_sum(h2 * xhat2)
        sums[6:7] = column_sum(h2)
        sums[7:8] = column_sum(ddown)
        sums[4:5] = column_sum(dbranch)
        for j in range(wu.shape[0]):
            sums[8 + j : 9 + j] = column_sum(dhid[:, j * size : (j + 1) * size])
        sums[12:16] = jnp.zeros((4, features), f32)
    for n in ("q0", "q1", "q2", "q3"):
        wait_weight(n)
    for pair, swap in enumerate(swaps):
        cols = slice(features + 2 * HD * pair, features + 2 * HD * (pair + 1))
        swap.wait()
        dqkv[:, cols] = (own_dkv[pair, 0] + land[pair, 0].astype(f32)).astype(bf16)
        dqkv[:, features + cols.start : features + cols.stop] = (
            own_dkv[pair, 1] + land[pair, 1].astype(f32)
        ).astype(bf16)
    hops = []
    pieces = 2 if first else 1
    for b in range(pieces):
        at = slice(b * rows // pieces, (b + 1) * rows // pieces)
        h1 = nt(dqkv[at], wq[...])
        dx = dmid[at] + norm_back(h1, gain1, xhat1[at], inverse1[at])
        dx_out[at] = dx.astype(bf16)
        if first:
            here = pl.ds(at.start, at.stop - at.start)
            hop = remote(
                dx_out.at[here], next_out.at[here], hsem.at[0, b], hsem.at[1, b], {"section": 1 - sec}
            )
            hop.start()
            hops.append(hop)
    if first:
        token_copies(y_in, home_out, tsem, homes, start=False)
    else:
        sums[0:1] = column_sum(h1 * xhat1)
        sums[1:2] = column_sum(h1)
        sums[2:3] = column_sum(dqkv[:, :features])
        sums[3:4] = column_sum(dqkv[:, 2 * features :])
    for hop in hops:
        hop.wait()


LINKS = ("x", "yl", "zl", "yh", "zh")
PIECE = 16
PORTIONS = 9


def position():
    f, z = lax.axis_index("fsdp"), lax.axis_index("seq")
    y = lax.div(f, 4)
    c, x = lax.rem(f, 2), lax.rem(lax.div(f, 2), 2)
    yh, zh = lax.div(y, 2), lax.div(z, 2)
    bits = {"c": c, "x": x, "yh": yh, "zh": zh, "yl": lax.rem(y + yh, 2), "zl": lax.rem(z + zh, 2)}
    low = lax.rem(f, 4)
    partner = {
        "c": {"fsdp": f + 1 - 2 * c},
        "x": {"fsdp": f + 2 - 4 * x},
        "yl": {"fsdp": 4 * (y + 1 - 2 * lax.rem(y, 2)) + low},
        "yh": {"fsdp": 4 * (3 - y) + low},
        "zl": {"seq": z + 1 - 2 * lax.rem(z, 2)},
        "zh": {"seq": 3 - z},
    }
    return f, bits, partner


def token_peers():
    f, z = lax.axis_index("fsdp"), lax.axis_index("seq")
    c = lax.rem(f, 2)
    base = f - c
    holders = [{"seq": 2 * m + c, "fsdp": base + lax.rem(z + 1, 2)} for m in (0, 1)]
    homes = [{"seq": 2 * r + 1 - c, "fsdp": base + lax.rem(z, 2)} for r in (0, 1)]
    return holders, homes


def token_copies(source, target, sems, peers, start):
    z = lax.axis_index("seq")
    place = lax.div(z, 2)
    cap = source.shape[0] // 2
    rows = lambda b: pl.ds(b * cap if isinstance(b, int) else pl.multiple_of(b * cap, 16), cap)
    for b in (0, 1):
        out = remote(
            source.at[rows(b)], target.at[rows(place)], sems.at[0, b], sems.at[1, place], peers[b]
        )
        if start:
            out.start()
        else:
            out.wait_send()
    if not start:
        for b in (0, 1):
            remote(
                source.at[rows(b)], target.at[rows(b)], sems.at[0, b], sems.at[1, b], peers[b]
            ).wait_recv()


def owner_bits(f):
    y = f // 4
    return {"c": f % 2, "x": (f // 2) % 2, "yh": y // 2, "yl": (y + y // 2) % 2}


def link_of(portion, step):
    return LINKS[(portion + step) % 5]


def piece_of(portion, bits):
    return sum(bits[link_of(portion, s)] << (4 - s) for s in range(5))


def row_groups(start, count):
    row, end = start, start + count
    while row < end:
        portion, size = row // (4 * PIECE), PIECE
        inner = row % (4 * PIECE)
        take = min(end - row, size - inner % size)
        yield portion, inner // size, inner % size, row - start, take
        row += take


def weight_grad_kernel(
    shape,
    act, ddown, n2, dhid, merged, dbranch, normed, dqkv, sums, dx,
    gdown, gup, gout, gqkv, home_out, vec_out,
    *scratch,
):
    shards, chunks = shape
    held, core_in, step_in, final, vec, vec_in, csem, ssem, zsem, vsem, tsem = scratch
    f, bits, partner = position()
    c = bits["c"]
    holders, homes = token_peers()
    greet([partner[n] for n in ("c", "x", "yl", "yh", "zl", "zh")] + holders + homes)
    token_copies(dx, home_out, tsem, homes, start=True)
    features = ddown.shape[1]
    owned = features // shards

    vec[0] = sums[...]

    def vec_copy(s):
        name = ("c", "x", "yl", "yh", "zl", "zh")[s]
        return remote(vec.at[s], vec_in.at[s], vsem.at[0, s], vsem.at[1, s], partner[name])

    def vec_step(s):
        copy = vec_copy(s)
        copy.wait()
        vec[s + 1] = vec[s] + vec_in[s]
        if s < 5:
            vec_copy(s + 1).start()

    def put(owner, start, value):
        value = value.astype(bf16)
        own = owner_bits(owner)
        for portion, quarter, inner, at, take in row_groups(start, value.shape[0]):
            place = piece_of(portion, {**own, "zh": quarter // 2, "zl": quarter % 2})
            held[portion, own["c"], place, inner : inner + take] = value[at : at + take]

    def core_copy(i, half):
        b = bits[link_of(i, 0)]
        at = pl.ds(16 * (1 - b if half == 0 else b), 16)
        return remote(
            held.at[i, 1 - c, at], core_in.at[i, at], csem.at[0, i, half], csem.at[1, i, half], partner["c"]
        )

    def ready(i):
        core_copy(i, 0).start()
        core_copy(i, 1).start()

    vec_copy(0).start()
    part = lambda j: slice(j * features, (j + 1) * features)

    def add_into(i, base, source, at, count):
        group = min(count, 8)

        def body(k, carry):
            here = pl.ds(base + group * k, group)
            held[i, c, here] = held[i, c, here] + source[i, pl.ds(at + group * k, group)]
            return carry

        lax.fori_loop(0, count // group, body, 0)

    bases = [0] * PORTIONS

    def step_copy(i, s, base):
        name = link_of(i, s)
        half = 16 >> s
        at = 32 - 2 * half
        return remote(
            held.at[i, c, pl.ds(base + (1 - bits[name]) * half, half)],
            step_in.at[i, pl.ds(at, half)],
            ssem.at[0, i, s],
            ssem.at[1, i, s],
            partner[name],
        )

    def z_copy(i, s):
        first, second = ("zl", "zh") if i % 2 == 0 else ("zh", "zl")
        if s == 0:
            at, to = pl.ds(2 * bits[second] + bits[first], 1), partner[first]
        else:
            at, to = pl.ds(2 * bits[second], 2), partner[second]
        return remote(final.at[i, at], final.at[i, at], zsem.at[0, i, s], zsem.at[1, i, s], to)

    def advance(i):
        b = bits[link_of(i, 0)]
        core_copy(i, 0).wait()
        add_into(i, 16 * (1 - b), core_in, 16 * (1 - b), 16)
        step_copy(i, 0, 0).start()
        core_copy(i, 1).wait()
        add_into(i, 16 * b, core_in, 16 * b, 16)

    for j in range(chunks):
        res = tn(act[:, part(j)], ddown[...])
        for k in range(4):
            put(4 * j + k, 0, res[4 * owned * k : 4 * owned * (k + 1)])
    for i in (0, 1, 2):
        ready(i)
    for j in range(chunks):
        res = tn(n2[...], dhid[:, part(j)])
        for k in range(shards):
            put(k, 192 + owned * j, res[owned * k : owned * (k + 1)])
        if j == 0:
            for i in (0, 1, 2):
                advance(i)
            vec_step(0)
        else:
            ready(2 + j)
            if j > 1:
                advance(1 + j)
    res = tn(merged[...], dbranch[...])
    for k in range(shards):
        put(k, 384, res[owned * k : owned * (k + 1)])
    advance(5)
    for j in range(3):
        res = tn(normed[...], dqkv[:, part(j)])
        for k in range(shards):
            put(k, 432 + owned * j, res[owned * k : owned * (k + 1)])
        ready(6 + j)
        if j > 0:
            advance(5 + j)
    advance(8)
    for s in range(5):
        for i in range(PORTIONS):
            half = 16 >> s
            copy = step_copy(i, s, bases[i])
            bases[i] = bases[i] + bits[link_of(i, s)] * half
            copy.wait()
            add_into(i, bases[i], step_in, 32 - 2 * half, half)
            if s < 4:
                step_copy(i, s + 1, bases[i]).start()
            else:
                first, second = ("zl", "zh") if i % 2 == 0 else ("zh", "zl")
                final[i, 2 * bits[second] + bits[first]] = held[i, c, bases[i]]
                z_copy(i, 0).start()
        vec_step(s + 1)

    for i in range(PORTIONS):
        z_copy(i, 0).wait()
        z_copy(i, 1).start()
    total = vec[6]
    mine = pltpu.roll(total, lax.rem(features - f * owned, features), 1)
    wide = 4 * owned
    quarter = pltpu.roll(total, lax.rem(features - lax.rem(f, 4) * wide, features), 1)
    chosen = lax.broadcasted_iota(jnp.int32, (16, 1), 0) == 8 + lax.div(f, 4)
    vec_out[0:8] = mine[0:8]
    vec_out[8:9] = jnp.sum(jnp.where(chosen, quarter, 0.0), axis=0, keepdims=True)
    vec_out[9:16] = jnp.zeros((7, features), f32)
    for i in range(PORTIONS):
        z_copy(i, 1).wait()

    def share(start, count):
        got = []
        for portion, quarter, inner, _, take in row_groups(start, count):
            zh, zl = quarter // 2, quarter % 2
            place = 2 * zh + zl if portion % 2 == 0 else 2 * zl + zh
            got.append(final[portion, place, inner : inner + take])
        return jnp.concatenate(got, axis=0)

    gdown[...] = share(0, 4 * owned)
    for j in range(chunks):
        gup[:, part(j)] = share(192 + owned * j, owned)
    gout[...] = share(384, owned)
    for j in range(3):
        gqkv[:, part(j)] = share(432 + owned * j, owned)
    token_copies(dx, home_out, tsem, homes, start=False)


def gather_forward_kernel(
    counts, wq_in, wo_in, wu_in, wd_in, x_in, cot_in, *refs
):
    vectors, refs = refs[:9], refs[9:]
    (qa_out, qb_out, wo_out, wu_out, wd_out, x_out, vec, count_out, next_out, cot_out,
     qa, qb, wo, wu, wd, small, count_in, count_land, kv, att, y_out,
     lsem, sems, tsem, nsem, ksem, hsem) = refs
    sec = lax.axis_index("section")
    _, bits, partner = position()
    f, z = lax.axis_index("fsdp"), lax.axis_index("seq")
    y = lax.div(f, 4)
    g = 2 * bits["zh"] + bits["zl"]
    rows, features = wo_in.shape
    half = features // 2
    wide_a, wide_b = qa.shape[-1], qb.shape[-1]
    fifth = lambda i: [link_of(i, s) for s in range(5)]
    everything, left, right = slice(None), pl.ds(0, half), pl.ds(half, half)
    owners_last = ("zh", "zl", "y", "x", "c")
    items = [
        (qa, ("zh", "y", "x", "c"), ["x", "yl", "yh", "zh"], everything),
        (qb, ("zl", "y", "x", "c"), ["yh", "yl", "x", "zl"], everything),
        (small, ("y", "x", "c"), ["x", "yl", "yh"], everything),
        (wu, owners_last, fifth(1), left),
        (wu, owners_last, fifth(2), right),
        (wd, ("y", "x", "c", "zh", "zl"), fifth(3), left),
        (wd, ("y", "x", "c", "zh", "zl"), fifth(4), right),
        (wo, ("y", "x", "c"), ["x", "yl", "yh"], everything),
    ]

    def places(item, free, fixed):
        ref, dims, _, columns = items[item]
        at = {n: slice(None) if n in free else fixed[n] for n in ("x", "c", "zh", "zl")}
        if "yl" in free and "yh" in free:
            ys = [slice(None)]
        elif "yl" in free:
            ys = [pl.ds(2 * fixed["yh"], 2)]
        else:
            here = 2 * fixed["yh"] + lax.rem(fixed["yh"] + fixed["yl"], 2)
            ys = [here, 3 - here] if "yh" in free else [here]
        return [
            ref.at[tuple(yy if n == "y" else at[n] for n in dims) + (slice(None), columns)] for yy in ys
        ]

    def copies(item, step, free, fixed, name):
        return [
            remote(own[item][0] if step == 0 else p, p, sems.at[0, item, step, k], sems.at[1, item, step, k], partner[name])
            for k, p in enumerate(places(item, free, fixed))
        ]

    def link_copies(item, s):
        order = items[item][2]
        return copies(item, s, order[:s], bits, order[s])

    def core_copies(item, late):
        order = items[item][2]
        fixed = dict(bits)
        if late:
            fixed[order[-1]] = 1 - bits[order[-1]]
        return copies(item, 5 + late, order[:-1], fixed, "c")

    own = [
        (wq_in.at[:, pl.ds(pl.multiple_of(bits["zh"] * wide_a, 128), wide_a)], places(0, (), bits)[0]),
        (
            wq_in.at[:, pl.ds(pl.multiple_of(2 * wide_a + bits["zl"] * wide_b, 128), wide_b)],
            places(1, (), bits)[0],
        ),
        (places(2, (), bits)[0], places(2, (), bits)[0]),
        (wu_in.at[:, pl.ds(pl.multiple_of(g * features, 128), half)], places(3, (), bits)[0]),
        (wu_in.at[:, pl.ds(pl.multiple_of(g * features + half, 128), half)], places(4, (), bits)[0]),
        (wd_in.at[pl.ds(g * rows, rows), left], places(5, (), bits)[0]),
        (wd_in.at[pl.ds(g * rows, rows), right], places(6, (), bits)[0]),
        (wo_in, places(7, (), bits)[0]),
    ]
    local = [pltpu.make_async_copy(a, b, lsem.at[k]) for k, (a, b) in enumerate(own) if k != 2]
    for copy in local:
        copy.start()
    line = jnp.concatenate([v[...].astype(f32) for v in vectors], axis=1)
    line = jnp.concatenate([line, jnp.zeros((1, small.shape[-1] - line.shape[1]), f32)], axis=1)
    small[y, bits["x"], bits["c"]] = jnp.broadcast_to(line, small.shape[3:]).astype(bf16)
    row = lax.broadcasted_iota(jnp.int32, count_in.shape, 0)
    lane = lax.broadcasted_iota(jnp.int32, count_in.shape, 1)
    live = jnp.zeros(count_in.shape, jnp.int32)
    for m in (0, 1):
        for r in range(4):
            live = jnp.where((row == m) & (lane == r), counts[m, r], live)
    count_in[...] = live
    holders, homes = token_peers()
    greet([partner[n] for n in ("c", "x", "yl", "yh", "zl", "zh")] + holders + homes + [{"section": 1 - sec}])
    counted = remote(count_in, count_land, nsem.at[0], nsem.at[1], partner["c"])
    for item in range(len(items)):
        for copy in link_copies(item, 0):
            copy.start()
    counted.start()
    for copy in local:
        copy.wait()

    def link_step(item, s):
        order = items[item][2]
        if s >= len(order):
            return
        for copy in link_copies(item, s):
            copy.wait()
        if s + 1 < len(order):
            for copy in link_copies(item, s + 1):
                copy.start()
        if s + 2 == len(order):
            for copy in core_copies(item, 0):
                copy.start()
        if s + 1 == len(order):
            for copy in core_copies(item, 1):
                copy.start()

    def arrived(item):
        for late in (0, 1):
            for copy in core_copies(item, late):
                copy.wait()

    def save(k, source, target):
        copy = pltpu.make_async_copy(source, target, lsem.at[8 + k])
        copy.start()
        return copy

    for s in range(4):
        if s == 1:
            token_copies(x_in, x_out, tsem.at[0], holders, start=True)
        for item in range(len(items)):
            link_step(item, s)
    arrived(2)
    counted.wait()
    chosen = jnp.where(lax.rem(z, 2) == bits["c"], count_in[...], count_land[...])
    chosen = jnp.where(lax.div(z, 2) == 0, chosen[0:1], chosen[1:2])
    count_out[...] = jnp.broadcast_to(chosen, count_out.shape)
    table = jnp.concatenate(
        [small[k // 4, (k // 2) % 2, k % 2][0:1].astype(f32) for k in range(16)], axis=0
    )
    lines = [
        jnp.concatenate([table[k : k + 1, j * rows : (j + 1) * rows] for k in range(16)], axis=1)
        for j in range(8)
    ]
    for r in range(4):
        lines.append(
            jnp.concatenate([table[k : k + 1, 8 * rows : 12 * rows] for k in range(4 * r, 4 * r + 4)], axis=1)
        )
    vec[...] = jnp.concatenate(lines + [jnp.zeros((4, features), f32)], axis=0)
    gain1, shift1, bq, bv, bo, gain2, shift2, bd = (vec[i : i + 1] for i in range(8))
    token_copies(x_in, x_out, tsem.at[0], holders, start=False)
    token_copies(cot_in, cot_out, tsem.at[1], holders, start=True)
    x = x_out[...].astype(f32)
    normed = (norm_parts(x)[0] * gain1 + shift1).astype(bf16)
    arrived(0)
    arrived(1)
    saved = [save(0, qa, qa_out), save(1, qb, qb_out)]
    block = lambda ref, n: nn(normed, ref[n].reshape(features, ref.shape[-1]))
    second, third = block(qa, 1), block(qb, 0)
    q_rest = features - wide_a
    k_end = 2 * features - 2 * wide_a
    kv[0, :, : wide_a - q_rest] = second[:, q_rest:].astype(bf16)
    kv[0, :, wide_a - q_rest : features] = third[:, :k_end].astype(bf16)
    kv[0, :, features : features + wide_b - k_end] = (third[:, k_end:] + bv[:, : wide_b - k_end]).astype(bf16)
    kv[0, :, features + wide_b - k_end :] = (block(qb, 1) + bv[:, wide_b - k_end :]).astype(bf16)
    swap = remote(kv.at[0], kv.at[1], ksem.at[0], ksem.at[1], partner["c"])
    swap.start()
    q = jnp.concatenate([block(qa, 0), second[:, :q_rest]], axis=1) + bq
    q = q.astype(bf16)
    lane = lax.broadcasted_iota(jnp.int32, chosen.shape, 1)
    count_of = lambda i: jnp.sum(jnp.where(lane == i, chosen.astype(f32), 0.0), axis=1, keepdims=True)
    cap = x.shape[0] // 2
    c = bits["c"]
    live = live_slots(count_of, cap, (c, 1 - c))
    swap.wait()
    attend(kv, q, live, att, None)
    for item in range(len(items)):
        link_step(item, 4)
    arrived(7)
    saved.append(save(2, wo, wo_out))
    mid = x + (nn(att[...], wo[...].reshape(features, features)) + bo)
    n2 = (norm_parts(mid)[0] * gain2 + shift2).astype(bf16)
    for item in (3, 4, 5, 6):
        arrived(item)
    saved += [save(3, wu, wu_out), save(4, wd, wd_out)]
    mine = live_slots(count_of, cap, (c,))
    hops = []
    for b in range(2):
        at = slice(b * cap, (b + 1) * cap)
        y_out[at] = feed_forward(
            n2[at], mid[at], vec, lambda j: wu[j // 2, j % 2].reshape(features, features),
            lambda j: wd[j].reshape(features, features), bd, mine[at],
        )
        here = pl.ds(b * cap, cap)
        hop = remote(
            y_out.at[here], next_out.at[here], hsem.at[0, b], hsem.at[1, b], {"section": 1 - sec}
        )
        hop.start()
        hops.append(hop)
    token_copies(cot_in, cot_out, tsem.at[1], holders, start=False)
    for copy in saved + hops:
        copy.wait()


def finish_kernel(gdown, gup, gout, gqkv, layer_in, grad_in, sums, *outs):
    for source, out in zip((gdown, gup, gout, gqkv), outs):
        out[...] = source[...].astype(f32)
    outs[4][...] = layer_in[...]
    outs[5][...] = grad_in[...]
    for r, out in enumerate(outs[6:]):
        out[...] = sums[r : r + 1, : out.shape[1]]


def per_device(
    images_in, counts, cotangent, gain_one, shift_one, w_qkv, bias_query, bias_value, w_out,
    bias_out, gain_two, shift_two, w_up, bias_up, w_down, bias_down,
):
    micro, images, cap, features = images_in.shape
    shards = lax.axis_size("fsdp")
    rows = micro * images * cap
    owned = features // shards
    ff = w_up.shape[-1]
    chunks = ff // features
    vmem = pl.BlockSpec(memory_space=pltpu.VMEM)
    smem = pl.BlockSpec(memory_space=pltpu.SMEM)
    hbm = pl.BlockSpec(memory_space=pl.ANY)
    dma = pltpu.SemaphoreType.DMA
    sds = jax.ShapeDtypeStruct

    def params(collective_id):
        return pltpu.CompilerParams(
            collective_id=collective_id, has_side_effects=True, vmem_limit_bytes=VMEM_LIMIT
        )

    tokens = sds((rows, features), bf16)
    wide_a, wide_b = 640, 512
    cot = cotangent.reshape(rows, features)
    pairs = features // (2 * HD)
    kv_shape = (2, rows, 2 * features)
    shapes = [
        (2, 4, 2, 2, owned, wide_a),
        (2, 4, 2, 2, owned, wide_b),
        (4, 2, 2, owned, features),
        (2, 2, 4, 2, 2, owned, features),
        (4, 2, 2, 2, 2, owned, features),
    ]
    qa_h, qb_h, wo_h, wu_h, wd_h, own, vec, table, got, cot = pl.pallas_call(
        gather_forward_kernel,
        name="gather_and_first_forward",
        out_shape=(
            *(sds(shape, bf16) for shape in shapes),
            tokens,
            sds((16, features), f32),
            sds((8, 128), jnp.int32),
            tokens,
            tokens,
        ),
        in_specs=[smem] + [hbm] * 6 + [vmem] * 9,
        out_specs=[hbm] * 5 + [vmem] * 4 + [hbm],
        scratch_shapes=[pltpu.VMEM(shape, bf16) for shape in shapes]
        + [
            pltpu.VMEM((4, 2, 2, 16, 640), bf16),
            pltpu.VMEM((8, 128), jnp.int32),
            pltpu.VMEM((8, 128), jnp.int32),
            pltpu.VMEM(kv_shape, bf16),
            pltpu.VMEM((rows, features), bf16),
            pltpu.VMEM((rows, features), bf16),
            dma((13,)),
            dma((2, 8, 7, 2)),
            dma((2, 2, 2)),
            dma((2,)),
            dma((2,)),
            dma((2, 2)),
        ],
        compiler_params=params(0),
    )(
        counts.reshape(micro * images, -1), w_qkv[0], w_out[0], w_up[0], w_down[0],
        images_in.reshape(rows, features), cot, gain_one, shift_one, bias_query, bias_value,
        bias_out, gain_two, shift_two, bias_down, bias_up,
    )
    weights = (
        vec,
        qa_h.reshape(2, features, wide_a),
        qb_h.reshape(2, features, wide_b),
        wo_h.reshape(features, features),
        wu_h.reshape(chunks, features, features),
        wd_h.reshape(ff, features),
    )
    weight_scratch = [
        pltpu.VMEM((features, 3 * features), bf16),
        pltpu.VMEM((features, features), bf16),
        pltpu.VMEM((chunks, features, features), bf16),
        pltpu.VMEM((ff, features), bf16),
    ]
    y, x, q, kv, lse, normed, mid, att, n2, act, slope = pl.pallas_call(
        forward_kernel,
        name="forward_second",
        out_shape=(
            tokens,
            tokens,
            tokens,
            sds(kv_shape, bf16),
            sds((8, 2 * rows), f32),
            tokens,
            sds((rows, features), f32),
            tokens,
            tokens,
            sds((rows, ff), bf16),
            sds((rows, ff), bf16),
        ),
        in_specs=[smem] + [vmem] * 3 + [hbm] * 5,
        out_specs=[vmem] * 11,
        scratch_shapes=weight_scratch + [dma((13,)), dma((2,))],
        compiler_params=params(2),
    )(table, own, got, *weights)
    exchange = [
        pltpu.VMEM((pairs, 2, rows, 2 * HD), f32),
        pltpu.VMEM((pairs, 2, rows, 2 * HD), bf16),
        pltpu.VMEM((pairs, 2, rows, 2 * HD), bf16),
        dma((13,)),
        dma((2, pairs)),
    ]
    ggot, layer_out = pl.pallas_call(
        functools.partial(backward_kernel, True),
        name="backward_first",
        out_shape=(tokens, tokens),
        in_specs=[smem] + [vmem] * 8 + [hbm] * 5 + [vmem],
        out_specs=[vmem] * 2,
        scratch_shapes=weight_scratch
        + [
            pltpu.VMEM((rows, features), bf16),
            pltpu.VMEM((rows, features), bf16),
            pltpu.VMEM((rows, ff), bf16),
            pltpu.VMEM((rows, 3 * features), bf16),
        ]
        + exchange
        + [dma((2, 2)), dma((2, 2))],
        compiler_params=params(3),
    )(table, cot, x, q, kv, lse, mid, slope, *weights, y)
    dx, ddown, dhid, dbranch, dqkv, sums = pl.pallas_call(
        functools.partial(backward_kernel, False),
        name="backward_second",
        out_shape=(
            tokens,
            tokens,
            sds((rows, ff), bf16),
            tokens,
            sds((rows, 3 * features), bf16),
            sds((16, features), f32),
        ),
        in_specs=[smem] + [vmem] * 9 + [hbm] * 5,
        out_specs=[vmem] * 6,
        scratch_shapes=weight_scratch + exchange,
        compiler_params=params(4),
    )(table, cot, ggot, x, q, kv, lse, mid, slope, *weights)

    vector = sds((1, owned), f32)
    grads = pl.pallas_call(
        functools.partial(weight_grad_kernel, (shards, chunks)),
        name="weight_gradients",
        out_shape=(
            sds((4 * owned, features), bf16),
            sds((owned, ff), bf16),
            sds((owned, features), bf16),
            sds((owned, 3 * features), bf16),
            tokens,
            sds((16, features), f32),
        ),
        in_specs=[vmem] * 10,
        out_specs=[vmem] * 6,
        scratch_shapes=[
            pltpu.VMEM((PORTIONS, 2, 32, PIECE, features), bf16),
            pltpu.VMEM((PORTIONS, 32, PIECE, features), bf16),
            pltpu.VMEM((PORTIONS, 32, PIECE, features), bf16),
            pltpu.VMEM((PORTIONS, 4, PIECE, features), bf16),
            pltpu.VMEM((7, 16, features), f32),
            pltpu.VMEM((6, 16, features), f32),
            dma((2, PORTIONS, 2)),
            dma((2, PORTIONS, 5)),
            dma((2, PORTIONS, 2)),
            dma((2, 6)),
            dma((2, 2)),
        ],
        compiler_params=params(5),
    )(act, ddown, n2, dhid, att, dbranch, normed, dqkv, sums, dx)
    gw_down, gw_up, gw_out, gw_qkv, layer_out, input_grad, *vectors = pl.pallas_call(
        finish_kernel,
        name="finish",
        out_shape=(
            *(sds(g.shape, f32) for g in grads[:4]),
            tokens,
            tokens,
            *([vector] * 8),
            sds((1, 4 * owned), f32),
        ),
        in_specs=[vmem] * 7,
        out_specs=[vmem] * 15,
    )(*grads[:4], layer_out, *grads[4:])
    gw_down, gw_up, gw_out, gw_qkv = (g[None] for g in (gw_down, gw_up, gw_out, gw_qkv))
    gg1, gs1, gbq, gbv, gbo, gg2, gs2, gbd, gbu = vectors
    out_shape = (1, micro, images, cap, features)
    return (
        layer_out.reshape(out_shape), input_grad.reshape(out_shape), gg1, gs1, gw_qkv, gbq, gbv,
        gw_out, gbo, gg2, gs2, gw_up, gbu, gw_down, gbd,
    )


def solution(mesh):
    token = P(None, "fsdp", "seq", None)
    vector = P("section", "fsdp")
    matrix = P("section", "fsdp", None)
    result = P("section", None, "fsdp", "seq", None)
    return jax.shard_map(
        per_device,
        mesh=mesh,
        in_specs=(
            token, P(None, "fsdp", None), token, vector, vector, matrix, vector, vector, matrix, vector,
            vector, vector, matrix, vector, matrix, vector,
        ),
        out_specs=(
            result, result, vector, vector, matrix, vector, vector, matrix, vector, vector, vector,
            matrix, vector, matrix, vector,
        ),
        check_vma=False,
    )
```

```python
import functools

import jax
import jax.numpy as jnp
from jax import lax
from jax.experimental import pallas as pl
from jax.experimental.pallas import tpu as pltpu
from jax.sharding import PartitionSpec as P

HD = 64
epsilon = 1e-06
masked_score = -1000000000.0
MESH = pl.DeviceIdType.MESH
bf16 = jnp.bfloat16
f32 = jnp.float32
VMEM_LIMIT = 56 * 1024 * 1024


def nn(a, b):
    return jnp.dot(a, b, preferred_element_type=f32)


def nt(a, b):
    return lax.dot_general(a, b, (((1,), (1,)), ((), ())), preferred_element_type=f32)


def tn(a, b):
    return lax.dot_general(a, b, (((0,), (0,)), ((), ())), preferred_element_type=f32)


def norm_parts(values):
    average = jnp.mean(values, axis=-1, keepdims=True)
    centered = values - average
    spread = jnp.mean(centered * centered, axis=-1, keepdims=True)
    inverse = lax.rsqrt(spread + epsilon)
    return centered * inverse, inverse


def norm_back(incoming, gain, xhat, inverse):
    e = incoming * gain
    inner = jnp.mean(e * xhat, axis=-1, keepdims=True)
    return (e - jnp.mean(e, axis=-1, keepdims=True) - xhat * inner) * inverse


def gelu_both(v):
    c = 0.7978845608028654
    square = v * v
    t = jnp.tanh(c * v * (1.0 + 0.044715 * square))
    half = 0.5 * (1.0 + t)
    slope = half + 0.5 * v * (1.0 - t * t) * (c * (1.0 + 0.134145 * square))
    return v * half, slope


def live_slots(count_of, cap, cores):
    pos = lax.broadcasted_iota(jnp.int32, (cap, 1), 0).astype(f32)
    return jnp.concatenate([pos < count_of(2 * r + 1 - c) for c in cores for r in (0, 1)], axis=0)


def counts_from(table):
    return lambda i: table[0, i].astype(f32)


def stacked_heads(pair):
    low = lax.broadcasted_iota(jnp.int32, (1, 2 * HD), 1) < HD
    zero = jnp.zeros_like(pair)
    return jnp.concatenate([jnp.where(low, pair, zero), jnp.where(low, zero, pair)], axis=0)


def joined_heads(stacked):
    low = lax.broadcasted_iota(jnp.int32, (1, 2 * HD), 1) < HD
    rows = stacked.shape[0] // 2
    return jnp.where(low, stacked[:rows], stacked[rows:])


def announce(peers):
    barrier = pltpu.get_barrier_semaphore()
    for ids in peers:
        pl.semaphore_signal(barrier, inc=1, device_id=ids, device_id_type=MESH)
    return lambda: pl.semaphore_wait(barrier, len(peers))


def remote(src, dst, ssem, rsem, ids):
    return pltpu.make_async_remote_copy(
        src_ref=src, dst_ref=dst, send_sem=ssem, recv_sem=rsem, device_id=ids, device_id_type=MESH
    )


def load_weights(refs, sems, order):
    for name in order:
        i, source, ref = refs[name]
        pltpu.make_async_copy(source, ref, sems.at[i]).start()

    def wait(name):
        i, source, ref = refs[name]
        pltpu.make_async_copy(source, ref, sems.at[i]).wait()

    return wait


def weight_refs(qa_h, qb_h, wo_h, wu_h, wd_h, wq, wo, wu, wd):
    a, b, size = qa_h.shape[2], qb_h.shape[2], wo.shape[0]
    return {
        "q0": (0, qa_h.at[0], wq.at[:, pl.ds(0, a)]),
        "q1": (1, qa_h.at[1], wq.at[:, pl.ds(a, a)]),
        "q2": (2, qb_h.at[0], wq.at[:, pl.ds(2 * a, b)]),
        "q3": (3, qb_h.at[1], wq.at[:, pl.ds(2 * a + b, b)]),
        "o": (4, wo_h, wo),
        **{f"u{j}": (5 + j, wu_h.at[j], wu.at[j]) for j in range(4)},
        **{f"d{j}": (9 + j, wd_h.at[pl.ds(j * size, size)], wd.at[pl.ds(j * size, size)]) for j in range(4)},
    }


def attend(kv, q, live, att, probs=None):
    rows, features = q.shape
    for pair in range(features // (2 * HD)):
        cols = slice(2 * HD * pair, 2 * HD * (pair + 1))
        k = kv[:, :, cols].reshape(2 * rows, 2 * HD)
        v = kv[:, :, features + cols.start : features + cols.stop].reshape(2 * rows, 2 * HD)
        qs = stacked_heads(q[:, cols] * jnp.asarray(HD ** (-0.5), bf16))
        s = jnp.where(live, nt(k, qs), masked_score)
        highest = jnp.max(s, axis=0, keepdims=True)
        raised = jnp.exp(s - highest)
        total = jnp.sum(raised, axis=0, keepdims=True)
        p = (raised * (1.0 / total)).astype(bf16)
        att[:, cols] = joined_heads(nn(v.T, p).T).astype(bf16)
        if probs is not None:
            probs[pair] = p


def feed_forward(n2, mid, vec, up, down, bd, mine, keep=None):
    total = None
    size = n2.shape[1]
    for j in range(4):
        part = slice(j * size, (j + 1) * size)
        hidden = nn(n2, up(j)) + vec[8 + j : 9 + j]
        activated, slope = gelu_both(hidden)
        activated = activated.astype(bf16)
        if keep is not None:
            keep[0][:, part] = activated
            keep[1][:, part] = slope.astype(bf16)
        term = nn(activated, down(j))
        total = term if total is None else total + term
    return jnp.where(mine, mid + (total + bd), 0.0).astype(bf16)


def stages_kernel(
    counts, own, got, vec, qa_h, qb_h, wo_h, wu_h, wd_h, cot_h,
    home_out, *refs
):
    mine_h, their_h, (sums, dx_h), refs = refs[:8], refs[8:16], refs[16:18], refs[18:]
    (
    wq, wo, wu, wd, kv, probs, att, act, slope, normed, n2_low, cot, y, ddown, dhid, dbranch, dqkv,
    dx, ggot, own_dkv, send, land, act_t, n2_t, att_t, normed_t, wsem, ksem, dsem, hsem, tsem, osem, xsem,
    ) = refs
    rows, features = own.shape
    cap = rows // 2
    half = rows // 2
    sec = lax.axis_index("section")
    _, bits, partner = position()
    c = bits["c"]
    holders, homes = token_peers()
    everyone_in = announce([partner["c"], {"section": 1 - sec}] + holders + homes)
    wait_weight = load_weights(
        {**weight_refs(qa_h, qb_h, wo_h, wu_h, wd_h, wq, wo, wu, wd), "cot": (13, cot_h, cot)},
        wsem,
        ("q0", "q1", "q2", "q3", "o", "u0", "d0", "u1", "d1", "u2", "d2", "u3", "d3", "cot"),
    )
    gain1, shift1, bq, bv, bo, gain2, shift2, bd = (vec[i : i + 1] for i in range(8))
    x_low = jnp.where(sec == 0, own[...], got[...])
    x = x_low.astype(f32)
    normed[...] = (norm_parts(x)[0] * gain1 + shift1).astype(bf16)
    kept = []

    def keep(k, source, target):
        copy = pltpu.make_async_copy(source, target, osem.at[k])
        copy.start()
        kept.append(copy)

    def share(k, source, halves):
        keep(k, source.at[:, c] if halves else source, mine_h[k])
        copy = remote(
            source.at[:, 1 - c] if halves else source, their_h[k], xsem.at[0, k], xsem.at[1, k], partner["c"]
        )
        copy.start()
        kept.append(copy)

    for n in ("q0", "q1", "q2", "q3"):
        wait_weight(n)
    kv[0, :, :features] = nn(normed[...], wq[:, features : 2 * features]).astype(bf16)
    kv[0, :, features:] = (nn(normed[...], wq[:, 2 * features :]) + bv).astype(bf16)
    everyone_in()
    swap = remote(kv.at[0], kv.at[1], ksem.at[0], ksem.at[1], partner["c"])
    swap.start()
    q = (nn(normed[...], wq[:, :features]) + bq).astype(bf16)
    count_of = counts_from(counts)
    live = live_slots(count_of, cap, (c, 1 - c))
    mine = live_slots(count_of, cap, (c,))
    swap.wait()
    attend(kv, q, live, att, probs)
    wait_weight("o")
    mid = x + (nn(att[...], wo[...]) + bo)
    xhat2, inverse2 = norm_parts(mid)
    n2 = (xhat2 * gain2 + shift2).astype(bf16)
    n2_low[...] = n2
    for j in range(4):
        wait_weight(f"u{j}")
        wait_weight(f"d{j}")
    y[...] = feed_forward(
        n2, mid, vec, lambda j: wu[j], lambda j: wd[j * features : (j + 1) * features], bd, mine,
        (act, slope),
    )
    token_copies(y, home_out, tsem, homes, start=True)

    def column_sum(values):
        return jnp.sum(values.astype(f32), axis=0, keepdims=True)

    wait_weight("cot")
    xhat1, inverse1 = norm_parts(x)
    for last in (False, True):
        g = jnp.where(sec == 0, ggot[...], cot[...]) if last else cot[...]
        down = jnp.where(mine, g.astype(f32), 0.0).astype(bf16)
        h2 = None
        for j in range(4):
            part = slice(j * features, (j + 1) * features)
            dh = (nt(down, wd[part]) * slope[:, part].astype(f32)).astype(bf16)
            if last:
                dhid[:, part] = dh
            term = nt(dh, wu[j])
            h2 = term if h2 is None else h2 + term
        dmid = down.astype(f32) + norm_back(h2, gain2, xhat2, inverse2)
        branch = dmid.astype(bf16)
        datt = nt(branch, wo[...]).astype(bf16)
        if last:
            ddown[...] = down
            dbranch[...] = branch
            share(4, ddown, False)
            share(5, dhid, False)
            share(6, dbranch, False)
        swaps = []
        for pair in range(features // (2 * HD)):
            cols = slice(2 * HD * pair, 2 * HD * (pair + 1))
            k = kv[:, :, cols].reshape(2 * rows, 2 * HD)
            v = kv[:, :, features + cols.start : features + cols.stop].reshape(2 * rows, 2 * HD)
            qs = stacked_heads(q[:, cols] * jnp.asarray(HD ** (-0.5), bf16))
            das = stacked_heads(datt[:, cols])
            p_low = probs[pair]
            p = p_low.astype(f32)
            dp = nt(v, das)
            inner = jnp.sum(p * dp, axis=0, keepdims=True)
            ds = (p * (dp - inner)).astype(bf16)
            dv = nn(p_low, das)
            dk = nn(ds, qs)
            dqkv[:, cols] = (joined_heads(nn(k.T, ds).T) * HD ** (-0.5)).astype(bf16)
            send[pair, 0] = dk[rows:].astype(bf16)
            send[pair, 1] = dv[rows:].astype(bf16)
            swap = remote(
                send.at[pair], land.at[int(last), pair], dsem.at[0, int(last), pair],
                dsem.at[1, int(last), pair], partner["c"],
            )
            swap.start()
            swaps.append(swap)
            own_dkv[pair, 0] = dk[:rows]
            own_dkv[pair, 1] = dv[:rows]
        if last:
            sums[5:6] = column_sum(h2 * xhat2)
            sums[6:7] = column_sum(h2)
            sums[7:8] = column_sum(down)
            sums[4:5] = column_sum(branch)
            for j in range(4):
                sums[8 + j : 9 + j] = column_sum(dhid[:, j * features : (j + 1) * features])
            sums[12:16] = jnp.zeros((4, features), f32)
        for pair, swap in enumerate(swaps):
            cols = slice(features + 2 * HD * pair, features + 2 * HD * (pair + 1))
            swap.wait()
            dqkv[:, cols] = (own_dkv[pair, 0] + land[int(last), pair, 0].astype(f32)).astype(bf16)
            dqkv[:, features + cols.start : features + cols.stop] = (
                own_dkv[pair, 1] + land[int(last), pair, 1].astype(f32)
            ).astype(bf16)
        if last:
            share(7, dqkv, False)
        hops = []
        pieces = 1 if last else 2
        for b in range(pieces):
            at = slice(b * rows // pieces, (b + 1) * rows // pieces)
            h1 = nt(dqkv[at], wq[...])
            grad = dmid[at] + norm_back(h1, gain1, xhat1[at], inverse1[at])
            dx[at] = grad.astype(bf16)
            if not last:
                here = pl.ds(b * half, half)
                hop = remote(
                    dx.at[here], ggot.at[here], hsem.at[0, b], hsem.at[1, b], {"section": 1 - sec}
                )
                hop.start()
                hops.append(hop)
        if not last:
            for j in range(4):
                turned = act[:, j * features : (j + 1) * features].T
                act_t[2 * j : 2 * j + 2] = turned.reshape(2, *act_t.shape[1:])
            n2_t[...] = n2_low[...].T.reshape(n2_t.shape)
            att_t[...] = att[...].T.reshape(n2_t.shape)
            normed_t[...] = normed[...].T.reshape(n2_t.shape)
            share(0, act_t, True)
            share(1, n2_t, True)
            share(2, att_t, True)
            share(3, normed_t, True)
        for hop in hops:
            hop.wait()
    keep(8, dx, dx_h)
    sums[0:1] = column_sum(h1 * xhat1)
    sums[1:2] = column_sum(h1)
    sums[2:3] = column_sum(dqkv[:, :features])
    sums[3:4] = column_sum(dqkv[:, 2 * features :])
    token_copies(y, home_out, tsem, homes, start=False)
    for copy in kept:
        copy.wait()


LINKS = ("x", "yl", "zl", "yh", "zh")
PIECE = 16
PORTIONS = 9


def position():
    f, z = lax.axis_index("fsdp"), lax.axis_index("seq")
    y = lax.div(f, 4)
    c, x = lax.rem(f, 2), lax.rem(lax.div(f, 2), 2)
    yh, zh = lax.div(y, 2), lax.div(z, 2)
    bits = {"c": c, "x": x, "yh": yh, "zh": zh, "yl": lax.rem(y + yh, 2), "zl": lax.rem(z + zh, 2)}
    low = lax.rem(f, 4)
    partner = {
        "c": {"fsdp": f + 1 - 2 * c},
        "x": {"fsdp": f + 2 - 4 * x},
        "yl": {"fsdp": 4 * (y + 1 - 2 * lax.rem(y, 2)) + low},
        "yh": {"fsdp": 4 * (3 - y) + low},
        "zl": {"seq": z + 1 - 2 * lax.rem(z, 2)},
        "zh": {"seq": 3 - z},
    }
    return f, bits, partner


def token_peers():
    f, z = lax.axis_index("fsdp"), lax.axis_index("seq")
    c = lax.rem(f, 2)
    base = f - c
    holders = [{"seq": 2 * m + c, "fsdp": base + lax.rem(z + 1, 2)} for m in (0, 1)]
    homes = [{"seq": 2 * r + 1 - c, "fsdp": base + lax.rem(z, 2)} for r in (0, 1)]
    return holders, homes


def token_copies(source, target, sems, peers, start):
    z = lax.axis_index("seq")
    place = lax.div(z, 2)
    cap = source.shape[0] // 2
    rows = lambda b: pl.ds(b * cap if isinstance(b, int) else pl.multiple_of(b * cap, 16), cap)
    for b in (0, 1):
        out = remote(
            source.at[rows(b)], target.at[rows(place)], sems.at[0, b], sems.at[1, place], peers[b]
        )
        if start:
            out.start()
        else:
            out.wait_send()
    if not start:
        for b in (0, 1):
            remote(
                source.at[rows(b)], target.at[rows(b)], sems.at[0, b], sems.at[1, b], peers[b]
            ).wait_recv()


def owner_bits(f):
    y = f // 4
    return {"c": f % 2, "x": (f // 2) % 2, "yh": y // 2, "yl": (y + y // 2) % 2}


def link_of(portion, step):
    return LINKS[(portion + step) % 5]


def piece_of(portion, bits):
    return sum(bits[link_of(portion, s)] << (4 - s) for s in range(5))


def row_groups(start, count):
    row, end = start, start + count
    while row < end:
        portion, size = row // (4 * PIECE), PIECE
        inner = row % (4 * PIECE)
        take = min(end - row, size - inner % size)
        yield portion, inner // size, inner % size, row - start, take
        row += take


def weight_grad_kernel(shape, *refs):
    shards, chunks = shape
    sources, (sums, dx), refs = refs[:16], refs[16:18], refs[18:]
    gdown, gup, gout, gqkv, home_out, vec_out = refs[:6]
    targets, refs = refs[6:22], refs[22:]
    held, step_in, final, vec, vec_in, ssem, zsem, vsem, tsem, isem = refs
    act, n2, att, normed, ddown, dhid, dbranch, dqkv = zip(targets[:8], targets[8:])
    loads = [pltpu.make_async_copy(a, b, isem.at[k]) for k, (a, b) in enumerate(zip(sources, targets))]
    order = (4, 0, 1, 5, 2, 6, 3, 7)
    for k in order:
        loads[k].start()
        loads[8 + k].start()

    def loaded(*which):
        for k in which:
            loads[k].wait()
            loads[8 + k].wait()

    f, bits, partner = position()
    c = bits["c"]
    holders, homes = token_peers()
    everyone_in = announce([partner[n] for n in ("c", "x", "yl", "yh", "zl", "zh")] + holders + homes)
    features = dx.shape[1]
    owned = features // shards

    vec[0] = sums[...]

    def vec_copy(s):
        name = ("c", "x", "yl", "yh", "zl", "zh")[s]
        return remote(vec.at[s], vec_in.at[s], vsem.at[0, s], vsem.at[1, s], partner[name])

    def vec_step(s):
        copy = vec_copy(s)
        copy.wait()
        vec[s + 1] = vec[s] + vec_in[s]
        if s < 5:
            vec_copy(s + 1).start()

    def put(owner, start, value):
        value = value.astype(bf16)
        own = owner_bits(2 * owner)
        for portion, quarter, inner, at, take in row_groups(start, value.shape[0]):
            place = piece_of(portion, {**own, "zh": quarter // 2, "zl": quarter % 2})
            held[portion, place, inner : inner + take] = value[at : at + take]

    def both_cores(lefts, rights, left_at, right_at):
        total = None
        for left, right in zip(lefts, rights):
            left = left[left_at]
            term = nn(left.reshape(-1, left.shape[-1]), right[:, right_at])
            total = term if total is None else total + term
        return total

    part = lambda j: slice(j * features, (j + 1) * features)

    def add_into(i, base, source, at, count):
        group = min(count, 8)

        def body(k, carry):
            here = pl.ds(base + group * k, group)
            held[i, here] = held[i, here] + source[i, pl.ds(at + group * k, group)]
            return carry

        lax.fori_loop(0, count // group, body, 0)

    bases = [0] * PORTIONS

    def step_copy(i, s, base):
        name = link_of(i, s)
        half = 16 >> s
        at = 32 - 2 * half
        return remote(
            held.at[i, pl.ds(base + (1 - bits[name]) * half, half)],
            step_in.at[i, pl.ds(at, half)],
            ssem.at[0, i, s],
            ssem.at[1, i, s],
            partner[name],
        )

    def z_copy(i, s):
        first, second = ("zl", "zh") if i % 2 == 0 else ("zh", "zl")
        if s == 0:
            at, to = pl.ds(2 * bits[second] + bits[first], 1), partner[first]
        else:
            at, to = pl.ds(2 * bits[second], 2), partner[second]
        return remote(final.at[i, at], final.at[i, at], zsem.at[0, i, s], zsem.at[1, i, s], to)

    whole = slice(None)

    def ready(*portions):
        for i in portions:
            step_copy(i, 0, 0).start()

    loaded(4, 0)
    for m in range(2):
        res = both_cores(act, ddown, slice(4 * m, 4 * m + 4), whole)
        for k in range(4):
            put(4 * m + k, 0, res[4 * owned * k : 4 * owned * (k + 1)])
    everyone_in()
    vec_copy(0).start()
    ready(0, 1, 2)
    loaded(1, 5)
    for j in range(chunks):
        res = both_cores(n2, dhid, whole, part(j))
        for k in range(8):
            put(k, 192 + owned * j, res[owned * k : owned * (k + 1)])
        if j > 0:
            ready(2 + j)
    vec_step(0)
    loaded(2, 6, 3, 7)
    res = both_cores(att, dbranch, whole, whole)
    for k in range(8):
        put(k, 384, res[owned * k : owned * (k + 1)])
    for j in range(3):
        res = both_cores(normed, dqkv, whole, part(j))
        for k in range(8):
            put(k, 432 + owned * j, res[owned * k : owned * (k + 1)])
        ready(6 + j)
    for s in range(5):
        for i in range(PORTIONS):
            half = 16 >> s
            copy = step_copy(i, s, bases[i])
            bases[i] = bases[i] + bits[link_of(i, s)] * half
            copy.wait()
            add_into(i, bases[i], step_in, 32 - 2 * half, half)
            if s < 4:
                step_copy(i, s + 1, bases[i]).start()
            else:
                first, second = ("zl", "zh") if i % 2 == 0 else ("zh", "zl")
                final[i, 2 * bits[second] + bits[first]] = held[i, bases[i]]
                z_copy(i, 0).start()
        vec_step(s + 1)
        if s == 1:
            token_copies(dx, home_out, tsem, homes, start=True)

    for i in range(PORTIONS):
        z_copy(i, 0).wait()
        z_copy(i, 1).start()
    total = vec[6]
    mine = pltpu.roll(total, lax.rem(features - f * owned, features), 1)
    wide = 4 * owned
    quarter = pltpu.roll(total, lax.rem(features - lax.rem(f, 4) * wide, features), 1)
    chosen = lax.broadcasted_iota(jnp.int32, (16, 1), 0) == 8 + lax.div(f, 4)
    vec_out[0:8] = mine[0:8]
    vec_out[8:9] = jnp.sum(jnp.where(chosen, quarter, 0.0), axis=0, keepdims=True)
    vec_out[9:16] = jnp.zeros((7, features), f32)
    for i in range(PORTIONS):
        z_copy(i, 1).wait()

    def share(start, count):
        got = []
        for portion, quarter, inner, _, take in row_groups(start, count):
            zh, zl = quarter // 2, quarter % 2
            place = 2 * zh + zl if portion % 2 == 0 else 2 * zl + zh
            got.append(final[portion, place, inner : inner + take])
        return jnp.concatenate(got, axis=0)

    gdown[...] = share(0, 4 * owned)
    for j in range(chunks):
        gup[:, part(j)] = share(192 + owned * j, owned)
    gout[...] = share(384, owned)
    for j in range(3):
        gqkv[:, part(j)] = share(432 + owned * j, owned)
    token_copies(dx, home_out, tsem, homes, start=False)


def gather_forward_kernel(
    counts, wq_in, wo_in, wu_in, wd_in, x_in, cot_in, *refs
):
    vectors, refs = refs[:9], refs[9:]
    (qa_out, qb_out, wo_out, wu_out, wd_out, x_out, vec, count_out, next_out, cot_out,
     qa, qb, wo, wu, wd, small, count_in, count_land, kv, att, y_out,
     lsem, sems, tsem, nsem, ksem, hsem) = refs
    sec = lax.axis_index("section")
    _, bits, partner = position()
    f, z = lax.axis_index("fsdp"), lax.axis_index("seq")
    y = lax.div(f, 4)
    g = 2 * bits["zh"] + bits["zl"]
    rows, features = wo_in.shape
    half = features // 2
    wide_a, wide_b = qa.shape[-1], qb.shape[-1]
    fifth = lambda i: [link_of(i, s) for s in range(5)]
    everything, left, right = slice(None), pl.ds(0, half), pl.ds(half, half)
    owners_last = ("zh", "zl", "y", "x", "c")
    items = [
        (qa, ("zh", "y", "x", "c"), ["x", "yl", "yh", "zh"], everything),
        (qb, ("zl", "y", "x", "c"), ["yh", "yl", "x", "zl"], everything),
        (small, ("y", "x", "c"), ["x", "yl", "yh"], everything),
        (wu, owners_last, fifth(1), left),
        (wu, owners_last, fifth(2), right),
        (wd, ("y", "x", "c", "zh", "zl"), fifth(3), left),
        (wd, ("y", "x", "c", "zh", "zl"), fifth(4), right),
        (wo, ("y", "x", "c"), ["x", "yl", "yh"], everything),
    ]

    def places(item, free, fixed):
        ref, dims, _, columns = items[item]
        at = {n: slice(None) if n in free else fixed[n] for n in ("x", "c", "zh", "zl")}
        if "yl" in free and "yh" in free:
            ys = [slice(None)]
        elif "yl" in free:
            ys = [pl.ds(2 * fixed["yh"], 2)]
        else:
            here = 2 * fixed["yh"] + lax.rem(fixed["yh"] + fixed["yl"], 2)
            ys = [here, 3 - here] if "yh" in free else [here]
        return [
            ref.at[tuple(yy if n == "y" else at[n] for n in dims) + (slice(None), columns)] for yy in ys
        ]

    def copies(item, step, free, fixed, name):
        return [
            remote(own[item][0] if step == 0 else p, p, sems.at[0, item, step, k], sems.at[1, item, step, k], partner[name])
            for k, p in enumerate(places(item, free, fixed))
        ]

    def link_copies(item, s):
        order = items[item][2]
        return copies(item, s, order[:s], bits, order[s])

    def core_copies(item, late):
        order = items[item][2]
        fixed = dict(bits)
        if late:
            fixed[order[-1]] = 1 - bits[order[-1]]
        return copies(item, 5 + late, order[:-1], fixed, "c")

    own = [
        (wq_in.at[:, pl.ds(pl.multiple_of(bits["zh"] * wide_a, 128), wide_a)], places(0, (), bits)[0]),
        (
            wq_in.at[:, pl.ds(pl.multiple_of(2 * wide_a + bits["zl"] * wide_b, 128), wide_b)],
            places(1, (), bits)[0],
        ),
        (places(2, (), bits)[0], places(2, (), bits)[0]),
        (wu_in.at[:, pl.ds(pl.multiple_of(g * features, 128), half)], places(3, (), bits)[0]),
        (wu_in.at[:, pl.ds(pl.multiple_of(g * features + half, 128), half)], places(4, (), bits)[0]),
        (wd_in.at[pl.ds(g * rows, rows), left], places(5, (), bits)[0]),
        (wd_in.at[pl.ds(g * rows, rows), right], places(6, (), bits)[0]),
        (wo_in, places(7, (), bits)[0]),
    ]
    holders, homes = token_peers()
    everyone_in = announce(
        [partner[n] for n in ("c", "x", "yl", "yh", "zl", "zh")] + holders + homes + [{"section": 1 - sec}]
    )
    local = [pltpu.make_async_copy(a, b, lsem.at[k]) for k, (a, b) in enumerate(own) if k != 2]
    for copy in local:
        copy.start()
    line = jnp.concatenate([v[...].astype(f32) for v in vectors], axis=1)
    line = jnp.concatenate([line, jnp.zeros((1, small.shape[-1] - line.shape[1]), f32)], axis=1)
    small[y, bits["x"], bits["c"]] = jnp.broadcast_to(line, small.shape[3:]).astype(bf16)
    row = lax.broadcasted_iota(jnp.int32, count_in.shape, 0)
    lane = lax.broadcasted_iota(jnp.int32, count_in.shape, 1)
    live = jnp.zeros(count_in.shape, jnp.int32)
    for m in (0, 1):
        for r in range(4):
            live = jnp.where((row == m) & (lane == r), counts[m, r], live)
    count_in[...] = live
    everyone_in()
    counted = remote(count_in, count_land, nsem.at[0], nsem.at[1], partner["c"])
    for item in range(len(items)):
        for copy in link_copies(item, 0):
            copy.start()
    counted.start()
    for copy in local:
        copy.wait()

    def link_step(item, s):
        order = items[item][2]
        if s >= len(order):
            return
        for copy in link_copies(item, s):
            copy.wait()
        if s + 1 < len(order):
            for copy in link_copies(item, s + 1):
                copy.start()
        if s + 2 == len(order):
            for copy in core_copies(item, 0):
                copy.start()
        if s + 1 == len(order):
            for copy in core_copies(item, 1):
                copy.start()

    def arrived(item):
        for late in (0, 1):
            for copy in core_copies(item, late):
                copy.wait()

    def save(k, source, target):
        copy = pltpu.make_async_copy(source, target, lsem.at[8 + k])
        copy.start()
        return copy

    for s in range(4):
        if s == 1:
            token_copies(x_in, x_out, tsem.at[0], holders, start=True)
        for item in range(len(items)):
            link_step(item, s)
    arrived(2)
    counted.wait()
    chosen = jnp.where(lax.rem(z, 2) == bits["c"], count_in[...], count_land[...])
    chosen = jnp.where(lax.div(z, 2) == 0, chosen[0:1], chosen[1:2])
    count_out[...] = jnp.broadcast_to(chosen, count_out.shape)
    table = jnp.concatenate(
        [small[k // 4, (k // 2) % 2, k % 2][0:1].astype(f32) for k in range(16)], axis=0
    )
    lines = [
        jnp.concatenate([table[k : k + 1, j * rows : (j + 1) * rows] for k in range(16)], axis=1)
        for j in range(8)
    ]
    for r in range(4):
        lines.append(
            jnp.concatenate([table[k : k + 1, 8 * rows : 12 * rows] for k in range(4 * r, 4 * r + 4)], axis=1)
        )
    vec[...] = jnp.concatenate(lines + [jnp.zeros((4, features), f32)], axis=0)
    gain1, shift1, bq, bv, bo, gain2, shift2, bd = (vec[i : i + 1] for i in range(8))
    token_copies(x_in, x_out, tsem.at[0], holders, start=False)
    token_copies(cot_in, cot_out, tsem.at[1], holders, start=True)
    x = x_out[...].astype(f32)
    normed = (norm_parts(x)[0] * gain1 + shift1).astype(bf16)
    arrived(0)
    arrived(1)
    saved = [save(0, qa, qa_out), save(1, qb, qb_out)]
    block = lambda ref, n: nn(normed, ref[n].reshape(features, ref.shape[-1]))
    second, third = block(qa, 1), block(qb, 0)
    q_rest = features - wide_a
    k_end = 2 * features - 2 * wide_a
    kv[0, :, : wide_a - q_rest] = second[:, q_rest:].astype(bf16)
    kv[0, :, wide_a - q_rest : features] = third[:, :k_end].astype(bf16)
    kv[0, :, features : features + wide_b - k_end] = (third[:, k_end:] + bv[:, : wide_b - k_end]).astype(bf16)
    kv[0, :, features + wide_b - k_end :] = (block(qb, 1) + bv[:, wide_b - k_end :]).astype(bf16)
    swap = remote(kv.at[0], kv.at[1], ksem.at[0], ksem.at[1], partner["c"])
    swap.start()
    q = jnp.concatenate([block(qa, 0), second[:, :q_rest]], axis=1) + bq
    q = q.astype(bf16)
    lane = lax.broadcasted_iota(jnp.int32, chosen.shape, 1)
    count_of = lambda i: jnp.sum(jnp.where(lane == i, chosen.astype(f32), 0.0), axis=1, keepdims=True)
    cap = x.shape[0] // 2
    c = bits["c"]
    live = live_slots(count_of, cap, (c, 1 - c))
    swap.wait()
    attend(kv, q, live, att)
    for item in range(len(items)):
        link_step(item, 4)
    arrived(7)
    saved.append(save(2, wo, wo_out))
    mid = x + (nn(att[...], wo[...].reshape(features, features)) + bo)
    n2 = (norm_parts(mid)[0] * gain2 + shift2).astype(bf16)
    for item in (3, 4, 5, 6):
        arrived(item)
    saved += [save(3, wu, wu_out), save(4, wd, wd_out)]
    mine = live_slots(count_of, cap, (c,))
    hops = []
    for b in range(2):
        at = slice(b * cap, (b + 1) * cap)
        y_out[at] = feed_forward(
            n2[at], mid[at], vec, lambda j: wu[j // 2, j % 2].reshape(features, features),
            lambda j: wd[j].reshape(features, features), bd, mine[at],
        )
        here = pl.ds(b * cap, cap)
        hop = remote(
            y_out.at[here], next_out.at[here], hsem.at[0, b], hsem.at[1, b], {"section": 1 - sec}
        )
        hop.start()
        hops.append(hop)
    token_copies(cot_in, cot_out, tsem.at[1], holders, start=False)
    for copy in saved + hops:
        copy.wait()


def finish_kernel(gdown, gup, gout, gqkv, layer_in, grad_in, sums, *outs):
    for source, out in zip((gdown, gup, gout, gqkv), outs):
        out[...] = source[...].astype(f32)
    outs[4][...] = layer_in[...]
    outs[5][...] = grad_in[...]
    for r, out in enumerate(outs[6:]):
        out[...] = sums[r : r + 1, : out.shape[1]]


def per_device(
    images_in, counts, cotangent, gain_one, shift_one, w_qkv, bias_query, bias_value, w_out,
    bias_out, gain_two, shift_two, w_up, bias_up, w_down, bias_down,
):
    micro, images, cap, features = images_in.shape
    shards = lax.axis_size("fsdp")
    rows = micro * images * cap
    owned = features // shards
    ff = w_up.shape[-1]
    chunks = ff // features
    vmem = pl.BlockSpec(memory_space=pltpu.VMEM)
    smem = pl.BlockSpec(memory_space=pltpu.SMEM)
    hbm = pl.BlockSpec(memory_space=pl.ANY)
    dma = pltpu.SemaphoreType.DMA
    sds = jax.ShapeDtypeStruct

    def params(collective_id):
        return pltpu.CompilerParams(
            collective_id=collective_id, has_side_effects=True, vmem_limit_bytes=VMEM_LIMIT
        )

    tokens = sds((rows, features), bf16)
    wide_a, wide_b = 640, 512
    cot = cotangent.reshape(rows, features)
    pairs = features // (2 * HD)
    kv_shape = (2, rows, 2 * features)
    shapes = [
        (2, 4, 2, 2, owned, wide_a),
        (2, 4, 2, 2, owned, wide_b),
        (4, 2, 2, owned, features),
        (2, 2, 4, 2, 2, owned, features),
        (4, 2, 2, 2, 2, owned, features),
    ]
    qa_h, qb_h, wo_h, wu_h, wd_h, own, vec, table, got, cot = pl.pallas_call(
        gather_forward_kernel,
        name="gather_and_first_forward",
        out_shape=(
            *(sds(shape, bf16) for shape in shapes),
            tokens,
            sds((16, features), f32),
            sds((8, 128), jnp.int32),
            tokens,
            tokens,
        ),
        in_specs=[smem] + [hbm] * 6 + [vmem] * 9,
        out_specs=[hbm] * 5 + [vmem] * 4 + [hbm],
        scratch_shapes=[pltpu.VMEM(shape, bf16) for shape in shapes]
        + [
            pltpu.VMEM((4, 2, 2, 16, 640), bf16),
            pltpu.VMEM((8, 128), jnp.int32),
            pltpu.VMEM((8, 128), jnp.int32),
            pltpu.VMEM(kv_shape, bf16),
            pltpu.VMEM((rows, features), bf16),
            pltpu.VMEM((rows, features), bf16),
            dma((13,)),
            dma((2, 8, 7, 2)),
            dma((2, 2, 2)),
            dma((2,)),
            dma((2,)),
            dma((2, 2)),
        ],
        compiler_params=params(0),
    )(
        counts.reshape(micro * images, -1), w_qkv[0], w_out[0], w_up[0], w_down[0],
        images_in.reshape(rows, features), cot, gain_one, shift_one, bias_query, bias_value,
        bias_out, gain_two, shift_two, bias_down, bias_up,
    )
    weights = (
        vec,
        qa_h.reshape(2, features, wide_a),
        qb_h.reshape(2, features, wide_b),
        wo_h.reshape(features, features),
        wu_h.reshape(chunks, features, features),
        wd_h.reshape(ff, features),
    )
    wide = sds((rows, ff), bf16)
    triple = sds((rows, 3 * features), bf16)
    turned = sds((8, owned, rows), bf16)
    operands = (sds((8, 4 * owned, rows), bf16), turned, turned, turned, tokens, wide, tokens, triple)
    exchange = (pairs, 2, rows, 2 * HD)
    flat = pltpu.VMEM((rows, features), bf16)
    layer_out, *operands_h, sums, dx = pl.pallas_call(
        stages_kernel,
        name="second_forward_and_backward",
        out_shape=(
            tokens, *operands, *operands, sds((16, features), f32), tokens,
        ),
        in_specs=[smem] + [vmem] * 3 + [hbm] * 6,
        out_specs=[vmem] + [hbm] * 16 + [vmem, hbm],
        scratch_shapes=[
            pltpu.VMEM((features, 3 * features), bf16),
            pltpu.VMEM((features, features), bf16),
            pltpu.VMEM((chunks, features, features), bf16),
            pltpu.VMEM((ff, features), bf16),
            pltpu.VMEM(kv_shape, bf16),
            pltpu.VMEM((pairs, 2 * rows, 2 * rows), bf16),
            flat,
            pltpu.VMEM((rows, ff), bf16),
            pltpu.VMEM((rows, ff), bf16),
            flat, flat, flat, flat, flat,
            pltpu.VMEM((rows, ff), bf16),
            flat,
            pltpu.VMEM((rows, 3 * features), bf16),
            flat, flat,
            pltpu.VMEM(exchange, f32),
            pltpu.VMEM(exchange, bf16),
            pltpu.VMEM((2, *exchange), bf16),
            pltpu.VMEM((8, 2, 4 * owned, rows), bf16),
            pltpu.VMEM((8, 2, owned, rows), bf16),
            pltpu.VMEM((8, 2, owned, rows), bf16),
            pltpu.VMEM((8, 2, owned, rows), bf16),
            dma((14,)),
            dma((2,)),
            dma((2, 2, pairs)),
            dma((2, 2)),
            dma((2, 2)),
            dma((9,)),
            dma((2, 8)),
        ],
        compiler_params=params(1),
    )(table, own, got, *weights, cot)

    vector = sds((1, owned), f32)
    grads = pl.pallas_call(
        functools.partial(weight_grad_kernel, (shards, chunks)),
        name="weight_gradients",
        out_shape=(
            sds((4 * owned, features), bf16),
            sds((owned, ff), bf16),
            sds((owned, features), bf16),
            sds((owned, 3 * features), bf16),
            tokens,
            sds((16, features), f32),
        ),
        in_specs=[hbm] * 16 + [vmem] * 2,
        out_specs=[vmem] * 6,
        scratch_shapes=[
            *(pltpu.VMEM(o.shape, bf16) for o in operands * 2),
            pltpu.VMEM((PORTIONS, 32, PIECE, features), bf16),
            pltpu.VMEM((PORTIONS, 32, PIECE, features), bf16),
            pltpu.VMEM((PORTIONS, 4, PIECE, features), bf16),
            pltpu.VMEM((7, 16, features), f32),
            pltpu.VMEM((6, 16, features), f32),
            dma((2, PORTIONS, 5)),
            dma((2, PORTIONS, 2)),
            dma((2, 6)),
            dma((2, 2)),
            dma((16,)),
        ],
        compiler_params=params(2),
    )(*operands_h, sums, dx)
    gw_down, gw_up, gw_out, gw_qkv, layer_out, input_grad, *vectors = pl.pallas_call(
        finish_kernel,
        name="finish",
        out_shape=(
            *(sds(g.shape, f32) for g in grads[:4]),
            tokens,
            tokens,
            *([vector] * 8),
            sds((1, 4 * owned), f32),
        ),
        in_specs=[vmem] * 7,
        out_specs=[vmem] * 15,
    )(*grads[:4], layer_out, *grads[4:])
    gw_down, gw_up, gw_out, gw_qkv = (g[None] for g in (gw_down, gw_up, gw_out, gw_qkv))
    gg1, gs1, gbq, gbv, gbo, gg2, gs2, gbd, gbu = vectors
    out_shape = (1, micro, images, cap, features)
    return (
        layer_out.reshape(out_shape), input_grad.reshape(out_shape), gg1, gs1, gw_qkv, gbq, gbv,
        gw_out, gbo, gg2, gs2, gw_up, gbu, gw_down, gbd,
    )


def solution(mesh):
    token = P(None, "fsdp", "seq", None)
    vector = P("section", "fsdp")
    matrix = P("section", "fsdp", None)
    result = P("section", None, "fsdp", "seq", None)
    return jax.shard_map(
        per_device,
        mesh=mesh,
        in_specs=(
            token, P(None, "fsdp", None), token, vector, vector, matrix, vector, vector, matrix, vector,
            vector, vector, matrix, vector, matrix, vector,
        ),
        out_specs=(
            result, result, vector, vector, matrix, vector, vector, matrix, vector, vector, vector,
            matrix, vector, matrix, vector,
        ),
        check_vma=False,
    )
```

```python
import functools

import jax
import jax.numpy as jnp
from jax import lax
from jax.experimental import pallas as pl
from jax.experimental.pallas import tpu as pltpu
from jax.sharding import PartitionSpec as P

HD = 64
epsilon = 1e-06
masked_score = -1000000000.0
MESH = pl.DeviceIdType.MESH
bf16 = jnp.bfloat16
f32 = jnp.float32
VMEM_LIMIT = 56 * 1024 * 1024


def nn(a, b):
    return jnp.dot(a, b, preferred_element_type=f32)


def nt(a, b):
    return lax.dot_general(a, b, (((1,), (1,)), ((), ())), preferred_element_type=f32)


def tn(a, b):
    return lax.dot_general(a, b, (((0,), (0,)), ((), ())), preferred_element_type=f32)


def norm_parts(values):
    average = jnp.mean(values, axis=-1, keepdims=True)
    centered = values - average
    spread = jnp.mean(centered * centered, axis=-1, keepdims=True)
    inverse = lax.rsqrt(spread + epsilon)
    return centered * inverse, inverse


def norm_back(incoming, gain, xhat, inverse):
    e = incoming * gain
    inner = jnp.mean(e * xhat, axis=-1, keepdims=True)
    return (e - jnp.mean(e, axis=-1, keepdims=True) - xhat * inner) * inverse


def gelu_both(v):
    c = 0.7978845608028654
    square = v * v
    t = jnp.tanh(c * v * (1.0 + 0.044715 * square))
    half = 0.5 * (1.0 + t)
    slope = half + 0.5 * v * (1.0 - t * t) * (c * (1.0 + 0.134145 * square))
    return v * half, slope


def live_slots(count_of, cap, cores):
    pos = lax.broadcasted_iota(jnp.int32, (cap, 1), 0).astype(f32)
    return jnp.concatenate([pos < count_of(2 * r + 1 - c) for c in cores for r in (0, 1)], axis=0)


def counts_from(table):
    return lambda i: table[0, i].astype(f32)


def stacked_heads(pair):
    low = lax.broadcasted_iota(jnp.int32, (1, 2 * HD), 1) < HD
    zero = jnp.zeros_like(pair)
    return jnp.concatenate([jnp.where(low, pair, zero), jnp.where(low, zero, pair)], axis=0)


def joined_heads(stacked):
    low = lax.broadcasted_iota(jnp.int32, (1, 2 * HD), 1) < HD
    rows = stacked.shape[0] // 2
    return jnp.where(low, stacked[:rows], stacked[rows:])


def announce(peers):
    barrier = pltpu.get_barrier_semaphore()
    for ids in peers:
        pl.semaphore_signal(barrier, inc=1, device_id=ids, device_id_type=MESH)
    return lambda: pl.semaphore_wait(barrier, len(peers))


def remote(src, dst, ssem, rsem, ids):
    return pltpu.make_async_remote_copy(
        src_ref=src, dst_ref=dst, send_sem=ssem, recv_sem=rsem, device_id=ids, device_id_type=MESH
    )


def load_weights(refs, sems, order):
    for name in order:
        i, source, ref = refs[name]
        pltpu.make_async_copy(source, ref, sems.at[i]).start()

    def wait(name):
        i, source, ref = refs[name]
        pltpu.make_async_copy(source, ref, sems.at[i]).wait()

    return wait


def weight_refs(qa_h, qb_h, wo_h, wu_h, wd_h, wq, wo, wu, wd):
    a, b, size = qa_h.shape[2], qb_h.shape[2], wo.shape[0]
    return {
        "q0": (0, qa_h.at[0], wq.at[:, pl.ds(0, a)]),
        "q1": (1, qa_h.at[1], wq.at[:, pl.ds(a, a)]),
        "q2": (2, qb_h.at[0], wq.at[:, pl.ds(2 * a, b)]),
        "q3": (3, qb_h.at[1], wq.at[:, pl.ds(2 * a + b, b)]),
        "o": (4, wo_h, wo),
        **{f"u{j}": (5 + j, wu_h.at[j], wu.at[j]) for j in range(4)},
        **{f"d{j}": (9 + j, wd_h.at[pl.ds(j * size, size)], wd.at[pl.ds(j * size, size)]) for j in range(4)},
    }


def attend(kv, q, live, att, pairs, probs=None):
    rows, features = q.shape
    for pair in pairs:
        cols = slice(2 * HD * pair, 2 * HD * (pair + 1))
        k = kv[:, :, cols].reshape(2 * rows, 2 * HD)
        v = kv[:, :, features + cols.start : features + cols.stop].reshape(2 * rows, 2 * HD)
        qs = stacked_heads(q[:, cols] * jnp.asarray(HD ** (-0.5), bf16))
        s = jnp.where(live, nt(k, qs), masked_score)
        highest = jnp.max(s, axis=0, keepdims=True)
        raised = jnp.exp(s - highest)
        total = jnp.sum(raised, axis=0, keepdims=True)
        p = (raised * (1.0 / total)).astype(bf16)
        att[:, cols] = joined_heads(nn(v.T, p).T).astype(bf16)
        if probs is not None:
            probs[pair] = p


def feed_forward(n2, mid, vec, up, down, bd, mine, keep=None):
    total = None
    size = n2.shape[1]
    for j in range(4):
        part = slice(j * size, (j + 1) * size)
        hidden = nn(n2, up(j)) + vec[8 + j : 9 + j]
        activated, slope = gelu_both(hidden)
        activated = activated.astype(bf16)
        if keep is not None:
            keep[0][:, part] = activated
            keep[1][:, part] = slope.astype(bf16)
        term = nn(activated, down(j))
        total = term if total is None else total + term
    return jnp.where(mine, mid + (total + bd), 0.0).astype(bf16)


def stages_kernel(
    counts, own, got, vec, qa_h, qb_h, wo_h, wu_h, wd_h, cot_h,
    home_out, *refs
):
    mine_h, their_h, (sums, dx_h), refs = refs[:8], refs[8:16], refs[16:18], refs[18:]
    (
    wq, wo, wu, wd, kv, probs, att, act, slope, normed, n2_low, cot, y, ddown, dhid, dbranch, dqkv,
    dx, ggot, own_dkv, send, land, act_t, n2_t, att_t, normed_t, wsem, ksem, dsem, hsem, tsem, osem, xsem,
    ) = refs
    rows, features = own.shape
    cap = rows // 2
    half = rows // 2
    sec = lax.axis_index("section")
    _, bits, partner = position()
    c = bits["c"]
    holders, homes = token_peers()
    everyone_in = announce([partner["c"], {"section": 1 - sec}] + holders + homes)
    wait_weight = load_weights(
        {**weight_refs(qa_h, qb_h, wo_h, wu_h, wd_h, wq, wo, wu, wd), "cot": (13, cot_h, cot)},
        wsem,
        ("q0", "q1", "q2", "q3", "o", "u0", "d0", "u1", "d1", "u2", "d2", "u3", "d3", "cot"),
    )
    gain1, shift1, bq, bv, bo, gain2, shift2, bd = (vec[i : i + 1] for i in range(8))
    x_low = jnp.where(sec == 0, own[...], got[...])
    x = x_low.astype(f32)
    normed[...] = (norm_parts(x)[0] * gain1 + shift1).astype(bf16)
    kept = []

    def keep(k, source, target):
        copy = pltpu.make_async_copy(source, target, osem.at[k])
        copy.start()
        kept.append(copy)

    def share(k, source, halves):
        keep(k, source.at[:, c] if halves else source, mine_h[k])
        copy = remote(
            source.at[:, 1 - c] if halves else source, their_h[k], xsem.at[0, k], xsem.at[1, k], partner["c"]
        )
        copy.start()
        kept.append(copy)

    for n in ("q0", "q1", "q2", "q3"):
        wait_weight(n)
    kv[0, :, :features] = nn(normed[...], wq[:, features : 2 * features]).astype(bf16)
    kv[0, :, features:] = (nn(normed[...], wq[:, 2 * features :]) + bv).astype(bf16)
    everyone_in()
    swap = remote(kv.at[0], kv.at[1], ksem.at[0], ksem.at[1], partner["c"])
    swap.start()
    q = (nn(normed[...], wq[:, :features]) + bq).astype(bf16)
    count_of = counts_from(counts)
    live = live_slots(count_of, cap, (c, 1 - c))
    mine = live_slots(count_of, cap, (c,))
    swap.wait()
    attend(kv, q, live, att, range(features // (2 * HD)), probs)
    wait_weight("o")
    mid = x + (nn(att[...], wo[...]) + bo)
    xhat2, inverse2 = norm_parts(mid)
    n2 = (xhat2 * gain2 + shift2).astype(bf16)
    n2_low[...] = n2
    for j in range(4):
        wait_weight(f"u{j}")
        wait_weight(f"d{j}")
    y[...] = feed_forward(
        n2, mid, vec, lambda j: wu[j], lambda j: wd[j * features : (j + 1) * features], bd, mine,
        (act, slope),
    )
    token_copies(y, home_out, tsem, homes, start=True)

    def column_sum(values):
        return jnp.sum(values.astype(f32), axis=0, keepdims=True)

    wait_weight("cot")
    xhat1, inverse1 = norm_parts(x)
    for last in (False, True):
        g = jnp.where(sec == 0, ggot[...], cot[...]) if last else cot[...]
        down = jnp.where(mine, g.astype(f32), 0.0).astype(bf16)
        h2 = None
        for j in range(4):
            part = slice(j * features, (j + 1) * features)
            dh = (nt(down, wd[part]) * slope[:, part].astype(f32)).astype(bf16)
            if last:
                dhid[:, part] = dh
            term = nt(dh, wu[j])
            h2 = term if h2 is None else h2 + term
        dmid = down.astype(f32) + norm_back(h2, gain2, xhat2, inverse2)
        branch = dmid.astype(bf16)
        datt = nt(branch, wo[...]).astype(bf16)
        if last:
            ddown[...] = down
            dbranch[...] = branch
            share(4, ddown, False)
            share(5, dhid, False)
            share(6, dbranch, False)
        swaps = []
        for pair in range(features // (2 * HD)):
            cols = slice(2 * HD * pair, 2 * HD * (pair + 1))
            k = kv[:, :, cols].reshape(2 * rows, 2 * HD)
            v = kv[:, :, features + cols.start : features + cols.stop].reshape(2 * rows, 2 * HD)
            qs = stacked_heads(q[:, cols] * jnp.asarray(HD ** (-0.5), bf16))
            das = stacked_heads(datt[:, cols])
            p_low = probs[pair]
            p = p_low.astype(f32)
            dp = nt(v, das)
            inner = jnp.sum(p * dp, axis=0, keepdims=True)
            ds = (p * (dp - inner)).astype(bf16)
            dv = nn(p_low, das)
            dk = nn(ds, qs)
            dqkv[:, cols] = (joined_heads(nn(k.T, ds).T) * HD ** (-0.5)).astype(bf16)
            send[pair, 0] = dk[rows:].astype(bf16)
            send[pair, 1] = dv[rows:].astype(bf16)
            swap = remote(
                send.at[pair], land.at[int(last), pair], dsem.at[0, int(last), pair],
                dsem.at[1, int(last), pair], partner["c"],
            )
            swap.start()
            swaps.append(swap)
            own_dkv[pair, 0] = dk[:rows]
            own_dkv[pair, 1] = dv[:rows]
        if last:
            sums[5:6] = column_sum(h2 * xhat2)
            sums[6:7] = column_sum(h2)
            sums[7:8] = column_sum(down)
            sums[4:5] = column_sum(branch)
            for j in range(4):
                sums[8 + j : 9 + j] = column_sum(dhid[:, j * features : (j + 1) * features])
            sums[12:16] = jnp.zeros((4, features), f32)
        for pair, swap in enumerate(swaps):
            cols = slice(features + 2 * HD * pair, features + 2 * HD * (pair + 1))
            swap.wait()
            dqkv[:, cols] = (own_dkv[pair, 0] + land[int(last), pair, 0].astype(f32)).astype(bf16)
            dqkv[:, features + cols.start : features + cols.stop] = (
                own_dkv[pair, 1] + land[int(last), pair, 1].astype(f32)
            ).astype(bf16)
        if last:
            share(7, dqkv, False)
        hops = []
        pieces = 1 if last else 2
        for b in range(pieces):
            at = slice(b * rows // pieces, (b + 1) * rows // pieces)
            h1 = nt(dqkv[at], wq[...])
            grad = dmid[at] + norm_back(h1, gain1, xhat1[at], inverse1[at])
            dx[at] = grad.astype(bf16)
            if not last:
                here = pl.ds(b * half, half)
                hop = remote(
                    dx.at[here], ggot.at[here], hsem.at[0, b], hsem.at[1, b], {"section": 1 - sec}
                )
                hop.start()
                hops.append(hop)
        if not last:
            for j in range(4):
                turned = act[:, j * features : (j + 1) * features].T
                act_t[2 * j : 2 * j + 2] = turned.reshape(2, *act_t.shape[1:])
            n2_t[...] = n2_low[...].T.reshape(n2_t.shape)
            att_t[...] = att[...].T.reshape(n2_t.shape)
            normed_t[...] = normed[...].T.reshape(n2_t.shape)
            share(0, act_t, True)
            share(1, n2_t, True)
            share(2, att_t, True)
            share(3, normed_t, True)
        for hop in hops:
            hop.wait()
    keep(8, dx, dx_h)
    sums[0:1] = column_sum(h1 * xhat1)
    sums[1:2] = column_sum(h1)
    sums[2:3] = column_sum(dqkv[:, :features])
    sums[3:4] = column_sum(dqkv[:, 2 * features :])
    token_copies(y, home_out, tsem, homes, start=False)
    for copy in kept:
        copy.wait()


LINKS = ("x", "yl", "zl", "yh", "zh")
PIECE = 16
PORTIONS = 9


def position():
    f, z = lax.axis_index("fsdp"), lax.axis_index("seq")
    y = lax.div(f, 4)
    c, x = lax.rem(f, 2), lax.rem(lax.div(f, 2), 2)
    yh, zh = lax.div(y, 2), lax.div(z, 2)
    bits = {"c": c, "x": x, "yh": yh, "zh": zh, "yl": lax.rem(y + yh, 2), "zl": lax.rem(z + zh, 2)}
    low = lax.rem(f, 4)
    partner = {
        "c": {"fsdp": f + 1 - 2 * c},
        "x": {"fsdp": f + 2 - 4 * x},
        "yl": {"fsdp": 4 * (y + 1 - 2 * lax.rem(y, 2)) + low},
        "yh": {"fsdp": 4 * (3 - y) + low},
        "zl": {"seq": z + 1 - 2 * lax.rem(z, 2)},
        "zh": {"seq": 3 - z},
    }
    return f, bits, partner


def token_peers():
    f, z = lax.axis_index("fsdp"), lax.axis_index("seq")
    c = lax.rem(f, 2)
    base = f - c
    holders = [{"seq": 2 * m + c, "fsdp": base + lax.rem(z + 1, 2)} for m in (0, 1)]
    homes = [{"seq": 2 * r + 1 - c, "fsdp": base + lax.rem(z, 2)} for r in (0, 1)]
    return holders, homes


def token_copies(source, target, sems, peers, start):
    z = lax.axis_index("seq")
    place = lax.div(z, 2)
    cap = source.shape[0] // 2
    rows = lambda b: pl.ds(b * cap if isinstance(b, int) else pl.multiple_of(b * cap, 16), cap)
    for b in (0, 1):
        out = remote(
            source.at[rows(b)], target.at[rows(place)], sems.at[0, b], sems.at[1, place], peers[b]
        )
        if start:
            out.start()
        else:
            out.wait_send()
    if not start:
        for b in (0, 1):
            remote(
                source.at[rows(b)], target.at[rows(b)], sems.at[0, b], sems.at[1, b], peers[b]
            ).wait_recv()


def owner_bits(f):
    y = f // 4
    return {"c": f % 2, "x": (f // 2) % 2, "yh": y // 2, "yl": (y + y // 2) % 2}


def link_of(portion, step):
    return LINKS[(portion + step) % 5]


def piece_of(portion, bits):
    return sum(bits[link_of(portion, s)] << (4 - s) for s in range(5))


def row_groups(start, count):
    row, end = start, start + count
    while row < end:
        portion, size = row // (4 * PIECE), PIECE
        inner = row % (4 * PIECE)
        take = min(end - row, size - inner % size)
        yield portion, inner // size, inner % size, row - start, take
        row += take


def weight_grad_kernel(shape, *refs):
    shards, chunks = shape
    sources, (sums, dx), refs = refs[:16], refs[16:18], refs[18:]
    gdown, gup, gout, gqkv, home_out, vec_out = refs[:6]
    targets, refs = refs[6:22], refs[22:]
    held, step_in, final, vec, vec_in, ssem, zsem, vsem, tsem, isem = refs
    act, n2, att, normed, ddown, dhid, dbranch, dqkv = zip(targets[:8], targets[8:])
    loads = [pltpu.make_async_copy(a, b, isem.at[k]) for k, (a, b) in enumerate(zip(sources, targets))]
    order = (4, 0, 1, 5, 2, 6, 3, 7)
    for k in order:
        loads[k].start()
        loads[8 + k].start()

    def loaded(*which):
        for k in which:
            loads[k].wait()
            loads[8 + k].wait()

    f, bits, partner = position()
    c = bits["c"]
    holders, homes = token_peers()
    everyone_in = announce([partner[n] for n in ("c", "x", "yl", "yh", "zl", "zh")] + holders + homes)
    features = dx.shape[1]
    owned = features // shards

    vec[0] = sums[...]

    def vec_copy(s):
        name = ("c", "x", "yl", "yh", "zl", "zh")[s]
        return remote(vec.at[s], vec_in.at[s], vsem.at[0, s], vsem.at[1, s], partner[name])

    def vec_step(s):
        copy = vec_copy(s)
        copy.wait()
        vec[s + 1] = vec[s] + vec_in[s]
        if s < 5:
            vec_copy(s + 1).start()

    def put(owner, start, value):
        value = value.astype(bf16)
        own = owner_bits(2 * owner)
        for portion, quarter, inner, at, take in row_groups(start, value.shape[0]):
            place = piece_of(portion, {**own, "zh": quarter // 2, "zl": quarter % 2})
            held[portion, place, inner : inner + take] = value[at : at + take]

    def both_cores(lefts, rights, left_at, right_at):
        total = None
        for left, right in zip(lefts, rights):
            left = left[left_at]
            term = nn(left.reshape(-1, left.shape[-1]), right[:, right_at])
            total = term if total is None else total + term
        return total

    part = lambda j: slice(j * features, (j + 1) * features)

    def add_into(i, base, source, at, count):
        group = min(count, 8)

        def body(k, carry):
            here = pl.ds(base + group * k, group)
            held[i, here] = held[i, here] + source[i, pl.ds(at + group * k, group)]
            return carry

        lax.fori_loop(0, count // group, body, 0)

    bases = [0] * PORTIONS

    def step_copy(i, s, base):
        name = link_of(i, s)
        half = 16 >> s
        at = 32 - 2 * half
        return remote(
            held.at[i, pl.ds(base + (1 - bits[name]) * half, half)],
            step_in.at[i, pl.ds(at, half)],
            ssem.at[0, i, s],
            ssem.at[1, i, s],
            partner[name],
        )

    def z_copy(i, s):
        first, second = ("zl", "zh") if i % 2 == 0 else ("zh", "zl")
        if s == 0:
            at, to = pl.ds(2 * bits[second] + bits[first], 1), partner[first]
        else:
            at, to = pl.ds(2 * bits[second], 2), partner[second]
        return remote(final.at[i, at], final.at[i, at], zsem.at[0, i, s], zsem.at[1, i, s], to)

    whole = slice(None)

    def ready(*portions):
        for i in portions:
            step_copy(i, 0, 0).start()

    everyone_in()
    token_copies(dx, home_out, tsem, homes, start=True)
    vec_copy(0).start()
    loaded(4, 0)
    for m in range(2):
        res = both_cores(act, ddown, slice(4 * m, 4 * m + 4), whole)
        for k in range(4):
            put(4 * m + k, 0, res[4 * owned * k : 4 * owned * (k + 1)])
    ready(0, 1, 2)
    loaded(1, 5)
    for j in range(chunks):
        res = both_cores(n2, dhid, whole, part(j))
        for k in range(8):
            put(k, 192 + owned * j, res[owned * k : owned * (k + 1)])
        if j > 0:
            ready(2 + j)
    vec_step(0)
    loaded(2, 6, 3, 7)
    res = both_cores(att, dbranch, whole, whole)
    for k in range(8):
        put(k, 384, res[owned * k : owned * (k + 1)])
    for j in range(3):
        res = both_cores(normed, dqkv, whole, part(j))
        for k in range(8):
            put(k, 432 + owned * j, res[owned * k : owned * (k + 1)])
        ready(6 + j)
    for s in range(5):
        for i in range(PORTIONS):
            half = 16 >> s
            copy = step_copy(i, s, bases[i])
            bases[i] = bases[i] + bits[link_of(i, s)] * half
            copy.wait()
            add_into(i, bases[i], step_in, 32 - 2 * half, half)
            if s < 4:
                step_copy(i, s + 1, bases[i]).start()
            else:
                first, second = ("zl", "zh") if i % 2 == 0 else ("zh", "zl")
                final[i, 2 * bits[second] + bits[first]] = held[i, bases[i]]
                z_copy(i, 0).start()
        vec_step(s + 1)

    for i in range(PORTIONS):
        z_copy(i, 0).wait()
        z_copy(i, 1).start()
    total = vec[6]
    mine = pltpu.roll(total, lax.rem(features - f * owned, features), 1)
    wide = 4 * owned
    quarter = pltpu.roll(total, lax.rem(features - lax.rem(f, 4) * wide, features), 1)
    chosen = lax.broadcasted_iota(jnp.int32, (16, 1), 0) == 8 + lax.div(f, 4)
    vec_out[0:8] = mine[0:8]
    vec_out[8:9] = jnp.sum(jnp.where(chosen, quarter, 0.0), axis=0, keepdims=True)
    vec_out[9:16] = jnp.zeros((7, features), f32)
    for i in range(PORTIONS):
        z_copy(i, 1).wait()

    def share(start, count):
        got = []
        for portion, quarter, inner, _, take in row_groups(start, count):
            zh, zl = quarter // 2, quarter % 2
            place = 2 * zh + zl if portion % 2 == 0 else 2 * zl + zh
            got.append(final[portion, place, inner : inner + take])
        return jnp.concatenate(got, axis=0)

    gdown[...] = share(0, 4 * owned)
    for j in range(chunks):
        gup[:, part(j)] = share(192 + owned * j, owned)
    gout[...] = share(384, owned)
    for j in range(3):
        gqkv[:, part(j)] = share(432 + owned * j, owned)
    token_copies(dx, home_out, tsem, homes, start=False)


def gather_forward_kernel(
    counts, wq_in, wo_in, wu_in, wd_in, x_in, cot_in, *refs
):
    vectors, refs = refs[:9], refs[9:]
    (qa_out, qb_out, wo_out, wu_out, wd_out, x_out, vec, count_out, next_out, cot_out,
     qa, qb, wo, wu, wd, small, count_in, count_land, kv, att, y_out,
     lsem, sems, tsem, nsem, ksem, hsem) = refs
    sec = lax.axis_index("section")
    _, bits, partner = position()
    f, z = lax.axis_index("fsdp"), lax.axis_index("seq")
    y = lax.div(f, 4)
    g = 2 * bits["zh"] + bits["zl"]
    rows, features = wo_in.shape
    half = features // 2
    wide_a, wide_b = qa.shape[-1], qb.shape[-1]
    fifth = lambda i: [link_of(i, s) for s in range(5)]
    everything, left, right = slice(None), pl.ds(0, half), pl.ds(half, half)
    owners_last = ("zh", "zl", "y", "x", "c")
    items = [
        (qa, ("zh", "y", "x", "c"), ["x", "yl", "yh", "zh"], everything),
        (qb, ("zl", "y", "x", "c"), ["yh", "yl", "x", "zl"], everything),
        (small, ("y", "x", "c"), ["x", "yl", "yh"], everything),
        (wu, owners_last, fifth(1), left),
        (wu, owners_last, fifth(2), right),
        (wd, ("y", "x", "c", "zh", "zl"), fifth(3), left),
        (wd, ("y", "x", "c", "zh", "zl"), fifth(4), right),
        (wo, ("y", "x", "c"), ["x", "yl", "yh"], everything),
    ]

    def places(item, free, fixed):
        ref, dims, _, columns = items[item]
        at = {n: slice(None) if n in free else fixed[n] for n in ("x", "c", "zh", "zl")}
        if "yl" in free and "yh" in free:
            ys = [slice(None)]
        elif "yl" in free:
            ys = [pl.ds(2 * fixed["yh"], 2)]
        else:
            here = 2 * fixed["yh"] + lax.rem(fixed["yh"] + fixed["yl"], 2)
            ys = [here, 3 - here] if "yh" in free else [here]
        return [
            ref.at[tuple(yy if n == "y" else at[n] for n in dims) + (slice(None), columns)] for yy in ys
        ]

    def copies(item, step, free, fixed, name):
        return [
            remote(own[item][0] if step == 0 else p, p, sems.at[0, item, step, k], sems.at[1, item, step, k], partner[name])
            for k, p in enumerate(places(item, free, fixed))
        ]

    def link_copies(item, s):
        order = items[item][2]
        return copies(item, s, order[:s], bits, order[s])

    def core_copies(item, late):
        order = items[item][2]
        fixed = dict(bits)
        if late:
            fixed[order[-1]] = 1 - bits[order[-1]]
        return copies(item, 5 + late, order[:-1], fixed, "c")

    own = [
        (wq_in.at[:, pl.ds(pl.multiple_of(bits["zh"] * wide_a, 128), wide_a)], places(0, (), bits)[0]),
        (
            wq_in.at[:, pl.ds(pl.multiple_of(2 * wide_a + bits["zl"] * wide_b, 128), wide_b)],
            places(1, (), bits)[0],
        ),
        (places(2, (), bits)[0], places(2, (), bits)[0]),
        (wu_in.at[:, pl.ds(pl.multiple_of(g * features, 128), half)], places(3, (), bits)[0]),
        (wu_in.at[:, pl.ds(pl.multiple_of(g * features + half, 128), half)], places(4, (), bits)[0]),
        (wd_in.at[pl.ds(g * rows, rows), left], places(5, (), bits)[0]),
        (wd_in.at[pl.ds(g * rows, rows), right], places(6, (), bits)[0]),
        (wo_in, places(7, (), bits)[0]),
    ]
    holders, homes = token_peers()
    everyone_in = announce(
        [partner[n] for n in ("c", "x", "yl", "yh", "zl", "zh")] + holders + homes + [{"section": 1 - sec}]
    )
    local = [pltpu.make_async_copy(a, b, lsem.at[k]) for k, (a, b) in enumerate(own) if k != 2]
    for copy in local:
        copy.start()
    line = jnp.concatenate([v[...].astype(f32) for v in vectors], axis=1)
    line = jnp.concatenate([line, jnp.zeros((1, small.shape[-1] - line.shape[1]), f32)], axis=1)
    small[y, bits["x"], bits["c"]] = jnp.broadcast_to(line, small.shape[3:]).astype(bf16)
    row = lax.broadcasted_iota(jnp.int32, count_in.shape, 0)
    lane = lax.broadcasted_iota(jnp.int32, count_in.shape, 1)
    live = jnp.zeros(count_in.shape, jnp.int32)
    for m in (0, 1):
        for r in range(4):
            live = jnp.where((row == m) & (lane == r), counts[m, r], live)
    count_in[...] = live
    everyone_in()
    counted = remote(count_in, count_land, nsem.at[0], nsem.at[1], partner["c"])
    for item in range(len(items)):
        for copy in link_copies(item, 0):
            copy.start()
    counted.start()
    for copy in local:
        copy.wait()

    def link_step(item, s):
        order = items[item][2]
        if s >= len(order):
            return
        for copy in link_copies(item, s):
            copy.wait()
        if s + 1 < len(order):
            for copy in link_copies(item, s + 1):
                copy.start()
        if s + 2 == len(order):
            for copy in core_copies(item, 0):
                copy.start()
        if s + 1 == len(order):
            for copy in core_copies(item, 1):
                copy.start()

    def arrived(item):
        for late in (0, 1):
            for copy in core_copies(item, late):
                copy.wait()

    def save(k, source, target):
        copy = pltpu.make_async_copy(source, target, lsem.at[8 + k])
        copy.start()
        return copy

    for s in range(4):
        if s == 1:
            token_copies(x_in, x_out, tsem.at[0], holders, start=True)
        for item in range(len(items)):
            link_step(item, s)
    arrived(2)
    counted.wait()
    chosen = jnp.where(lax.rem(z, 2) == bits["c"], count_in[...], count_land[...])
    chosen = jnp.where(lax.div(z, 2) == 0, chosen[0:1], chosen[1:2])
    count_out[...] = jnp.broadcast_to(chosen, count_out.shape)
    table = jnp.concatenate(
        [small[k // 4, (k // 2) % 2, k % 2][0:1].astype(f32) for k in range(16)], axis=0
    )
    lines = [
        jnp.concatenate([table[k : k + 1, j * rows : (j + 1) * rows] for k in range(16)], axis=1)
        for j in range(8)
    ]
    for r in range(4):
        lines.append(
            jnp.concatenate([table[k : k + 1, 8 * rows : 12 * rows] for k in range(4 * r, 4 * r + 4)], axis=1)
        )
    vec[...] = jnp.concatenate(lines + [jnp.zeros((4, features), f32)], axis=0)
    gain1, shift1, bq, bv, bo, gain2, shift2, bd = (vec[i : i + 1] for i in range(8))
    token_copies(x_in, x_out, tsem.at[0], holders, start=False)
    x = x_out[...].astype(f32)
    normed = (norm_parts(x)[0] * gain1 + shift1).astype(bf16)
    arrived(0)
    arrived(1)
    saved = [save(0, qa, qa_out), save(1, qb, qb_out)]
    block = lambda ref, n: nn(normed, ref[n].reshape(features, ref.shape[-1]))
    second, third = block(qa, 1), block(qb, 0)
    q_rest = features - wide_a
    k_end = 2 * features - 2 * wide_a
    kv[0, :, : wide_a - q_rest] = second[:, q_rest:].astype(bf16)
    kv[0, :, wide_a - q_rest : features] = third[:, :k_end].astype(bf16)
    kv[0, :, features : features + wide_b - k_end] = (third[:, k_end:] + bv[:, : wide_b - k_end]).astype(bf16)
    kv[0, :, features + wide_b - k_end :] = (block(qb, 1) + bv[:, wide_b - k_end :]).astype(bf16)
    swap = remote(kv.at[0], kv.at[1], ksem.at[0], ksem.at[1], partner["c"])
    swap.start()
    q = jnp.concatenate([block(qa, 0), second[:, :q_rest]], axis=1) + bq
    q = q.astype(bf16)
    lane = lax.broadcasted_iota(jnp.int32, chosen.shape, 1)
    count_of = lambda i: jnp.sum(jnp.where(lane == i, chosen.astype(f32), 0.0), axis=1, keepdims=True)
    cap = x.shape[0] // 2
    c = bits["c"]
    live = live_slots(count_of, cap, (c, 1 - c))
    swap.wait()
    pairs = features // (2 * HD)
    attend(kv, q, live, att, range(pairs // 2))
    for item in range(len(items)):
        link_step(item, 4)
    attend(kv, q, live, att, range(pairs // 2, pairs))
    arrived(7)
    saved.append(save(2, wo, wo_out))
    mid = x + (nn(att[...], wo[...].reshape(features, features)) + bo)
    n2 = (norm_parts(mid)[0] * gain2 + shift2).astype(bf16)
    for item in (3, 4, 5, 6):
        arrived(item)
    token_copies(cot_in, cot_out, tsem.at[1], holders, start=True)
    saved += [save(3, wu, wu_out), save(4, wd, wd_out)]
    mine = live_slots(count_of, cap, (c,))
    hops = []
    for b in range(2):
        at = slice(b * cap, (b + 1) * cap)
        y_out[at] = feed_forward(
            n2[at], mid[at], vec, lambda j: wu[j // 2, j % 2].reshape(features, features),
            lambda j: wd[j].reshape(features, features), bd, mine[at],
        )
        here = pl.ds(b * cap, cap)
        hop = remote(
            y_out.at[here], next_out.at[here], hsem.at[0, b], hsem.at[1, b], {"section": 1 - sec}
        )
        hop.start()
        hops.append(hop)
    token_copies(cot_in, cot_out, tsem.at[1], holders, start=False)
    for copy in saved + hops:
        copy.wait()


def finish_kernel(gdown, gup, gout, gqkv, layer_in, grad_in, sums, *outs):
    for source, out in zip((gdown, gup, gout, gqkv), outs):
        out[...] = source[...].astype(f32)
    outs[4][...] = layer_in[...]
    outs[5][...] = grad_in[...]
    for r, out in enumerate(outs[6:]):
        out[...] = sums[r : r + 1, : out.shape[1]]


def per_device(
    images_in, counts, cotangent, gain_one, shift_one, w_qkv, bias_query, bias_value, w_out,
    bias_out, gain_two, shift_two, w_up, bias_up, w_down, bias_down,
):
    micro, images, cap, features = images_in.shape
    shards = lax.axis_size("fsdp")
    rows = micro * images * cap
    owned = features // shards
    ff = w_up.shape[-1]
    chunks = ff // features
    vmem = pl.BlockSpec(memory_space=pltpu.VMEM)
    smem = pl.BlockSpec(memory_space=pltpu.SMEM)
    hbm = pl.BlockSpec(memory_space=pl.ANY)
    dma = pltpu.SemaphoreType.DMA
    sds = jax.ShapeDtypeStruct

    def params(collective_id):
        return pltpu.CompilerParams(
            collective_id=collective_id, has_side_effects=True, vmem_limit_bytes=VMEM_LIMIT
        )

    tokens = sds((rows, features), bf16)
    wide_a, wide_b = 640, 512
    cot = cotangent.reshape(rows, features)
    pairs = features // (2 * HD)
    kv_shape = (2, rows, 2 * features)
    shapes = [
        (2, 4, 2, 2, owned, wide_a),
        (2, 4, 2, 2, owned, wide_b),
        (4, 2, 2, owned, features),
        (2, 2, 4, 2, 2, owned, features),
        (4, 2, 2, 2, 2, owned, features),
    ]
    qa_h, qb_h, wo_h, wu_h, wd_h, own, vec, table, got, cot = pl.pallas_call(
        gather_forward_kernel,
        name="gather_and_first_forward",
        out_shape=(
            *(sds(shape, bf16) for shape in shapes),
            tokens,
            sds((16, features), f32),
            sds((8, 128), jnp.int32),
            tokens,
            tokens,
        ),
        in_specs=[smem] + [hbm] * 6 + [vmem] * 9,
        out_specs=[hbm] * 5 + [vmem] * 4 + [hbm],
        scratch_shapes=[pltpu.VMEM(shape, bf16) for shape in shapes]
        + [
            pltpu.VMEM((4, 2, 2, 16, 640), bf16),
            pltpu.VMEM((8, 128), jnp.int32),
            pltpu.VMEM((8, 128), jnp.int32),
            pltpu.VMEM(kv_shape, bf16),
            pltpu.VMEM((rows, features), bf16),
            pltpu.VMEM((rows, features), bf16),
            dma((13,)),
            dma((2, 8, 7, 2)),
            dma((2, 2, 2)),
            dma((2,)),
            dma((2,)),
            dma((2, 2)),
        ],
        compiler_params=params(0),
    )(
        counts.reshape(micro * images, -1), w_qkv[0], w_out[0], w_up[0], w_down[0],
        images_in.reshape(rows, features), cot, gain_one, shift_one, bias_query, bias_value,
        bias_out, gain_two, shift_two, bias_down, bias_up,
    )
    weights = (
        vec,
        qa_h.reshape(2, features, wide_a),
        qb_h.reshape(2, features, wide_b),
        wo_h.reshape(features, features),
        wu_h.reshape(chunks, features, features),
        wd_h.reshape(ff, features),
    )
    wide = sds((rows, ff), bf16)
    triple = sds((rows, 3 * features), bf16)
    turned = sds((8, owned, rows), bf16)
    operands = (sds((8, 4 * owned, rows), bf16), turned, turned, turned, tokens, wide, tokens, triple)
    exchange = (pairs, 2, rows, 2 * HD)
    flat = pltpu.VMEM((rows, features), bf16)
    layer_out, *operands_h, sums, dx = pl.pallas_call(
        stages_kernel,
        name="second_forward_and_backward",
        out_shape=(
            tokens, *operands, *operands, sds((16, features), f32), tokens,
        ),
        in_specs=[smem] + [vmem] * 3 + [hbm] * 6,
        out_specs=[vmem] + [hbm] * 16 + [vmem, hbm],
        scratch_shapes=[
            pltpu.VMEM((features, 3 * features), bf16),
            pltpu.VMEM((features, features), bf16),
            pltpu.VMEM((chunks, features, features), bf16),
            pltpu.VMEM((ff, features), bf16),
            pltpu.VMEM(kv_shape, bf16),
            pltpu.VMEM((pairs, 2 * rows, 2 * rows), bf16),
            flat,
            pltpu.VMEM((rows, ff), bf16),
            pltpu.VMEM((rows, ff), bf16),
            flat, flat, flat, flat, flat,
            pltpu.VMEM((rows, ff), bf16),
            flat,
            pltpu.VMEM((rows, 3 * features), bf16),
            flat, flat,
            pltpu.VMEM(exchange, f32),
            pltpu.VMEM(exchange, bf16),
            pltpu.VMEM((2, *exchange), bf16),
            pltpu.VMEM((8, 2, 4 * owned, rows), bf16),
            pltpu.VMEM((8, 2, owned, rows), bf16),
            pltpu.VMEM((8, 2, owned, rows), bf16),
            pltpu.VMEM((8, 2, owned, rows), bf16),
            dma((14,)),
            dma((2,)),
            dma((2, 2, pairs)),
            dma((2, 2)),
            dma((2, 2)),
            dma((9,)),
            dma((2, 8)),
        ],
        compiler_params=params(1),
    )(table, own, got, *weights, cot)

    vector = sds((1, owned), f32)
    grads = pl.pallas_call(
        functools.partial(weight_grad_kernel, (shards, chunks)),
        name="weight_gradients",
        out_shape=(
            sds((4 * owned, features), bf16),
            sds((owned, ff), bf16),
            sds((owned, features), bf16),
            sds((owned, 3 * features), bf16),
            tokens,
            sds((16, features), f32),
        ),
        in_specs=[hbm] * 16 + [vmem] * 2,
        out_specs=[vmem] * 6,
        scratch_shapes=[
            *(pltpu.VMEM(o.shape, bf16) for o in operands * 2),
            pltpu.VMEM((PORTIONS, 32, PIECE, features), bf16),
            pltpu.VMEM((PORTIONS, 32, PIECE, features), bf16),
            pltpu.VMEM((PORTIONS, 4, PIECE, features), bf16),
            pltpu.VMEM((7, 16, features), f32),
            pltpu.VMEM((6, 16, features), f32),
            dma((2, PORTIONS, 5)),
            dma((2, PORTIONS, 2)),
            dma((2, 6)),
            dma((2, 2)),
            dma((16,)),
        ],
        compiler_params=params(2),
    )(*operands_h, sums, dx)
    gw_down, gw_up, gw_out, gw_qkv, layer_out, input_grad, *vectors = pl.pallas_call(
        finish_kernel,
        name="finish",
        out_shape=(
            *(sds(g.shape, f32) for g in grads[:4]),
            tokens,
            tokens,
            *([vector] * 8),
            sds((1, 4 * owned), f32),
        ),
        in_specs=[vmem] * 7,
        out_specs=[vmem] * 15,
    )(*grads[:4], layer_out, *grads[4:])
    gw_down, gw_up, gw_out, gw_qkv = (g[None] for g in (gw_down, gw_up, gw_out, gw_qkv))
    gg1, gs1, gbq, gbv, gbo, gg2, gs2, gbd, gbu = vectors
    out_shape = (1, micro, images, cap, features)
    return (
        layer_out.reshape(out_shape), input_grad.reshape(out_shape), gg1, gs1, gw_qkv, gbq, gbv,
        gw_out, gbo, gg2, gs2, gw_up, gbu, gw_down, gbd,
    )


def solution(mesh):
    token = P(None, "fsdp", "seq", None)
    vector = P("section", "fsdp")
    matrix = P("section", "fsdp", None)
    result = P("section", None, "fsdp", "seq", None)
    return jax.shard_map(
        per_device,
        mesh=mesh,
        in_specs=(
            token, P(None, "fsdp", None), token, vector, vector, matrix, vector, vector, matrix, vector,
            vector, vector, matrix, vector, matrix, vector,
        ),
        out_specs=(
            result, result, vector, vector, matrix, vector, vector, matrix, vector, vector, vector,
            matrix, vector, matrix, vector,
        ),
        check_vma=False,
    )
```
